32 devices in a mesh: img: 8 (over z, y), row: 4 (over x, core).
Axes of the slice: x: 2, y: 2, z: 4, core: 2. Of those that a mesh axis runs over, the one named last changes fastest.
Arguments:
- images: bfloat16 [24, 32, 32, 384], P('img', 'row'), may hold values from -8 to 8
- level_count: int32 [24], P('img'), may hold values from 2 to 1280
- level_index: int32 [24], P('img'), may hold values from 0 to 1278, as said below
- labels: int32 [24], P('img'), may hold values from 0 to 999
- first_gain: bfloat16 [384], replicated, may hold values from 0.5 to 1.5
- first_shift: bfloat16 [384], replicated, may hold values from -1.75 to 1.75
- first_kernel: bfloat16 [3456, 384], replicated, may hold values from -0.109375 to 0.109375
- first_offset: bfloat16 [384], replicated, may hold values from -1.75 to 1.75
- embed_weight: bfloat16 [768, 768], replicated, may hold values from -0.21875 to 0.21875
- embed_offset: bfloat16 [768], replicated, may hold values from -1.75 to 1.75
- class_table: bfloat16 [1000, 768], replicated, may hold values from -6 to 6
- second_gain: bfloat16 [384], replicated, may hold values from 0.5 to 1.5
- second_shift: bfloat16 [384], replicated, may hold values from -1.75 to 1.75
- second_kernel: bfloat16 [3456, 384], replicated, may hold values from -0.109375 to 0.109375
- second_offset: bfloat16 [384], replicated, may hold values from -1.75 to 1.75
- third_gain: bfloat16 [384], replicated, may hold values from 0.5 to 1.5
- third_shift: bfloat16 [384], replicated, may hold values from -1.75 to 1.75
- joint_weight: bfloat16 [384, 1152], replicated, may hold values from -0.3125 to 0.3125
- joint_offset: bfloat16 [768], replicated, may hold values from -1.75 to 1.75
- output_weight: bfloat16 [384, 384], replicated, may hold values from -2.5 to 2.5
- output_offset: bfloat16 [384], replicated, may hold values from -1.75 to 1.75
- cotangent: bfloat16 [24, 32, 32, 384], P('img', 'row'), may hold values from -8 to 8
Outputs:
- result: bfloat16 [24, 32, 32, 384], P('img', 'row')
- images_gradient: float32 [24, 32, 32, 384], P('img', 'row')
- first_gain_gradient: float32 [384], P('row')
- first_shift_gradient: float32 [384], P('row')
- first_kernel_gradient: float32 [3456, 384], P('row')
- first_offset_gradient: float32 [384], P('row')
- embed_weight_gradient: float32 [768, 768], P('row')
- embed_offset_gradient: float32 [768], P('row')
- class_table_gradient: float32 [1000, 768], P('row')
- second_gain_gradient: float32 [384], P('row')
- second_shift_gradient: float32 [384], P('row')
- second_kernel_gradient: float32 [3456, 384], P('row')
- second_offset_gradient: float32 [384], P('row')
- third_gain_gradient: float32 [384], P('row')
- third_shift_gradient: float32 [384], P('row')
- joint_weight_gradient: float32 [384, 1152], P('row')
- joint_offset_gradient: float32 [768], P('row')
- output_weight_gradient: float32 [384, 384], P('row')
- output_offset_gradient: float32 [384], P('row')
The draws below stay inside these ranges and needn't reach their ends.
Inputs may be any that keep to these rules, and one draw needn't show every extreme that they name: Each image's level_index is below its level_count - 1.
All inputs are finite; a program needn't handle non-finite values.
Results may differ from the reference program's by a relative error of at most 0.017.
Values may be sent and summed in bfloat16 or wider, within the bound.
A program may use at most 192 MiB of HBM per device.

```python
import math
import jax
import jax.numpy as jnp
from jax import lax

C = 384
GROUPS = 32
HEAD = 64
EMB = 768
CLASSES = 1000
HEIGHT = 32
WIDTH = 32
IMAGES = 24


def level_pair(key):
    count_key, index_key, place_key = jax.random.split(jax.random.fold_in(key, 11), 3)
    counts = jax.random.randint(count_key, (IMAGES,), 2, 1281)
    indices = jax.random.randint(index_key, (IMAGES,), 0, counts - 1)
    order = jax.random.permutation(place_key, IMAGES)
    top_place = order[0]
    bottom_place = order[1]
    counts = counts.at[top_place].set(1280).at[bottom_place].set(2)
    indices = indices.at[top_place].set(1278).at[bottom_place].set(0)
    return (counts.astype(jnp.int32), indices.astype(jnp.int32))


def draw_level_count(key, part):
    return level_pair(key)[0]


def draw_level_index(key, part):
    return level_pair(key)[1]


def draw_images(key, part):
    key = jax.random.fold_in(key, 3)
    noise_key = jax.random.fold_in(key, 0)
    position = jnp.arange(HEIGHT, dtype=jnp.float32) / (HEIGHT - 1)
    row_ramp = (0.6 + 1.2 * position)[None, :, None, None]
    values = jnp.clip(jax.random.normal(noise_key, (IMAGES, HEIGHT, WIDTH, C), jnp.float32), -4.0, 4.0) * row_ramp
    return values.astype(jnp.bfloat16)


def set_ends(result, stream_key, smallest, top_value):
    shape = result.shape
    index_at = [jax.random.randint(jax.random.fold_in(stream_key, axis), (), 0, shape[axis]) for axis in range(len(shape))]
    result = result.at[tuple(index_at)].set(smallest)
    longest = shape.index(max(shape))
    index_at[longest] = (index_at[longest] + 1) % shape[longest]
    return result.at[tuple(index_at)].set(top_value)


def with_spikes(values, rng, source, target, shards_of, factor):
    def block_of(dim):
        return (jnp.arange(values.shape[dim]) // (values.shape[dim] // shards_of)).reshape((-1,) + (1,) * (values.ndim - 1 - dim))

    first = jax.random.permutation(rng, shards_of)[block_of(target)]
    far = (block_of(target) + shards_of // 2) % shards_of
    return jnp.where((block_of(source) == first) | (block_of(source) == far), factor * values, values)


def steps_of(key, shape, cuts, low, high):
    def one(dim, parts):
        heights = jax.random.uniform(jax.random.fold_in(jax.random.fold_in(key, 6), dim), (parts,), jnp.float32, low / len(cuts), high / len(cuts))
        return jnp.repeat(jnp.exp(heights), shape[dim] // parts).reshape((-1,) + (1,) * (len(shape) - dim - 1))

    factor_of = one(*cuts[0])
    for cut in cuts[1:]:
        factor_of = factor_of * one(*cut)
    return factor_of


def gaussian(stream_key, extent, scale, limit, cuts=(), kind=jnp.bfloat16):
    loudness = steps_of(stream_key, extent, cuts, -0.22, 0.18) if cuts else 1.0
    values = jax.random.normal(stream_key, extent, jnp.float32) * scale * loudness
    return jnp.minimum(jnp.maximum(values, -limit), limit).astype(kind)


def bell_draw_with(own_key, extent, scale, reach, shards, heavy, kind=jnp.bfloat16):
    entries = scale * jax.random.normal(own_key, extent, jnp.float32)
    if shards:
        entries = entries * steps_of(own_key, extent, shards, -0.22, 0.18)
    return jnp.clip(with_spikes(entries, jax.random.fold_in(own_key, 3), *heavy), -reach, reach).astype(kind)


def setup_inputs(seed: int = 0) -> dict:
    streams_of = jax.random.split(jax.random.key(seed), 23)
    return {
        "images": draw_images(jax.random.fold_in(streams_of[22], 71), 0),
        "level_count": draw_level_count(jax.random.fold_in(streams_of[22], 71), 0),
        "level_index": draw_level_index(jax.random.fold_in(streams_of[22], 71), 0),
        "labels": set_ends(jax.random.randint(streams_of[3], (IMAGES,), 0, CLASSES), jax.random.fold_in(streams_of[3], 1), 0, CLASSES - 1).astype(jnp.int32),
        "first_gain": jnp.clip(1.0 + 0.1 * jax.random.normal(streams_of[4], (C,), jnp.float32), 0.5, 1.5).astype(jnp.bfloat16),
        "first_shift": gaussian(streams_of[5], (C,), 0.3, 1.75),
        "first_kernel": gaussian(streams_of[6], (9 * C, C), (9 * C) ** -0.5, 0.109375),
        "first_offset": gaussian(streams_of[7], (C,), 0.3, 1.75),
        "embed_weight": gaussian(streams_of[8], (EMB, 2 * C), EMB ** -0.5, 0.21875),
        "embed_offset": gaussian(streams_of[9], (2 * C,), 0.3, 1.75),
        "class_table": gaussian(streams_of[10], (CLASSES, EMB), 1.0, 6.0),
        "second_gain": jnp.clip(1.0 + 0.1 * jax.random.normal(streams_of[11], (C,), jnp.float32), 0.5, 1.5).astype(jnp.bfloat16),
        "second_shift": gaussian(streams_of[12], (C,), 0.3, 1.75),
        "second_kernel": gaussian(streams_of[13], (9 * C, C), (9 * C) ** -0.5, 0.109375),
        "second_offset": gaussian(streams_of[14], (C,), 0.3, 1.75),
        "third_gain": jnp.clip(1.0 + 0.1 * jax.random.normal(streams_of[15], (C,), jnp.float32), 0.5, 1.5).astype(jnp.bfloat16),
        "third_shift": gaussian(streams_of[16], (C,), 0.3, 1.75),
        "joint_weight": gaussian(streams_of[17], (C, 3 * C), C ** -0.5, 0.3125),
        "joint_offset": gaussian(streams_of[18], (2 * C,), 0.3, 1.75),
        "output_weight": gaussian(streams_of[19], (C, C), (max(C // 64, 1)) ** -0.5, 2.5),
        "output_offset": gaussian(streams_of[20], (C,), 0.3, 1.75),
        "cotangent": bell_draw_with(streams_of[21], (IMAGES, HEIGHT, WIDTH, C), 1.0, 8.0, ((0, 8), (1, 4)), (0, 3, 8, 2.0)),
    }


@jax.custom_vjp
def low(v):
    return lax.optimization_barrier(v.astype(jnp.bfloat16)).astype(jnp.float32)

@jax.custom_vjp
def low_back(v):
    return v

def low_keep(v):
    return (low(v), None)

def low_pass(kept, grad):
    return (grad,)

def back_keep(v):
    return (v, None)

def back_low(kept, grad):
    return (low(grad),)
low.defvjp(low_keep, low_pass)
low_back.defvjp(back_keep, back_low)
sigma_least = 0.002
sigma_most = 80.0
sigma_power = 7.0
norm_eps = 1e-05
highest = lax.Precision.HIGHEST

def noise_features(level_count, level_index):
    position = (level_index.astype(jnp.float32) + 1.0) / (level_count.astype(jnp.float32) - 1.0)
    low_root = sigma_least ** (1.0 / sigma_power)
    high_root = sigma_most ** (1.0 / sigma_power)
    noise_level = (low_root + position * (high_root - low_root)) ** sigma_power
    noise_time = 250.0 * jnp.log(noise_level)
    half_width = EMB // 2
    frequency = jnp.exp(-math.log(10000.0) * jnp.arange(half_width, dtype=jnp.float32) / half_width)
    angles = noise_time[:, None] * frequency[None, :]
    return jnp.concatenate([jnp.cos(angles), jnp.sin(angles)], axis=-1)

def group_norm(values, gain_vector, shift_vector):
    pixels, channels = values.shape
    grouped = values.reshape(pixels, GROUPS, channels // GROUPS)
    centre = lax.optimization_barrier(jnp.mean(grouped, axis=(0, 2)))
    square = lax.optimization_barrier(jnp.mean(grouped * grouped, axis=(0, 2)))
    scaled = lax.rsqrt(square - centre * centre + norm_eps)
    normed = ((grouped - centre[None, :, None]) * scaled[None, :, None]).reshape(pixels, channels)
    return normed * gain_vector + shift_vector

def convolve(values, kernel):
    channels = values.shape[-1]
    filters = kernel.reshape(3, 3, channels, kernel.shape[1])
    return lax.conv_general_dilated(values[None], filters, (1, 1), 'SAME', dimension_numbers=('NHWC', 'HWIO', 'NHWC'), precision=highest)[0]

def image_forward(params, picture, feature_row, class_id):
    first_gain, first_shift, first_kernel, first_offset, embed_weight, embed_offset, class_table, second_gain, second_shift, second_kernel, second_offset, third_gain, third_shift, joint_weight, joint_offset, output_weight, output_offset = params
    height, width, channels = picture.shape
    pixels = height * width
    embedded = feature_row + class_table[class_id]
    embed_act = low(jax.nn.silu(embedded))
    modulate = jnp.dot(embed_act, embed_weight, precision=highest) + embed_offset
    scale_part = modulate[:channels]
    shift_part = modulate[channels:]
    flattened = picture.reshape(pixels, channels)
    first_act = low(jax.nn.silu(group_norm(flattened, first_gain, first_shift)))
    hidden = low_back(convolve(first_act.reshape(height, width, channels), first_kernel).reshape(pixels, channels) + first_offset)
    shaped = group_norm(hidden, second_gain, second_shift)
    second_act = low(jax.nn.silu(shaped * (1.0 + scale_part) + shift_part))
    branch = low_back(convolve(second_act.reshape(height, width, channels), second_kernel).reshape(pixels, channels) + second_offset)
    middle = (flattened + branch) * math.sqrt(0.5)
    attend_input = low(group_norm(middle, third_gain, third_shift))
    zero_part = jnp.zeros((channels,), middle.dtype)
    joint_bias = jnp.concatenate([joint_offset[:channels], zero_part, joint_offset[channels:]])
    joint_rows = low(low_back(jnp.dot(attend_input, joint_weight, precision=highest) + joint_bias))
    head_count = channels // HEAD
    query_rows = joint_rows[:, :channels].reshape(pixels, head_count, HEAD)
    key_rows = joint_rows[:, channels:2 * channels].reshape(pixels, head_count, HEAD)
    value_rows = joint_rows[:, 2 * channels:].reshape(pixels, head_count, HEAD)
    scores = low_back(jnp.einsum('phd,khd->hpk', query_rows, key_rows, precision=highest) * HEAD ** (-0.5))
    weights = low(jax.nn.softmax(scores, axis=-1))
    mixed_rows = jnp.einsum('hpk,khd->phd', weights, value_rows, precision=highest).reshape(pixels, channels)
    mixed_rows = low(low_back(mixed_rows))
    outcome = middle + jnp.dot(mixed_rows, output_weight, precision=highest) + output_offset
    return outcome.reshape(height, width, channels)

def reference(images, level_count, level_index, labels, first_gain, first_shift, first_kernel, first_offset, embed_weight, embed_offset, class_table, second_gain, second_shift, second_kernel, second_offset, third_gain, third_shift, joint_weight, joint_offset, output_weight, output_offset, cotangent):
    features = noise_features(level_count, level_index)
    params = tuple((array_item.astype(jnp.float32) for array_item in (first_gain, first_shift, first_kernel, first_offset, embed_weight, embed_offset, class_table, second_gain, second_shift, second_kernel, second_offset, third_gain, third_shift, joint_weight, joint_offset, output_weight, output_offset)))

    def image_step(totals, inputs):
        picture, feature_row, class_id, incoming = inputs

        def per_image(params_now, picture_now):
            return image_forward(params_now, picture_now, feature_row, class_id)
        outcome, pullback = jax.vjp(per_image, params, picture.astype(jnp.float32))
        param_grads, picture_grad = pullback(incoming.astype(jnp.float32))
        totals = jax.tree.map(jnp.add, totals, param_grads)
        return (totals, (outcome.astype(jnp.bfloat16), picture_grad))
    initial = jax.tree.map(jnp.zeros_like, params)
    totals, (outputs, picture_grads) = lax.scan(image_step, initial, (images, features, labels, cotangent))
    return (outputs, picture_grads, totals[0], totals[1], totals[2], totals[3], totals[4], totals[5], totals[6], totals[7], totals[8], totals[9], totals[10], totals[11], totals[12], totals[13], totals[14], totals[15], totals[16])
```

```python
import math

import jax
import jax.numpy as jnp
from jax import lax
from jax.experimental import pallas as pl
from jax.experimental.pallas import tpu as pltpu
from jax.sharding import PartitionSpec as P

GROUPS = 32
HEAD = 64
EMB = 768
MESH = pl.DeviceIdType.MESH

norm_eps = 1e-05
sigma_least = 0.002
sigma_most = 80.0
sigma_power = 7.0
highest = lax.Precision.HIGHEST
float_type = jnp.float32
low_type = jnp.bfloat16
contract_rows = (((0,), (0,)), ((), ()))
contract_cols = (((1,), (1,)), ((), ()))


def noise_features(level_count, level_index):
    position = (level_index.astype(jnp.float32) + 1.0) / (level_count.astype(jnp.float32) - 1.0)
    low_root = sigma_least ** (1.0 / sigma_power)
    high_root = sigma_most ** (1.0 / sigma_power)
    noise_level = (low_root + position * (high_root - low_root)) ** sigma_power
    noise_time = 250.0 * jnp.log(noise_level)
    half_width = EMB // 2
    frequency = jnp.exp(-math.log(10000.0) * jnp.arange(half_width, dtype=jnp.float32) / half_width)
    angles = noise_time[:, None] * frequency[None, :]
    return jnp.concatenate([jnp.cos(angles), jnp.sin(angles)], axis=-1)


def silu_slope(values):
    sigmoid_part = jax.nn.sigmoid(values)
    return sigmoid_part * (1.0 + values * (1.0 - sigmoid_part))


def normalize(values, centre, scaled):
    return (values - centre) * scaled


def group_fold(v):
    return v.reshape(v.shape[:-1] + (GROUPS, v.shape[-1] // GROUPS))


def group_back(upstream, normed, scaled):
    image_count, pixels, channels = upstream.shape
    first_sum = jnp.sum(group_fold(jnp.sum(upstream, axis=1)), axis=-1)
    second_sum = jnp.sum(group_fold(jnp.sum(upstream * normed, axis=1)), axis=-1)
    first_sum, second_sum = lax.psum((first_sum, second_sum), "row")
    entries = pixels * lax.axis_size("row") * (channels // GROUPS)
    per = channels // GROUPS
    first_sum = jnp.repeat(first_sum / entries, per, axis=-1)
    second_sum = jnp.repeat(second_sum / entries, per, axis=-1)
    return scaled * (upstream - first_sum[:, None, :] - normed * second_sum[:, None, :])


def padded_grads(activity):
    size, length = lax.axis_size("row"), activity.shape[1]
    up = [(i, i + 1) for i in range(size - 1)]
    down = [(j, i) for i, j in up]
    last = lax.slice_in_dim(activity, length - 1, length, axis=1)
    initial = lax.slice_in_dim(activity, 0, 1, axis=1)
    before = lax.ppermute(last, "row", up)
    after = lax.ppermute(initial, "row", down)
    framed = jnp.concatenate([before, activity, after], axis=1)
    return jnp.pad(framed, ((0, 0), (0, 0), (1, 1), (0, 0)))


def backward_patches(framed, stripe_rows, image_width):
    pieces = [
        framed[
            :, 2 - row_tap : 2 - row_tap + stripe_rows, 2 - col_tap : 2 - col_tap + image_width, :
        ]
        for row_tap in range(3)
        for col_tap in range(3)
    ]
    joined = jnp.concatenate(pieces, axis=-1)
    return joined.reshape(-1, joined.shape[-1])


def transpose_product(columns, kernel):
    channels = kernel.shape[1]
    stacked = columns.reshape(columns.shape[0], 9, channels)
    kernel_taps = kernel.reshape(9, kernel.shape[0] // 9, channels)
    return lax.dot_general(
        stacked, kernel_taps, (((1, 2), (0, 2)), ((), ())), preferred_element_type=float_type
    )


def peers():
    i = lax.axis_index("img")
    r = lax.axis_index("row")
    c = lax.rem(r, 2)
    near = r + 1 - 2 * c
    return (i, r, c, {1: (i, near), 2: (i, lax.rem(r + 2, 4)), 3: (i, 3 - r)})


def half_silu(v):
    h = 0.5 * v
    return h * jnp.tanh(h) + h


def col_iota(n, width, channels):
    return lax.rem(lax.broadcasted_iota(jnp.int32, (n, channels), 0), width)


def fill_row(buf, start, act, channels, width):
    col = lax.broadcasted_iota(jnp.int32, (width, channels), 0)
    left = jnp.where(col == 0, 0.0, pltpu.roll(act, 1, 0))
    right = jnp.where(col == width - 1, 0.0, pltpu.roll(act, width - 1, 0))
    rows = pl.ds(start, width)
    buf[rows, 0:channels] = left.astype(low_type)
    buf[rows, channels : 2 * channels] = act.astype(low_type)
    buf[rows, 2 * channels : 3 * channels] = right.astype(low_type)


def pack_stats(first, second):
    channels = first.shape[1]
    row = lax.broadcasted_iota(jnp.int32, (8, channels), 0)

    def terms(v):
        a = v.astype(low_type).astype(float_type)
        b = (v - a).astype(low_type).astype(float_type)
        c = v - a - b
        return jnp.where(row == 0, a, jnp.where(row == 1, b, jnp.where(row == 2, c, 0.0)))

    return jnp.concatenate([terms(first), terms(second)], axis=0).astype(low_type)


def block_ones(channels, per):
    a = lax.broadcasted_iota(jnp.int32, (channels, channels), 0)
    b = lax.broadcasted_iota(jnp.int32, (channels, channels), 1)
    a = lax.shift_right_logical(a * 43691, 19)
    b = lax.shift_right_logical(b * 43691, 19)
    return jnp.where(a == b, 1.0, 0.0).astype(low_type)


def combine_stats(parts, ones, entries):
    total = jnp.dot(jnp.concatenate(parts, axis=0), ones, preferred_element_type=float_type)
    first = total[0:8] + total[16:24] + total[32:40] + total[48:56]
    second = total[8:16] + total[24:32] + total[40:48] + total[56:64]
    first = jnp.sum(first, axis=0, keepdims=True) * (1.0 / entries)
    second = jnp.sum(second, axis=0, keepdims=True) * (1.0 / entries)
    return first, second


def forward_kernel(
    x_ref, vec_ref, mod_ref, w1_any, w2_any,
    hid_ref, mid_ref, att_ref, act1_ref, act2_ref, st_ref,
    w1, w2, ones, abuf, m1, m3, got, wsem, ssem, rsem,
):
    images, pixels, channels = x_ref.shape
    width = 32
    edge = pixels - width
    entries = 4.0 * pixels * (channels // GROUPS)
    i, r, c, who = peers()
    load1 = pltpu.make_async_copy(w1_any, w1, wsem.at[0])
    load2 = pltpu.make_async_copy(w2_any, w2, wsem.at[1])
    load1.start()
    load2.start()
    barrier = pltpu.get_barrier_semaphore()
    for k in (1, 2, 3):
        pl.semaphore_signal(barrier, inc=1, device_id=who[k], device_id_type=MESH)
    ones[...] = block_ones(channels, channels // GROUPS)
    inner = pl.multiple_of(edge * (1 - c), width)
    outer = pl.multiple_of(edge * c, width)
    inner_live = None
    outer_live = jnp.logical_and(r > 0, r < 3)
    stat = pl.ds(0, 16)
    halo = pl.ds(16, width)

    def copies(p, b):
        full = p < 2
        rows = pl.ds(0, 48) if full else stat
        return [
            pltpu.make_async_remote_copy(
                src.at[p, b, rs], got.at[p, b, k - 1, rs], ssem.at[p, b, k - 1],
                rsem.at[p, b, k - 1], device_id=who[k], device_id_type=MESH,
            )
            for k, src, rs in ((1, m1, rows), (2, m1, stat), (3, m3, rows))
        ]

    def send(p, b, first, second, edges):
        packed = pack_stats(first, second)
        m1[p, b, 0:16] = packed
        m3[p, b, 0:16] = packed
        if edges is not None:
            m1[p, b, 16:48] = edges(inner)
            m3[p, b, 16:48] = edges(outer)
        for cp in copies(p, b):
            cp.start()

    def receive(p, b):
        for cp in copies(p, b):
            cp.wait_recv()
        parts = [m1[p, b, 0:16]] + [got[p, b, k, 0:16] for k in range(3)]
        first, second = combine_stats(parts, ones[...], entries)
        return first, lax.rsqrt(second - first * first + norm_eps)

    def expand(p, b, affine, own, keep):
        for row in range(pixels // width):
            a = half_silu(affine(own(row)))
            keep[b, pl.ds(row * width, width)] = a.astype(low_type)
            fill_row(abuf, (row + 1) * width, a, channels, width)
        a = half_silu(affine(got[p, b, 0, 16:48].astype(float_type)))
        fill_row(abuf, pl.multiple_of((pixels + width) * (1 - c), width), a, channels, width)
        a = half_silu(affine(got[p, b, 2, 16:48].astype(float_type)))
        a = jnp.where(outer_live, a, 0.0)
        fill_row(abuf, pl.multiple_of((pixels + width) * c, width), a, channels, width)

    def convolve(w):
        depth = 3 * channels
        return sum(
            jnp.dot(
                abuf[width * dy : width * dy + pixels, :],
                w[depth * dy : depth * (dy + 1), :],
                preferred_element_type=float_type,
            )
            for dy in range(3)
        )

    def vec(n):
        return vec_ref[n : n + 1, :]

    pl.semaphore_wait(barrier, 3)

    def step0(b, _):
        v = x_ref[b].astype(float_type)
        send(
            0, b, jnp.sum(v, axis=0, keepdims=True), jnp.sum(v * v, axis=0, keepdims=True),
            lambda at: x_ref[b, pl.ds(at, width)],
        )
        return 0

    lax.fori_loop(0, images, step0, 0)
    load1.wait()

    def step1(b, _):
        centre, scaled = receive(0, b)
        st_ref[b, 0:1] = centre
        st_ref[b, 1:2] = scaled
        slope = scaled * vec(0)
        shift = vec(1)
        expand(
            0, b, lambda v: (v - centre) * slope + shift,
            lambda row: x_ref[b, pl.ds(row * width, width)].astype(float_type), act1_ref,
        )
        hidden = convolve(w1) + vec(2)
        hid_ref[b] = hidden
        send(
            1, b, jnp.sum(hidden, axis=0, keepdims=True),
            jnp.sum(hidden * hidden, axis=0, keepdims=True),
            lambda at: hid_ref[b, pl.ds(at, width)].astype(low_type),
        )
        return 0

    lax.fori_loop(0, images, step1, 0)
    load2.wait()

    def step2(b, _):
        centre, scaled = receive(1, b)
        st_ref[b, 2:3] = centre
        st_ref[b, 3:4] = scaled
        grow = 1.0 + mod_ref[b, 0:1]
        slope = scaled * vec(3) * grow
        shift = vec(4) * grow + mod_ref[b, 1:2]
        expand(
            1, b, lambda v: (v - centre) * slope + shift,
            lambda row: hid_ref[b, pl.ds(row * width, width)], act2_ref,
        )
        middle = (convolve(w2) + vec(5) + x_ref[b].astype(float_type)) * math.sqrt(0.5)
        mid_ref[b] = middle
        send(
            2, b, jnp.sum(middle, axis=0, keepdims=True),
            jnp.sum(middle * middle, axis=0, keepdims=True), None,
        )
        return 0

    lax.fori_loop(0, images, step2, 0)

    def step3(b, _):
        centre, scaled = receive(2, b)
        st_ref[b, 4:5] = centre
        st_ref[b, 5:6] = scaled
        slope = scaled * vec(6)
        att_ref[b] = ((mid_ref[b] - centre) * slope + vec(7)).astype(low_type)
        for p in range(3):
            for cp in copies(p, b):
                cp.wait_send()
        return 0

    lax.fori_loop(0, images, step3, 0)


def forward_call(x, vectors, modulate, first_kernel, second_kernel):
    images, pixels, channels = x.shape
    depth = 9 * channels
    vm = pl.BlockSpec(memory_space=pltpu.VMEM)
    hbm = pl.BlockSpec(memory_space=pl.ANY)
    wide = jax.ShapeDtypeStruct(x.shape, float_type)
    low = jax.ShapeDtypeStruct(x.shape, low_type)
    return pl.pallas_call(
        forward_kernel,
        out_shape=(wide, wide, low, low, low, jax.ShapeDtypeStruct((images, 8, channels), float_type)),
        in_specs=[vm, vm, vm, hbm, hbm],
        out_specs=(vm,) * 6,
        scratch_shapes=[
            pltpu.VMEM((depth, channels), low_type),
            pltpu.VMEM((depth, channels), low_type),
            pltpu.VMEM((channels, channels), low_type),
            pltpu.VMEM((pixels + 64, 3 * channels), low_type),
            pltpu.VMEM((3, images, 48, channels), low_type),
            pltpu.VMEM((3, images, 48, channels), low_type),
            pltpu.VMEM((3, images, 3, 48, channels), low_type),
            pltpu.SemaphoreType.DMA((2,)),
            pltpu.SemaphoreType.DMA((3, images, 3)),
            pltpu.SemaphoreType.DMA((3, images, 3)),
        ],
        compiler_params=pltpu.CompilerParams(
            collective_id=0, has_side_effects=True, vmem_limit_bytes=56 << 20
        ),
        name="forward",
    )(x, vectors, modulate, first_kernel, second_kernel)


def shards(
    images,
    level_count,
    level_index,
    labels,
    first_gain,
    first_shift,
    first_kernel,
    first_offset,
    embed_weight,
    embed_offset,
    class_table,
    second_gain,
    second_shift,
    second_kernel,
    second_offset,
    third_gain,
    third_shift,
    joint_weight,
    joint_offset,
    output_weight,
    output_offset,
    cotangent,
):
    image_count, stripe_rows, image_width, channels = images.shape
    layout = (image_count, stripe_rows, image_width, channels)
    pixels = stripe_rows * image_width
    head_count = channels // HEAD
    score_scale = HEAD ** (-0.5)
    gain_one = first_gain.astype(float_type)
    shift_one = first_shift.astype(float_type)
    gain_two = second_gain.astype(float_type)
    shift_two = second_shift.astype(float_type)
    gain_three = third_gain.astype(float_type)
    features = noise_features(level_count, level_index)
    class_count = class_table.shape[0]
    one_hot = (labels[:, None] == jnp.arange(class_count, dtype=jnp.int32)[None, :]).astype(
        low_type
    )
    embedded = features + jnp.dot(one_hot, class_table, preferred_element_type=float_type)
    embed_act = jax.nn.silu(embedded).astype(low_type)
    modulate = jnp.dot(
        embed_act, embed_weight, preferred_element_type=float_type
    ) + embed_offset.astype(float_type)
    scale_part = modulate[:, :channels]
    vectors = jnp.stack(
        [
            first_gain, first_shift, first_offset, second_gain, second_shift, second_offset,
            third_gain, third_shift,
        ]
    ).astype(float_type)
    x = images.reshape(image_count, pixels, channels)
    hidden, middle, attend, act_one, act_two, stats = forward_call(
        x, vectors, modulate.reshape(image_count, 2, channels), first_kernel, second_kernel
    )
    flattened = x.astype(float_type)
    scaled_one, scaled_two, scaled_three = (stats[:, n : n + 1] for n in (1, 3, 5))
    normed_one = normalize(flattened, stats[:, 0:1], scaled_one)
    normed_two = normalize(hidden, stats[:, 2:3], scaled_two)
    normed_three = normalize(middle, stats[:, 4:5], scaled_three)
    pre_one = normed_one * gain_one + shift_one
    shaped = normed_two * gain_two + shift_two
    pre_two = shaped * (1.0 + scale_part[:, None, :]) + modulate[:, None, channels:]
    attend_input = attend.reshape(image_count * pixels, channels)
    columns_one = backward_patches(padded_grads(act_one.reshape(layout)), stripe_rows, image_width)
    columns_two = backward_patches(padded_grads(act_two.reshape(layout)), stripe_rows, image_width)

    def forward_order(columns):
        return columns.reshape(-1, 9, channels)[:, ::-1].reshape(-1, 9 * channels)

    columns_one, columns_two = forward_order(columns_one), forward_order(columns_two)
    zero_part = jnp.zeros((channels,), low_type)
    joint_bias = jnp.concatenate(
        [joint_offset[:channels], zero_part, joint_offset[channels:]]
    ).astype(float_type)
    joint_rows = (
        jnp.dot(attend_input, joint_weight, preferred_element_type=float_type) + joint_bias
    ).astype(low_type)
    joint_rows = joint_rows.reshape(image_count, pixels, 3 * channels)
    query_local = joint_rows[:, :, :channels]
    key_local = joint_rows[:, :, channels : 2 * channels]
    value_local = joint_rows[:, :, 2 * channels :]
    key_rows, value_rows = (
        lax.all_gather(key_local, "row", axis=1, tiled=True),
        lax.all_gather(value_local, "row", axis=1, tiled=True),
    )
    query_heads = query_local.reshape(image_count, pixels, head_count, HEAD)
    key_heads = key_rows.reshape(image_count, -1, head_count, HEAD)
    value_heads = value_rows.reshape(image_count, -1, head_count, HEAD)
    scores = (
        jnp.einsum("iphd,ikhd->ihpk", query_heads, key_heads, preferred_element_type=float_type)
        * score_scale
    )
    row_peak = jnp.max(scores, axis=-1, keepdims=True)
    raised = jnp.exp(scores - row_peak)
    row_total = jnp.sum(raised, axis=-1, keepdims=True)
    weights = raised / row_total
    log_total = row_peak + jnp.log(row_total)
    weights_low = weights.astype(low_type)
    mixed_rows = jnp.einsum(
        "ihpk,ikhd->iphd", weights_low, value_heads, preferred_element_type=float_type
    )
    mixed_rows = mixed_rows.reshape(image_count * pixels, channels).astype(low_type)
    outcome = (
        middle.reshape(image_count * pixels, channels)
        + jnp.dot(mixed_rows, output_weight, preferred_element_type=float_type)
        + output_offset.astype(float_type)
    )
    result = outcome.astype(low_type).reshape(layout)
    cotangent_low = cotangent.reshape(image_count * pixels, channels)
    upstream = cotangent_low.astype(float_type)
    output_weight_grad = lax.dot_general(
        mixed_rows, cotangent_low, contract_rows, preferred_element_type=float_type
    )
    output_offset_grad = jnp.sum(upstream, axis=0)
    mixed_grad = lax.dot_general(
        cotangent_low, output_weight, contract_cols, preferred_element_type=float_type
    )
    mixed_grad = mixed_grad.astype(low_type).reshape(image_count, pixels, head_count, HEAD)
    scores = (
        jnp.einsum("iphd,ikhd->ihpk", query_heads, key_heads, preferred_element_type=float_type)
        * score_scale
    )
    weights = jnp.exp(scores - log_total)
    weights_low = weights.astype(low_type)
    value_part = jnp.einsum(
        "ihpk,iphd->ikhd", weights_low, mixed_grad, preferred_element_type=float_type
    )
    weight_grad = jnp.einsum(
        "iphd,ikhd->ihpk", mixed_grad, value_heads, preferred_element_type=float_type
    )
    row_inner = jnp.sum(weights * weight_grad, axis=-1, keepdims=True)
    score_grad = (weights * (weight_grad - row_inner)).astype(low_type)
    query_grad = (
        jnp.einsum("ihpk,ikhd->iphd", score_grad, key_heads, preferred_element_type=float_type)
        * score_scale
    )
    key_part = (
        jnp.einsum("ihpk,iphd->ikhd", score_grad, query_heads, preferred_element_type=float_type)
        * score_scale
    )
    key_grad, value_grad = (
        lax.psum_scatter(
            key_part.astype(jnp.bfloat16), "row", scatter_dimension=1, tiled=True
        ).astype(jnp.float32),
        lax.psum_scatter(
            value_part.astype(jnp.bfloat16), "row", scatter_dimension=1, tiled=True
        ).astype(jnp.float32),
    )
    joint_grad = jnp.concatenate(
        [
            query_grad.reshape(image_count * pixels, channels),
            key_grad.reshape(image_count * pixels, channels),
            value_grad.reshape(image_count * pixels, channels),
        ],
        axis=-1,
    ).astype(low_type)
    joint_grad_wide = joint_grad.astype(float_type)
    joint_offset_grad = jnp.concatenate(
        [
            jnp.sum(joint_grad_wide[:, :channels], axis=0),
            jnp.sum(joint_grad_wide[:, 2 * channels :], axis=0),
        ]
    )
    joint_weight_grad = lax.dot_general(
        attend_input, joint_grad, contract_rows, preferred_element_type=float_type
    )
    attend_grad = lax.dot_general(
        joint_grad, joint_weight, contract_cols, preferred_element_type=float_type
    )
    attend_grad = attend_grad.reshape(image_count, pixels, channels)
    third_gain_grad = jnp.sum(attend_grad * normed_three, axis=(0, 1))
    third_shift_grad = jnp.sum(attend_grad, axis=(0, 1))
    middle_grad = upstream.reshape(image_count, pixels, channels) + group_back(
        attend_grad * gain_three, normed_three, scaled_three
    )
    skip_grad = middle_grad * math.sqrt(0.5)
    branch_grad = skip_grad.reshape(image_count * pixels, channels).astype(low_type)
    second_offset_grad = jnp.sum(branch_grad.astype(float_type), axis=0)
    second_kernel_grad = lax.dot_general(
        columns_two, branch_grad, contract_rows, preferred_element_type=float_type
    )
    framed_two = padded_grads(branch_grad.reshape(layout))
    act_two_grad = transpose_product(
        backward_patches(framed_two, stripe_rows, image_width), second_kernel
    )
    pre_two_grad = act_two_grad.reshape(image_count, pixels, channels) * silu_slope(pre_two)
    scale_grad = jnp.sum(pre_two_grad * shaped, axis=1)
    shift_grad = jnp.sum(pre_two_grad, axis=1)
    modulate_grad = jnp.concatenate([scale_grad, shift_grad], axis=-1)
    shaped_grad = pre_two_grad * (1.0 + scale_part[:, None, :])
    second_gain_grad = jnp.sum(shaped_grad * normed_two, axis=(0, 1))
    second_shift_grad = jnp.sum(shaped_grad, axis=(0, 1))
    hidden_grad = group_back(shaped_grad * gain_two, normed_two, scaled_two)
    hidden_grad = hidden_grad.reshape(image_count * pixels, channels).astype(low_type)
    first_offset_grad = jnp.sum(hidden_grad.astype(float_type), axis=0)
    first_kernel_grad = lax.dot_general(
        columns_one, hidden_grad, contract_rows, preferred_element_type=float_type
    )
    framed_one = padded_grads(hidden_grad.reshape(layout))
    act_one_grad = transpose_product(
        backward_patches(framed_one, stripe_rows, image_width), first_kernel
    )
    pre_one_grad = act_one_grad.reshape(image_count, pixels, channels) * silu_slope(pre_one)
    first_gain_grad = jnp.sum(pre_one_grad * normed_one, axis=(0, 1))
    first_shift_grad = jnp.sum(pre_one_grad, axis=(0, 1))
    images_gradient = skip_grad + group_back(pre_one_grad * gain_one, normed_one, scaled_one)
    images_gradient = images_gradient.reshape(layout)
    modulate_grad = lax.psum(modulate_grad, "row")
    every_grad, every_embedded, every_label = lax.all_gather(
        (modulate_grad, embedded, labels), "img", axis=0, tiled=True
    )
    stripe_index = lax.axis_index("row")
    stripe_count = lax.axis_size("row")

    def own_rows(v, axis):
        size = v.shape[axis] // stripe_count
        return lax.dynamic_slice_in_dim(v, stripe_index * size, size, axis)

    every_act = jax.nn.silu(every_embedded).astype(low_type).astype(float_type)
    embed_weight_grad = lax.dot_general(
        own_rows(every_act, 1), every_grad, contract_rows, precision=highest
    )
    embed_offset_grad = own_rows(jnp.sum(every_grad, axis=0), 0)
    active_grad = lax.dot_general(
        every_grad, embed_weight.astype(float_type), contract_cols, precision=highest
    )
    embedded_grad = active_grad * silu_slope(every_embedded)
    own_classes = stripe_index * (class_count // stripe_count) + jnp.arange(
        class_count // stripe_count, dtype=jnp.int32
    )
    own_hot = (every_label[:, None] == own_classes[None, :]).astype(float_type)
    class_table_grad = lax.dot_general(own_hot, embedded_grad, contract_rows, precision=highest)

    def scattered(v):
        v = lax.psum_scatter(v.astype(low_type), "row", scatter_dimension=0, tiled=True)
        return lax.psum(v.astype(low_type), "img").astype(float_type)

    first_kernel_grad, second_kernel_grad, joint_weight_grad, output_weight_grad = (
        scattered(v)
        for v in (first_kernel_grad, second_kernel_grad, joint_weight_grad, output_weight_grad)
    )
    small = (
        first_gain_grad, first_shift_grad, first_offset_grad, second_gain_grad, second_shift_grad,
        second_offset_grad, third_gain_grad, third_shift_grad, joint_offset_grad,
        output_offset_grad,
    )
    summed = lax.psum(jnp.concatenate(small), ("img", "row"))
    pieces, at = [], 0
    for v in small:
        pieces.append(own_rows(summed[at : at + v.shape[0]], 0))
        at += v.shape[0]
    (
        first_gain_grad, first_shift_grad, first_offset_grad, second_gain_grad, second_shift_grad,
        second_offset_grad, third_gain_grad, third_shift_grad, joint_offset_grad,
        output_offset_grad,
    ) = pieces
    return (
        result, images_gradient, first_gain_grad, first_shift_grad, first_kernel_grad,
        first_offset_grad, embed_weight_grad, embed_offset_grad, class_table_grad,
        second_gain_grad, second_shift_grad, second_kernel_grad, second_offset_grad,
        third_gain_grad, third_shift_grad, joint_weight_grad, joint_offset_grad,
        output_weight_grad, output_offset_grad,
    )


def solution(mesh):
    in_specs = (
        (P("img", "row", None, None),) + (P("img"),) * 3 + (P(),) * 17
        + (P("img", "row", None, None),)
    )
    row, rows = P("row"), P("row", None)
    out_specs = (
        P("img", "row", None, None), P("img", "row", None, None), row, row, rows, row, rows, row,
        rows, row, row, rows, row, row, row, rows, row, rows, row,
    )
    return jax.shard_map(shards, mesh=mesh, in_specs=in_specs, out_specs=out_specs, check_vma=False)
```

```python
import math

import jax
import jax.numpy as jnp
from jax import lax
from jax.experimental import pallas as pl
from jax.experimental.pallas import tpu as pltpu
from jax.sharding import PartitionSpec as P

GROUPS = 32
HEAD = 64
EMB = 768
MESH = pl.DeviceIdType.MESH

norm_eps = 1e-05
sigma_least = 0.002
sigma_most = 80.0
sigma_power = 7.0
highest = lax.Precision.HIGHEST
float_type = jnp.float32
low_type = jnp.bfloat16
contract_rows = (((0,), (0,)), ((), ()))
contract_cols = (((1,), (1,)), ((), ()))


def noise_features(level_count, level_index):
    position = (level_index.astype(jnp.float32) + 1.0) / (level_count.astype(jnp.float32) - 1.0)
    low_root = sigma_least ** (1.0 / sigma_power)
    high_root = sigma_most ** (1.0 / sigma_power)
    noise_level = (low_root + position * (high_root - low_root)) ** sigma_power
    noise_time = 250.0 * jnp.log(noise_level)
    half_width = EMB // 2
    frequency = jnp.exp(-math.log(10000.0) * jnp.arange(half_width, dtype=jnp.float32) / half_width)
    angles = noise_time[:, None] * frequency[None, :]
    return jnp.concatenate([jnp.cos(angles), jnp.sin(angles)], axis=-1)


def silu_slope(values):
    sigmoid_part = jax.nn.sigmoid(values)
    return sigmoid_part * (1.0 + values * (1.0 - sigmoid_part))


def normalize(values, centre, scaled):
    return (values - centre) * scaled


def group_fold(v):
    return v.reshape(v.shape[:-1] + (GROUPS, v.shape[-1] // GROUPS))


def group_back(upstream, normed, scaled):
    image_count, pixels, channels = upstream.shape
    first_sum = jnp.sum(group_fold(jnp.sum(upstream, axis=1)), axis=-1)
    second_sum = jnp.sum(group_fold(jnp.sum(upstream * normed, axis=1)), axis=-1)
    first_sum, second_sum = lax.psum((first_sum, second_sum), "row")
    entries = pixels * lax.axis_size("row") * (channels // GROUPS)
    per = channels // GROUPS
    first_sum = jnp.repeat(first_sum / entries, per, axis=-1)
    second_sum = jnp.repeat(second_sum / entries, per, axis=-1)
    return scaled * (upstream - first_sum[:, None, :] - normed * second_sum[:, None, :])


def padded_grads(activity):
    size, length = lax.axis_size("row"), activity.shape[1]
    up = [(i, i + 1) for i in range(size - 1)]
    down = [(j, i) for i, j in up]
    last = lax.slice_in_dim(activity, length - 1, length, axis=1)
    initial = lax.slice_in_dim(activity, 0, 1, axis=1)
    before = lax.ppermute(last, "row", up)
    after = lax.ppermute(initial, "row", down)
    framed = jnp.concatenate([before, activity, after], axis=1)
    return jnp.pad(framed, ((0, 0), (0, 0), (1, 1), (0, 0)))


def backward_patches(framed, stripe_rows, image_width):
    pieces = [
        framed[
            :, 2 - row_tap : 2 - row_tap + stripe_rows, 2 - col_tap : 2 - col_tap + image_width, :
        ]
        for row_tap in range(3)
        for col_tap in range(3)
    ]
    joined = jnp.concatenate(pieces, axis=-1)
    return joined.reshape(-1, joined.shape[-1])


def transpose_product(columns, kernel):
    channels = kernel.shape[1]
    stacked = columns.reshape(columns.shape[0], 9, channels)
    kernel_taps = kernel.reshape(9, kernel.shape[0] // 9, channels)
    return lax.dot_general(
        stacked, kernel_taps, (((1, 2), (0, 2)), ((), ())), preferred_element_type=float_type
    )


def peers():
    i = lax.axis_index("img")
    r = lax.axis_index("row")
    c = lax.rem(r, 2)
    near = r + 1 - 2 * c
    return (i, r, c, {1: (i, near), 2: (i, lax.rem(r + 2, 4)), 3: (i, 3 - r)})


def half_silu(v):
    h = 0.5 * v
    return h * jnp.tanh(h) + h


def col_iota(n, width, channels):
    return lax.rem(lax.broadcasted_iota(jnp.int32, (n, channels), 0), width)


def fill_row(buf, start, act, channels, width):
    col = lax.broadcasted_iota(jnp.int32, (width, channels), 0)
    left = jnp.where(col == 0, 0.0, pltpu.roll(act, 1, 0))
    right = jnp.where(col == width - 1, 0.0, pltpu.roll(act, width - 1, 0))
    rows = pl.ds(start, width)
    buf[rows, 0:channels] = left.astype(low_type)
    buf[rows, channels : 2 * channels] = act.astype(low_type)
    buf[rows, 2 * channels : 3 * channels] = right.astype(low_type)


def pack_stats(first, second):
    channels = first.shape[1]
    row = lax.broadcasted_iota(jnp.int32, (8, channels), 0)

    def terms(v):
        a = v.astype(low_type).astype(float_type)
        b = (v - a).astype(low_type).astype(float_type)
        c = v - a - b
        return jnp.where(row == 0, a, jnp.where(row == 1, b, jnp.where(row == 2, c, 0.0)))

    return jnp.concatenate([terms(first), terms(second)], axis=0).astype(low_type)


def block_ones(channels, per):
    a = lax.broadcasted_iota(jnp.int32, (channels, channels), 0)
    b = lax.broadcasted_iota(jnp.int32, (channels, channels), 1)
    a = lax.shift_right_logical(a * 43691, 19)
    b = lax.shift_right_logical(b * 43691, 19)
    return jnp.where(a == b, 1.0, 0.0).astype(low_type)


def combine_stats(parts, ones, entries):
    total = jnp.dot(jnp.concatenate(parts, axis=0), ones, preferred_element_type=float_type)
    first = total[0:8] + total[16:24] + total[32:40] + total[48:56]
    second = total[8:16] + total[24:32] + total[40:48] + total[56:64]
    first = jnp.sum(first, axis=0, keepdims=True) * (1.0 / entries)
    second = jnp.sum(second, axis=0, keepdims=True) * (1.0 / entries)
    return first, second


def forward_kernel(
    x_ref, vec_ref, mod_ref, w1_any, w2_any,
    hid_ref, mid_ref, att_ref, act1_ref, act2_ref, st_ref,
    w1, w2, ones, abuf, m1, m3, got, wsem, ssem, rsem,
):
    images, pixels, channels = x_ref.shape
    width = 32
    edge = pixels - width
    entries = 4.0 * pixels * (channels // GROUPS)
    i, r, c, who = peers()
    load1 = pltpu.make_async_copy(w1_any, w1, wsem.at[0])
    load2 = pltpu.make_async_copy(w2_any, w2, wsem.at[1])
    load1.start()
    load2.start()
    barrier = pltpu.get_barrier_semaphore()
    for k in (1, 2, 3):
        pl.semaphore_signal(barrier, inc=1, device_id=who[k], device_id_type=MESH)
    ones[...] = block_ones(channels, channels // GROUPS)
    inner = pl.multiple_of(edge * (1 - c), width)
    outer = pl.multiple_of(edge * c, width)
    inner_live = None
    outer_live = jnp.logical_and(r > 0, r < 3)
    stat = pl.ds(0, 16)
    halo = pl.ds(16, width)

    def copies(p, b):
        full = p < 2
        rows = pl.ds(0, 48) if full else stat
        return [
            pltpu.make_async_remote_copy(
                src.at[p, b, rs], got.at[p, b, k - 1, rs], ssem.at[p, b, k - 1],
                rsem.at[p, b, k - 1], device_id=who[k], device_id_type=MESH,
            )
            for k, src, rs in ((1, m1, rows), (2, m1, stat), (3, m3, rows))
        ]

    def send(p, b, first, second, edges):
        packed = pack_stats(first, second)
        m1[p, b, 0:16] = packed
        m3[p, b, 0:16] = packed
        if edges is not None:
            m1[p, b, 16:48] = edges(inner)
            m3[p, b, 16:48] = edges(outer)
        for cp in copies(p, b):
            cp.start()

    def receive(p, b):
        for cp in copies(p, b):
            cp.wait_recv()
        parts = [m1[p, b, 0:16]] + [got[p, b, k, 0:16] for k in range(3)]
        first, second = combine_stats(parts, ones[...], entries)
        return first, lax.rsqrt(second - first * first + norm_eps)

    def expand(p, b, affine, own, keep):
        for row in range(pixels // width):
            a = half_silu(affine(own(row)))
            keep[b, pl.ds(row * width, width)] = a.astype(low_type)
            fill_row(abuf, (row + 1) * width, a, channels, width)
        a = half_silu(affine(got[p, b, 0, 16:48].astype(float_type)))
        fill_row(abuf, pl.multiple_of((pixels + width) * (1 - c), width), a, channels, width)
        a = half_silu(affine(got[p, b, 2, 16:48].astype(float_type)))
        a = jnp.where(outer_live, a, 0.0)
        fill_row(abuf, pl.multiple_of((pixels + width) * c, width), a, channels, width)

    def convolve(w):
        depth = 3 * channels
        return sum(
            jnp.dot(
                abuf[width * dy : width * dy + pixels, :],
                w[depth * dy : depth * (dy + 1), :],
                preferred_element_type=float_type,
            )
            for dy in range(3)
        )

    def vec(n):
        return vec_ref[n : n + 1, :]

    pl.semaphore_wait(barrier, 3)

    def step0(b, _):
        v = x_ref[b].astype(float_type)
        send(
            0, b, jnp.sum(v, axis=0, keepdims=True), jnp.sum(v * v, axis=0, keepdims=True),
            lambda at: x_ref[b, pl.ds(at, width)],
        )
        return 0

    lax.fori_loop(0, images, step0, 0)
    load1.wait()

    def step1(b, _):
        centre, scaled = receive(0, b)
        st_ref[b, 0:1] = centre
        st_ref[b, 1:2] = scaled
        slope = scaled * vec(0)
        shift = vec(1)
        expand(
            0, b, lambda v: (v - centre) * slope + shift,
            lambda row: x_ref[b, pl.ds(row * width, width)].astype(float_type), act1_ref,
        )
        hidden = convolve(w1) + vec(2)
        hid_ref[b] = hidden
        send(
            1, b, jnp.sum(hidden, axis=0, keepdims=True),
            jnp.sum(hidden * hidden, axis=0, keepdims=True),
            lambda at: hid_ref[b, pl.ds(at, width)].astype(low_type),
        )
        return 0

    lax.fori_loop(0, images, step1, 0)
    load2.wait()

    def step2(b, _):
        centre, scaled = receive(1, b)
        st_ref[b, 2:3] = centre
        st_ref[b, 3:4] = scaled
        grow = 1.0 + mod_ref[b, 0:1]
        slope = scaled * vec(3) * grow
        shift = vec(4) * grow + mod_ref[b, 1:2]
        expand(
            1, b, lambda v: (v - centre) * slope + shift,
            lambda row: hid_ref[b, pl.ds(row * width, width)], act2_ref,
        )
        middle = (convolve(w2) + vec(5) + x_ref[b].astype(float_type)) * math.sqrt(0.5)
        mid_ref[b] = middle
        send(
            2, b, jnp.sum(middle, axis=0, keepdims=True),
            jnp.sum(middle * middle, axis=0, keepdims=True), None,
        )
        return 0

    lax.fori_loop(0, images, step2, 0)

    def step3(b, _):
        centre, scaled = receive(2, b)
        st_ref[b, 4:5] = centre
        st_ref[b, 5:6] = scaled
        slope = scaled * vec(6)
        att_ref[b] = ((mid_ref[b] - centre) * slope + vec(7)).astype(low_type)
        for p in range(3):
            for cp in copies(p, b):
                cp.wait_send()
        return 0

    lax.fori_loop(0, images, step3, 0)


def forward_call(x, vectors, modulate, first_kernel, second_kernel):
    images, pixels, channels = x.shape
    depth = 9 * channels
    vm = pl.BlockSpec(memory_space=pltpu.VMEM)
    hbm = pl.BlockSpec(memory_space=pl.ANY)
    wide = jax.ShapeDtypeStruct(x.shape, float_type)
    low = jax.ShapeDtypeStruct(x.shape, low_type)
    return pl.pallas_call(
        forward_kernel,
        out_shape=(wide, wide, low, low, low, jax.ShapeDtypeStruct((images, 8, channels), float_type)),
        in_specs=[vm, vm, vm, hbm, hbm],
        out_specs=(vm,) * 6,
        scratch_shapes=[
            pltpu.VMEM((depth, channels), low_type),
            pltpu.VMEM((depth, channels), low_type),
            pltpu.VMEM((channels, channels), low_type),
            pltpu.VMEM((pixels + 64, 3 * channels), low_type),
            pltpu.VMEM((3, images, 48, channels), low_type),
            pltpu.VMEM((3, images, 48, channels), low_type),
            pltpu.VMEM((3, images, 3, 48, channels), low_type),
            pltpu.SemaphoreType.DMA((2,)),
            pltpu.SemaphoreType.DMA((3, images, 3)),
            pltpu.SemaphoreType.DMA((3, images, 3)),
        ],
        compiler_params=pltpu.CompilerParams(
            collective_id=0, has_side_effects=True, vmem_limit_bytes=56 << 20
        ),
        name="forward",
    )(x, vectors, modulate, first_kernel, second_kernel)


def attention_kernel(
    att_ref, mid_ref, cot_ref, vec_ref, jw_any, ow_any,
    res_ref, ag_ref, gj_ref, go_ref, gs_ref,
    jw, ow, att, att_t, kv, kv_t, q8, d_out_t, qm, dom, s_ref, eb, dsb, mix_t, dq_t, dq, dkv,
    part, got_core, to_x, got_x, wsem, gsem, hsem, asem, bsem,
):
    images, pixels, channels = att_ref.shape
    whole = 4 * pixels
    chunk = 128
    pair_lanes = 2 * HEAD
    pairs = channels // pair_lanes
    i, r, c, who = peers()
    loads = [
        pltpu.make_async_copy(jw_any, jw, wsem.at[0]),
        pltpu.make_async_copy(ow_any, ow, wsem.at[1]),
    ]
    for cp in loads:
        cp.start()
    barrier = pltpu.get_barrier_semaphore()
    for k in (1, 2):
        pl.semaphore_signal(barrier, inc=1, device_id=who[k], device_id_type=MESH)

    def block(n):
        return pl.ds(pl.multiple_of(n * pixels, pixels), pixels)

    def shares(b):
        own, far = block(r), block(lax.rem(r + 2, 4))
        return [
            pltpu.make_async_remote_copy(
                att.at[b, rows], att.at[b, rows], gsem.at[b, n], hsem.at[b, n],
                device_id=who[k], device_id_type=MESH,
            )
            for n, (rows, k) in enumerate(((own, 1), (own, 2), (far, 1)))
        ]

    def arrivals(b):
        mate = r + 1 - 2 * c
        rows = (block(mate), block(lax.rem(r + 2, 4)), block(lax.rem(mate + 2, 4)))
        return [
            pltpu.make_async_remote_copy(
                att.at[b, w], att.at[b, w], gsem.at[b, n], hsem.at[b, n],
                device_id=who[(1, 2, 1)[n]], device_id_type=MESH,
            )
            for n, w in enumerate(rows)
        ]

    def forward(b):
        arrivals(b)[1].wait_recv()
        shares(b)[2].start()

    def sums_core(b):
        return [
            pltpu.make_async_remote_copy(
                part.at[b, block(2 * n + 1 - c)], got_core.at[b, n], asem.at[b, n], bsem.at[b, n],
                device_id=who[1], device_id_type=MESH,
            )
            for n in range(2)
        ]

    def sum_x(b):
        return pltpu.make_async_remote_copy(
            to_x.at[b], got_x.at[b], asem.at[b, 2], bsem.at[b, 2],
            device_id=who[2], device_id_type=MESH,
        )

    def pass_on(b):
        x = lax.div(r, 2)
        for cp in sums_core(b):
            cp.wait_recv()
        far = 1 - x
        to_x[b] = (
            part[b, block(2 * far + c)].astype(float_type) + got_core[b, far].astype(float_type)
        ).astype(low_type)
        sum_x(b).start()
        ag_ref[b] = part[b, block(r)].astype(float_type) + got_core[b, x].astype(float_type)

    def keep_own(b, _):
        att[b, block(r)] = att_ref[b]
        return 0

    lax.fori_loop(0, images, keep_own, 0)
    pl.semaphore_wait(barrier, 2)
    for b in range(images):
        shares(b)[0].start()
        shares(b)[1].start()
    for cp in loads:
        cp.wait()
    forward(0)
    lane = lax.broadcasted_iota(jnp.int32, (pixels, pair_lanes), 1)

    def masked(v):
        return jnp.concatenate(
            [jnp.where(lane < HEAD, v, 0.0), jnp.where(lane >= HEAD, v, 0.0)], axis=0
        ).astype(low_type)

    def dot(a, b):
        return jnp.dot(a, b, preferred_element_type=float_type)

    def dot_nt(a, b):
        return lax.dot_general(a, b, contract_cols, preferred_element_type=float_type)

    def one_image(b, _):
        a = arrivals(b)
        a[0].wait_recv()
        a[2].wait_recv()
        bias = jnp.concatenate([jnp.zeros((1, channels), float_type), vec_ref[1:2]], axis=1)
        for n in range(4):
            rows = pl.ds(n * pixels, pixels)
            kv[rows] = (dot(att[b, rows], jw[:, channels:]) + bias).astype(low_type)
        for n in range(2 * channels // 128):
            cols = pl.ds(n * 128, 128)
            kv_t[cols, :] = kv[:, cols].T
        q = (dot(att_ref[b], jw[:, :channels]) + vec_ref[0:1]).astype(low_type)
        q8[...] = (q.astype(float_type) * HEAD ** (-0.5)).astype(low_type)
        d_out = dot_nt(cot_ref[b], ow[...]).astype(low_type).astype(float_type)
        d_out_t[...] = d_out.T

        @pl.when(b > 0)
        def _():
            pass_on(b - 1)

        def one_pair(t, _):
            lanes = pl.ds(pl.multiple_of(t * pair_lanes, pair_lanes), pair_lanes)
            v_lanes = pl.ds(pl.multiple_of(channels + t * pair_lanes, pair_lanes), pair_lanes)
            qm[...] = masked(q8[:, lanes].astype(float_type))
            peak = None
            for n in range(whole // chunk):
                rows = pl.ds(n * chunk, chunk)
                s = dot_nt(kv[rows, lanes], qm[...])
                s_ref[rows] = s
                top = jnp.max(s.reshape(chunk // 8, 8, 2 * pixels), axis=0)
                peak = top if peak is None else jnp.maximum(peak, top)
            peak = jnp.max(peak, axis=0, keepdims=True)
            total = None
            for n in range(whole // chunk):
                rows = pl.ds(n * chunk, chunk)
                e = jnp.exp(s_ref[rows] - peak)
                eb[rows] = e.astype(low_type)
                more = jnp.sum(e.reshape(chunk // 8, 8, 2 * pixels), axis=0)
                total = more if total is None else total + more
            over = 1.0 / jnp.sum(total, axis=0, keepdims=True)
            inner, scaled = [], []
            for j in range(2):
                head = pl.ds(pl.multiple_of(t * pair_lanes + j * HEAD, HEAD), HEAD)
                v_head = pl.ds(pl.multiple_of(channels + t * pair_lanes + j * HEAD, HEAD), HEAD)
                cols = slice(j * pixels, (j + 1) * pixels)
                mt = dot(kv_t[v_head, :], eb[:, cols]) * over[:, cols]
                mix_t[b, head] = mt.astype(low_type)
                g = (d_out_t[head] * over[:, cols]).astype(low_type).astype(float_type)
                inner.append(jnp.sum(g * mt, axis=0, keepdims=True))
                scaled.append(g)
            inner = jnp.concatenate(inner, axis=1)
            dom[...] = masked(jnp.concatenate(scaled, axis=0).T)
            for n in range(whole // chunk):
                rows = pl.ds(n * chunk, chunk)
                dp = dot_nt(kv[rows, v_lanes], dom[...])
                dsb[rows] = (eb[rows].astype(float_type) * (dp - inner)).astype(low_type)
            for j in range(2):
                head = pl.ds(pl.multiple_of(t * pair_lanes + j * HEAD, HEAD), HEAD)
                cols = slice(j * pixels, (j + 1) * pixels)
                dq_t[head] = dot(kv_t[head, :], dsb[:, cols]) * HEAD ** (-0.5)
            dkv[b, :, lanes] = dot(dsb[...], qm[...]).astype(low_type)
            dkv[b, :, v_lanes] = dot(eb[...], dom[...]).astype(low_type)
            return 0

        lax.fori_loop(0, pairs, one_pair, 0)
        dq[b] = dq_t[...].T.astype(low_type)
        for n in range(4):
            rows = pl.ds(n * pixels, pixels)
            part[b, rows] = dot_nt(dkv[b, rows], jw[:, channels:]).astype(low_type)
        part[b, block(r)] = (
            part[b, block(r)].astype(float_type) + dot_nt(dq[b], jw[:, :channels])
        ).astype(low_type)
        for cp in sums_core(b):
            cp.start()

        @pl.when(b + 1 < images)
        def _():
            forward(b + 1)

        mixed = mix_t[b].T
        res_ref[b] = (mid_ref[b] + dot(mixed, ow[...]) + vec_ref[2:3]).astype(low_type)
        return 0

    lax.fori_loop(0, images, one_image, 0)
    pass_on(images - 1)
    ones = jnp.ones((16, whole), low_type)
    for b in range(images):
        att_t[b, 0:channels] = att[b].T
        att_t[b, channels:] = ones
    kv_sum = None
    q_sum = None
    o_sum = None
    for b in range(images):
        more = dot(att_t[b], dkv[b])
        kv_sum = more if kv_sum is None else kv_sum + more
        more = dot(att_t[b, :, block(r)], dq[b])
        q_sum = more if q_sum is None else q_sum + more
        more = dot(mix_t[b], cot_ref[b])
        o_sum = more if o_sum is None else o_sum + more
    gj_ref[:, :channels] = q_sum[:channels]
    gj_ref[:, channels:] = kv_sum[:channels]
    go_ref[...] = o_sum
    cot_sum = jnp.sum(jnp.sum(cot_ref[...].astype(float_type), axis=0), axis=0, keepdims=True)
    gs_ref[0:1] = q_sum[channels : channels + 1]
    gs_ref[1:2] = kv_sum[channels : channels + 1, channels:]
    gs_ref[2:3] = cot_sum
    for b in range(images):
        sum_x(b).wait_recv()
        ag_ref[b] += got_x[b].astype(float_type)
    for b in range(images):
        for cp in shares(b) + sums_core(b) + [sum_x(b)]:
            cp.wait_send()


def attention_call(att, middle, cot, vectors, joint_weight, output_weight):
    images, pixels, channels = att.shape
    whole = 4 * pixels
    vm = pl.BlockSpec(memory_space=pltpu.VMEM)
    hbm = pl.BlockSpec(memory_space=pl.ANY)

    def low(*shape):
        return pltpu.VMEM(shape, low_type)

    def wide(*shape):
        return pltpu.VMEM(shape, float_type)

    return pl.pallas_call(
        attention_kernel,
        out_shape=(
            jax.ShapeDtypeStruct(att.shape, low_type),
            jax.ShapeDtypeStruct(att.shape, float_type),
            jax.ShapeDtypeStruct(joint_weight.shape, float_type),
            jax.ShapeDtypeStruct(output_weight.shape, float_type),
            jax.ShapeDtypeStruct((8, channels), float_type),
        ),
        in_specs=[vm, vm, vm, vm, hbm, hbm],
        out_specs=(vm,) * 5,
        scratch_shapes=[
            low(channels, 3 * channels), low(channels, channels), low(images, whole, channels),
            low(images, channels + 16, whole), low(whole, 2 * channels), low(2 * channels, whole),
            low(pixels, channels), wide(channels, pixels), low(2 * pixels, 2 * HEAD),
            low(2 * pixels, 2 * HEAD), wide(whole, 2 * pixels), low(whole, 2 * pixels),
            low(whole, 2 * pixels), low(images, channels, pixels), wide(channels, pixels),
            low(images, pixels, channels), low(images, whole, 2 * channels),
            low(images, whole, channels), low(images, 2, pixels, channels),
            low(images, pixels, channels), low(images, pixels, channels),
            pltpu.SemaphoreType.DMA((2,)), pltpu.SemaphoreType.DMA((images, 3)),
            pltpu.SemaphoreType.DMA((images, 3)), pltpu.SemaphoreType.DMA((images, 3)),
            pltpu.SemaphoreType.DMA((images, 3)),
        ],
        compiler_params=pltpu.CompilerParams(
            collective_id=1, has_side_effects=True, vmem_limit_bytes=56 << 20
        ),
        name="attention",
    )(att, middle, cot, vectors, joint_weight, output_weight)


def shards(
    images,
    level_count,
    level_index,
    labels,
    first_gain,
    first_shift,
    first_kernel,
    first_offset,
    embed_weight,
    embed_offset,
    class_table,
    second_gain,
    second_shift,
    second_kernel,
    second_offset,
    third_gain,
    third_shift,
    joint_weight,
    joint_offset,
    output_weight,
    output_offset,
    cotangent,
):
    image_count, stripe_rows, image_width, channels = images.shape
    layout = (image_count, stripe_rows, image_width, channels)
    pixels = stripe_rows * image_width
    gain_one = first_gain.astype(float_type)
    shift_one = first_shift.astype(float_type)
    gain_two = second_gain.astype(float_type)
    shift_two = second_shift.astype(float_type)
    gain_three = third_gain.astype(float_type)
    features = noise_features(level_count, level_index)
    class_count = class_table.shape[0]
    one_hot = (labels[:, None] == jnp.arange(class_count, dtype=jnp.int32)[None, :]).astype(
        low_type
    )
    embedded = features + jnp.dot(one_hot, class_table, preferred_element_type=float_type)
    embed_act = jax.nn.silu(embedded).astype(low_type)
    modulate = jnp.dot(
        embed_act, embed_weight, preferred_element_type=float_type
    ) + embed_offset.astype(float_type)
    scale_part = modulate[:, :channels]
    vectors = jnp.stack(
        [
            first_gain, first_shift, first_offset, second_gain, second_shift, second_offset,
            third_gain, third_shift,
        ]
    ).astype(float_type)
    x = images.reshape(image_count, pixels, channels)
    hidden, middle, attend, act_one, act_two, stats = forward_call(
        x, vectors, modulate.reshape(image_count, 2, channels), first_kernel, second_kernel
    )
    flattened = x.astype(float_type)
    scaled_one, scaled_two, scaled_three = (stats[:, n : n + 1] for n in (1, 3, 5))
    normed_one = normalize(flattened, stats[:, 0:1], scaled_one)
    normed_two = normalize(hidden, stats[:, 2:3], scaled_two)
    normed_three = normalize(middle, stats[:, 4:5], scaled_three)
    pre_one = normed_one * gain_one + shift_one
    shaped = normed_two * gain_two + shift_two
    pre_two = shaped * (1.0 + scale_part[:, None, :]) + modulate[:, None, channels:]
    columns_one = backward_patches(padded_grads(act_one.reshape(layout)), stripe_rows, image_width)
    columns_two = backward_patches(padded_grads(act_two.reshape(layout)), stripe_rows, image_width)

    def forward_order(columns):
        return columns.reshape(-1, 9, channels)[:, ::-1].reshape(-1, 9 * channels)

    columns_one, columns_two = forward_order(columns_one), forward_order(columns_two)
    attention_vectors = jnp.stack(
        [joint_offset[:channels], joint_offset[channels:], output_offset]
    ).astype(float_type)
    cot = cotangent.reshape(image_count, pixels, channels)
    result, attend_grad, joint_weight_grad, output_weight_grad, sums = attention_call(
        attend, middle, cot, attention_vectors, joint_weight, output_weight
    )
    result = result.reshape(layout)
    joint_offset_grad = jnp.concatenate([sums[0], sums[1]])
    output_offset_grad = sums[2]
    upstream = cot.astype(float_type)
    third_gain_grad = jnp.sum(attend_grad * normed_three, axis=(0, 1))
    third_shift_grad = jnp.sum(attend_grad, axis=(0, 1))
    middle_grad = upstream.reshape(image_count, pixels, channels) + group_back(
        attend_grad * gain_three, normed_three, scaled_three
    )
    skip_grad = middle_grad * math.sqrt(0.5)
    branch_grad = skip_grad.reshape(image_count * pixels, channels).astype(low_type)
    second_offset_grad = jnp.sum(branch_grad.astype(float_type), axis=0)
    second_kernel_grad = lax.dot_general(
        columns_two, branch_grad, contract_rows, preferred_element_type=float_type
    )
    framed_two = padded_grads(branch_grad.reshape(layout))
    act_two_grad = transpose_product(
        backward_patches(framed_two, stripe_rows, image_width), second_kernel
    )
    pre_two_grad = act_two_grad.reshape(image_count, pixels, channels) * silu_slope(pre_two)
    scale_grad = jnp.sum(pre_two_grad * shaped, axis=1)
    shift_grad = jnp.sum(pre_two_grad, axis=1)
    modulate_grad = jnp.concatenate([scale_grad, shift_grad], axis=-1)
    shaped_grad = pre_two_grad * (1.0 + scale_part[:, None, :])
    second_gain_grad = jnp.sum(shaped_grad * normed_two, axis=(0, 1))
    second_shift_grad = jnp.sum(shaped_grad, axis=(0, 1))
    hidden_grad = group_back(shaped_grad * gain_two, normed_two, scaled_two)
    hidden_grad = hidden_grad.reshape(image_count * pixels, channels).astype(low_type)
    first_offset_grad = jnp.sum(hidden_grad.astype(float_type), axis=0)
    first_kernel_grad = lax.dot_general(
        columns_one, hidden_grad, contract_rows, preferred_element_type=float_type
    )
    framed_one = padded_grads(hidden_grad.reshape(layout))
    act_one_grad = transpose_product(
        backward_patches(framed_one, stripe_rows, image_width), first_kernel
    )
    pre_one_grad = act_one_grad.reshape(image_count, pixels, channels) * silu_slope(pre_one)
    first_gain_grad = jnp.sum(pre_one_grad * normed_one, axis=(0, 1))
    first_shift_grad = jnp.sum(pre_one_grad, axis=(0, 1))
    images_gradient = skip_grad + group_back(pre_one_grad * gain_one, normed_one, scaled_one)
    images_gradient = images_gradient.reshape(layout)
    modulate_grad = lax.psum(modulate_grad, "row")
    every_grad, every_embedded, every_label = lax.all_gather(
        (modulate_grad, embedded, labels), "img", axis=0, tiled=True
    )
    stripe_index = lax.axis_index("row")
    stripe_count = lax.axis_size("row")

    def own_rows(v, axis):
        size = v.shape[axis] // stripe_count
        return lax.dynamic_slice_in_dim(v, stripe_index * size, size, axis)

    every_act = jax.nn.silu(every_embedded).astype(low_type).astype(float_type)
    embed_weight_grad = lax.dot_general(
        own_rows(every_act, 1), every_grad, contract_rows, precision=highest
    )
    embed_offset_grad = own_rows(jnp.sum(every_grad, axis=0), 0)
    active_grad = lax.dot_general(
        every_grad, embed_weight.astype(float_type), contract_cols, precision=highest
    )
    embedded_grad = active_grad * silu_slope(every_embedded)
    own_classes = stripe_index * (class_count // stripe_count) + jnp.arange(
        class_count // stripe_count, dtype=jnp.int32
    )
    own_hot = (every_label[:, None] == own_classes[None, :]).astype(float_type)
    class_table_grad = lax.dot_general(own_hot, embedded_grad, contract_rows, precision=highest)

    def scattered(v):
        v = lax.psum_scatter(v.astype(low_type), "row", scatter_dimension=0, tiled=True)
        return lax.psum(v.astype(low_type), "img").astype(float_type)

    first_kernel_grad, second_kernel_grad, joint_weight_grad, output_weight_grad = (
        scattered(v)
        for v in (first_kernel_grad, second_kernel_grad, joint_weight_grad, output_weight_grad)
    )
    small = (
        first_gain_grad, first_shift_grad, first_offset_grad, second_gain_grad, second_shift_grad,
        second_offset_grad, third_gain_grad, third_shift_grad, joint_offset_grad,
        output_offset_grad,
    )
    summed = lax.psum(jnp.concatenate(small), ("img", "row"))
    pieces, at = [], 0
    for v in small:
        pieces.append(own_rows(summed[at : at + v.shape[0]], 0))
        at += v.shape[0]
    (
        first_gain_grad, first_shift_grad, first_offset_grad, second_gain_grad, second_shift_grad,
        second_offset_grad, third_gain_grad, third_shift_grad, joint_offset_grad,
        output_offset_grad,
    ) = pieces
    return (
        result, images_gradient, first_gain_grad, first_shift_grad, first_kernel_grad,
        first_offset_grad, embed_weight_grad, embed_offset_grad, class_table_grad,
        second_gain_grad, second_shift_grad, second_kernel_grad, second_offset_grad,
        third_gain_grad, third_shift_grad, joint_weight_grad, joint_offset_grad,
        output_weight_grad, output_offset_grad,
    )


def solution(mesh):
    in_specs = (
        (P("img", "row", None, None),) + (P("img"),) * 3 + (P(),) * 17
        + (P("img", "row", None, None),)
    )
    row, rows = P("row"), P("row", None)
    out_specs = (
        P("img", "row", None, None), P("img", "row", None, None), row, row, rows, row, rows, row,
        rows, row, row, rows, row, row, row, rows, row, rows, row,
    )
    return jax.shard_map(shards, mesh=mesh, in_specs=in_specs, out_specs=out_specs, check_vma=False)
```

```python
import math

import jax
import jax.numpy as jnp
from jax import lax
from jax.experimental import pallas as pl
from jax.experimental.pallas import tpu as pltpu
from jax.sharding import PartitionSpec as P

GROUPS = 32
HEAD = 64
EMB = 768
MESH = pl.DeviceIdType.MESH

norm_eps = 1e-05
sigma_least = 0.002
sigma_most = 80.0
sigma_power = 7.0
highest = lax.Precision.HIGHEST
float_type = jnp.float32
low_type = jnp.bfloat16
contract_rows = (((0,), (0,)), ((), ()))
contract_cols = (((1,), (1,)), ((), ()))


def noise_features(level_count, level_index):
    position = (level_index.astype(jnp.float32) + 1.0) / (level_count.astype(jnp.float32) - 1.0)
    low_root = sigma_least ** (1.0 / sigma_power)
    high_root = sigma_most ** (1.0 / sigma_power)
    noise_level = (low_root + position * (high_root - low_root)) ** sigma_power
    noise_time = 250.0 * jnp.log(noise_level)
    half_width = EMB // 2
    frequency = jnp.exp(-math.log(10000.0) * jnp.arange(half_width, dtype=jnp.float32) / half_width)
    angles = noise_time[:, None] * frequency[None, :]
    return jnp.concatenate([jnp.cos(angles), jnp.sin(angles)], axis=-1)


def silu_slope(values):
    sigmoid_part = jax.nn.sigmoid(values)
    return sigmoid_part * (1.0 + values * (1.0 - sigmoid_part))


def normalize(values, centre, scaled):
    return (values - centre) * scaled


def group_fold(v):
    return v.reshape(v.shape[:-1] + (GROUPS, v.shape[-1] // GROUPS))


def group_back(upstream, normed, scaled):
    image_count, pixels, channels = upstream.shape
    first_sum = jnp.sum(group_fold(jnp.sum(upstream, axis=1)), axis=-1)
    second_sum = jnp.sum(group_fold(jnp.sum(upstream * normed, axis=1)), axis=-1)
    first_sum, second_sum = lax.psum((first_sum, second_sum), "row")
    entries = pixels * lax.axis_size("row") * (channels // GROUPS)
    per = channels // GROUPS
    first_sum = jnp.repeat(first_sum / entries, per, axis=-1)
    second_sum = jnp.repeat(second_sum / entries, per, axis=-1)
    return scaled * (upstream - first_sum[:, None, :] - normed * second_sum[:, None, :])


def padded_grads(activity):
    size, length = lax.axis_size("row"), activity.shape[1]
    up = [(i, i + 1) for i in range(size - 1)]
    down = [(j, i) for i, j in up]
    last = lax.slice_in_dim(activity, length - 1, length, axis=1)
    initial = lax.slice_in_dim(activity, 0, 1, axis=1)
    before = lax.ppermute(last, "row", up)
    after = lax.ppermute(initial, "row", down)
    framed = jnp.concatenate([before, activity, after], axis=1)
    return jnp.pad(framed, ((0, 0), (0, 0), (1, 1), (0, 0)))


def backward_patches(framed, stripe_rows, image_width):
    pieces = [
        framed[
            :, 2 - row_tap : 2 - row_tap + stripe_rows, 2 - col_tap : 2 - col_tap + image_width, :
        ]
        for row_tap in range(3)
        for col_tap in range(3)
    ]
    joined = jnp.concatenate(pieces, axis=-1)
    return joined.reshape(-1, joined.shape[-1])


def transpose_product(columns, kernel):
    channels = kernel.shape[1]
    stacked = columns.reshape(columns.shape[0], 9, channels)
    kernel_taps = kernel.reshape(9, kernel.shape[0] // 9, channels)
    return lax.dot_general(
        stacked, kernel_taps, (((1, 2), (0, 2)), ((), ())), preferred_element_type=float_type
    )


def peers():
    i = lax.axis_index("img")
    r = lax.axis_index("row")
    c = lax.rem(r, 2)
    near = r + 1 - 2 * c
    return (i, r, c, {1: (i, near), 2: (i, lax.rem(r + 2, 4)), 3: (i, 3 - r)})


def half_silu(v):
    h = 0.5 * v
    return h * jnp.tanh(h) + h


def col_iota(n, width, channels):
    return lax.rem(lax.broadcasted_iota(jnp.int32, (n, channels), 0), width)


def fill_row(buf, start, act, channels, width):
    col = lax.broadcasted_iota(jnp.int32, (width, channels), 0)
    left = jnp.where(col == 0, 0.0, pltpu.roll(act, 1, 0))
    right = jnp.where(col == width - 1, 0.0, pltpu.roll(act, width - 1, 0))
    rows = pl.ds(start, width)
    buf[rows, 0:channels] = left.astype(low_type)
    buf[rows, channels : 2 * channels] = act.astype(low_type)
    buf[rows, 2 * channels : 3 * channels] = right.astype(low_type)


def pack_stats(first, second):
    channels = first.shape[1]
    row = lax.broadcasted_iota(jnp.int32, (8, channels), 0)

    def terms(v):
        a = v.astype(low_type).astype(float_type)
        b = (v - a).astype(low_type).astype(float_type)
        c = v - a - b
        return jnp.where(row == 0, a, jnp.where(row == 1, b, jnp.where(row == 2, c, 0.0)))

    return jnp.concatenate([terms(first), terms(second)], axis=0).astype(low_type)


def block_ones(channels, per):
    a = lax.broadcasted_iota(jnp.int32, (channels, channels), 0)
    b = lax.broadcasted_iota(jnp.int32, (channels, channels), 1)
    a = lax.shift_right_logical(a * 43691, 19)
    b = lax.shift_right_logical(b * 43691, 19)
    return jnp.where(a == b, 1.0, 0.0).astype(low_type)


def combine_stats(parts, ones, entries):
    total = jnp.dot(jnp.concatenate(parts, axis=0), ones, preferred_element_type=float_type)
    first = total[0:8] + total[16:24] + total[32:40] + total[48:56]
    second = total[8:16] + total[24:32] + total[40:48] + total[56:64]
    first = jnp.sum(first, axis=0, keepdims=True) * (1.0 / entries)
    second = jnp.sum(second, axis=0, keepdims=True) * (1.0 / entries)
    return first, second


def forward_kernel(
    x_ref, vec_ref, mod_ref, w1_any, w2_any,
    hid_ref, mid_ref, att_ref, act1_ref, act2_ref, st_ref,
    w1, w2, ones, abuf, m1, m3, got, wsem, ssem, rsem,
):
    images, pixels, channels = x_ref.shape
    width = 32
    edge = pixels - width
    entries = 4.0 * pixels * (channels // GROUPS)
    i, r, c, who = peers()
    load1 = pltpu.make_async_copy(w1_any, w1, wsem.at[0])
    load2 = pltpu.make_async_copy(w2_any, w2, wsem.at[1])
    load1.start()
    load2.start()
    barrier = pltpu.get_barrier_semaphore()
    for k in (1, 2, 3):
        pl.semaphore_signal(barrier, inc=1, device_id=who[k], device_id_type=MESH)
    ones[...] = block_ones(channels, channels // GROUPS)
    inner = pl.multiple_of(edge * (1 - c), width)
    outer = pl.multiple_of(edge * c, width)
    inner_live = None
    outer_live = jnp.logical_and(r > 0, r < 3)
    stat = pl.ds(0, 16)
    halo = pl.ds(16, width)

    def copies(p, b):
        full = p < 2
        rows = pl.ds(0, 48) if full else stat
        return [
            pltpu.make_async_remote_copy(
                src.at[p, b, rs], got.at[p, b, k - 1, rs], ssem.at[p, b, k - 1],
                rsem.at[p, b, k - 1], device_id=who[k], device_id_type=MESH,
            )
            for k, src, rs in ((1, m1, rows), (2, m1, stat), (3, m3, rows))
        ]

    def send(p, b, first, second, edges):
        packed = pack_stats(first, second)
        m1[p, b, 0:16] = packed
        m3[p, b, 0:16] = packed
        if edges is not None:
            m1[p, b, 16:48] = edges(inner)
            m3[p, b, 16:48] = edges(outer)
        for cp in copies(p, b):
            cp.start()

    def receive(p, b):
        for cp in copies(p, b):
            cp.wait_recv()
        parts = [m1[p, b, 0:16]] + [got[p, b, k, 0:16] for k in range(3)]
        first, second = combine_stats(parts, ones[...], entries)
        return first, lax.rsqrt(second - first * first + norm_eps)

    def expand(p, b, affine, own, keep):
        for row in range(pixels // width):
            a = half_silu(affine(own(row)))
            keep[b, pl.ds(row * width, width)] = a.astype(low_type)
            fill_row(abuf, (row + 1) * width, a, channels, width)
        a = half_silu(affine(got[p, b, 0, 16:48].astype(float_type)))
        fill_row(abuf, pl.multiple_of((pixels + width) * (1 - c), width), a, channels, width)
        a = half_silu(affine(got[p, b, 2, 16:48].astype(float_type)))
        a = jnp.where(outer_live, a, 0.0)
        fill_row(abuf, pl.multiple_of((pixels + width) * c, width), a, channels, width)

    def convolve(w):
        depth = 3 * channels
        return sum(
            jnp.dot(
                abuf[width * dy : width * dy + pixels, :],
                w[depth * dy : depth * (dy + 1), :],
                preferred_element_type=float_type,
            )
            for dy in range(3)
        )

    def vec(n):
        return vec_ref[n : n + 1, :]

    pl.semaphore_wait(barrier, 3)

    def step0(b, _):
        v = x_ref[b].astype(float_type)
        send(
            0, b, jnp.sum(v, axis=0, keepdims=True), jnp.sum(v * v, axis=0, keepdims=True),
            lambda at: x_ref[b, pl.ds(at, width)],
        )
        return 0

    lax.fori_loop(0, images, step0, 0)
    load1.wait()

    def step1(b, _):
        centre, scaled = receive(0, b)
        st_ref[b, 0:1] = centre
        st_ref[b, 1:2] = scaled
        slope = scaled * vec(0)
        shift = vec(1)
        expand(
            0, b, lambda v: (v - centre) * slope + shift,
            lambda row: x_ref[b, pl.ds(row * width, width)].astype(float_type), act1_ref,
        )
        hidden = convolve(w1) + vec(2)
        hid_ref[b] = hidden
        send(
            1, b, jnp.sum(hidden, axis=0, keepdims=True),
            jnp.sum(hidden * hidden, axis=0, keepdims=True),
            lambda at: hid_ref[b, pl.ds(at, width)].astype(low_type),
        )
        return 0

    lax.fori_loop(0, images, step1, 0)
    load2.wait()

    def step2(b, _):
        centre, scaled = receive(1, b)
        st_ref[b, 2:3] = centre
        st_ref[b, 3:4] = scaled
        grow = 1.0 + mod_ref[b, 0:1]
        slope = scaled * vec(3) * grow
        shift = vec(4) * grow + mod_ref[b, 1:2]
        expand(
            1, b, lambda v: (v - centre) * slope + shift,
            lambda row: hid_ref[b, pl.ds(row * width, width)], act2_ref,
        )
        middle = (convolve(w2) + vec(5) + x_ref[b].astype(float_type)) * math.sqrt(0.5)
        mid_ref[b] = middle
        send(
            2, b, jnp.sum(middle, axis=0, keepdims=True),
            jnp.sum(middle * middle, axis=0, keepdims=True), None,
        )
        return 0

    lax.fori_loop(0, images, step2, 0)

    def step3(b, _):
        centre, scaled = receive(2, b)
        st_ref[b, 4:5] = centre
        st_ref[b, 5:6] = scaled
        slope = scaled * vec(6)
        att_ref[b] = ((mid_ref[b] - centre) * slope + vec(7)).astype(low_type)
        for p in range(3):
            for cp in copies(p, b):
                cp.wait_send()
        return 0

    lax.fori_loop(0, images, step3, 0)


def forward_call(x, vectors, modulate, first_kernel, second_kernel):
    images, pixels, channels = x.shape
    depth = 9 * channels
    vm = pl.BlockSpec(memory_space=pltpu.VMEM)
    hbm = pl.BlockSpec(memory_space=pl.ANY)
    wide = jax.ShapeDtypeStruct(x.shape, float_type)
    low = jax.ShapeDtypeStruct(x.shape, low_type)
    return pl.pallas_call(
        forward_kernel,
        out_shape=(wide, wide, low, low, low, jax.ShapeDtypeStruct((images, 8, channels), float_type)),
        in_specs=[vm, vm, vm, hbm, hbm],
        out_specs=(vm,) * 6,
        scratch_shapes=[
            pltpu.VMEM((depth, channels), low_type),
            pltpu.VMEM((depth, channels), low_type),
            pltpu.VMEM((channels, channels), low_type),
            pltpu.VMEM((pixels + 64, 3 * channels), low_type),
            pltpu.VMEM((3, images, 48, channels), low_type),
            pltpu.VMEM((3, images, 48, channels), low_type),
            pltpu.VMEM((3, images, 3, 48, channels), low_type),
            pltpu.SemaphoreType.DMA((2,)),
            pltpu.SemaphoreType.DMA((3, images, 3)),
            pltpu.SemaphoreType.DMA((3, images, 3)),
        ],
        compiler_params=pltpu.CompilerParams(
            collective_id=0, has_side_effects=True, vmem_limit_bytes=56 << 20
        ),
        name="forward",
    )(x, vectors, modulate, first_kernel, second_kernel)


def attention_kernel(
    att_ref, mid_ref, cot_ref, vec_ref, jw_any, ow_any,
    res_ref, ag_ref, gj_ref, go_ref, gs_ref,
    jw, ow, att, att_t, kv, kv_t, q8, d_out_t, qm, dom, s_ref, eb, dsb, mix_t, dq_t, dq, dkv,
    part, got_core, to_x, got_x, wsem, gsem, hsem, asem, bsem,
):
    images, pixels, channels = att_ref.shape
    whole = 4 * pixels
    chunk = 128
    pair_lanes = 2 * HEAD
    pairs = channels // pair_lanes
    i, r, c, who = peers()
    loads = [
        pltpu.make_async_copy(jw_any, jw, wsem.at[0]),
        pltpu.make_async_copy(ow_any, ow, wsem.at[1]),
    ]
    for cp in loads:
        cp.start()
    barrier = pltpu.get_barrier_semaphore()
    for k in (1, 2):
        pl.semaphore_signal(barrier, inc=1, device_id=who[k], device_id_type=MESH)

    def block(n):
        return pl.ds(pl.multiple_of(n * pixels, pixels), pixels)

    def shares(b):
        own, far = block(r), block(lax.rem(r + 2, 4))
        return [
            pltpu.make_async_remote_copy(
                att.at[b, rows], att.at[b, rows], gsem.at[b, n], hsem.at[b, n],
                device_id=who[k], device_id_type=MESH,
            )
            for n, (rows, k) in enumerate(((own, 1), (own, 2), (far, 1)))
        ]

    def arrivals(b):
        mate = r + 1 - 2 * c
        rows = (block(mate), block(lax.rem(r + 2, 4)), block(lax.rem(mate + 2, 4)))
        return [
            pltpu.make_async_remote_copy(
                att.at[b, w], att.at[b, w], gsem.at[b, n], hsem.at[b, n],
                device_id=who[(1, 2, 1)[n]], device_id_type=MESH,
            )
            for n, w in enumerate(rows)
        ]

    def forward(b):
        arrivals(b)[1].wait_recv()
        shares(b)[2].start()

    def sums_core(b):
        return [
            pltpu.make_async_remote_copy(
                part.at[b, block(2 * n + 1 - c)], got_core.at[b, n], asem.at[b, n], bsem.at[b, n],
                device_id=who[1], device_id_type=MESH,
            )
            for n in range(2)
        ]

    def sum_x(b):
        return pltpu.make_async_remote_copy(
            to_x.at[b], got_x.at[b], asem.at[b, 2], bsem.at[b, 2],
            device_id=who[2], device_id_type=MESH,
        )

    def pass_on(b):
        x = lax.div(r, 2)
        for cp in sums_core(b):
            cp.wait_recv()
        far = 1 - x
        to_x[b] = (
            part[b, block(2 * far + c)].astype(float_type) + got_core[b, far].astype(float_type)
        ).astype(low_type)
        sum_x(b).start()
        ag_ref[b] = part[b, block(r)].astype(float_type) + got_core[b, x].astype(float_type)

    def keep_own(b, _):
        att[b, block(r)] = att_ref[b]
        return 0

    lax.fori_loop(0, images, keep_own, 0)
    pl.semaphore_wait(barrier, 2)
    for b in range(images):
        shares(b)[0].start()
        shares(b)[1].start()
    for cp in loads:
        cp.wait()
    forward(0)
    lane = lax.broadcasted_iota(jnp.int32, (pixels, pair_lanes), 1)

    def masked(v):
        return jnp.concatenate(
            [jnp.where(lane < HEAD, v, 0.0), jnp.where(lane >= HEAD, v, 0.0)], axis=0
        ).astype(low_type)

    def dot(a, b):
        return jnp.dot(a, b, preferred_element_type=float_type)

    def dot_nt(a, b):
        return lax.dot_general(a, b, contract_cols, preferred_element_type=float_type)

    def one_image(b, _):
        a = arrivals(b)
        a[0].wait_recv()
        a[2].wait_recv()
        bias = jnp.concatenate([jnp.zeros((1, channels), float_type), vec_ref[1:2]], axis=1)
        for n in range(4):
            rows = pl.ds(n * pixels, pixels)
            kv[rows] = (dot(att[b, rows], jw[:, channels:]) + bias).astype(low_type)
        for n in range(2 * channels // 128):
            cols = pl.ds(n * 128, 128)
            kv_t[cols, :] = kv[:, cols].T
        q = (dot(att_ref[b], jw[:, :channels]) + vec_ref[0:1]).astype(low_type)
        q8[...] = (q.astype(float_type) * HEAD ** (-0.5)).astype(low_type)
        d_out = dot_nt(cot_ref[b], ow[...]).astype(low_type).astype(float_type)
        d_out_t[...] = d_out.T

        @pl.when(b > 0)
        def _():
            pass_on(b - 1)

        def one_pair(t, _):
            lanes = pl.ds(pl.multiple_of(t * pair_lanes, pair_lanes), pair_lanes)
            v_lanes = pl.ds(pl.multiple_of(channels + t * pair_lanes, pair_lanes), pair_lanes)
            qm[...] = masked(q8[:, lanes].astype(float_type))
            peak = None
            for n in range(whole // chunk):
                rows = pl.ds(n * chunk, chunk)
                s = dot_nt(kv[rows, lanes], qm[...])
                s_ref[rows] = s
                top = jnp.max(s.reshape(chunk // 8, 8, 2 * pixels), axis=0)
                peak = top if peak is None else jnp.maximum(peak, top)
            peak = jnp.max(peak, axis=0, keepdims=True)
            total = None
            for n in range(whole // chunk):
                rows = pl.ds(n * chunk, chunk)
                e = jnp.exp(s_ref[rows] - peak)
                eb[rows] = e.astype(low_type)
                more = jnp.sum(e.reshape(chunk // 8, 8, 2 * pixels), axis=0)
                total = more if total is None else total + more
            over = 1.0 / jnp.sum(total, axis=0, keepdims=True)
            inner, scaled = [], []
            for j in range(2):
                head = pl.ds(pl.multiple_of(t * pair_lanes + j * HEAD, HEAD), HEAD)
                v_head = pl.ds(pl.multiple_of(channels + t * pair_lanes + j * HEAD, HEAD), HEAD)
                cols = slice(j * pixels, (j + 1) * pixels)
                mt = dot(kv_t[v_head, :], eb[:, cols]) * over[:, cols]
                mix_t[b, head] = mt.astype(low_type)
                g = (d_out_t[head] * over[:, cols]).astype(low_type).astype(float_type)
                inner.append(jnp.sum(g * mt, axis=0, keepdims=True))
                scaled.append(g)
            inner = jnp.concatenate(inner, axis=1)
            dom[...] = masked(jnp.concatenate(scaled, axis=0).T)
            for n in range(whole // chunk):
                rows = pl.ds(n * chunk, chunk)
                dp = dot_nt(kv[rows, v_lanes], dom[...])
                dsb[rows] = (eb[rows].astype(float_type) * (dp - inner)).astype(low_type)
            for j in range(2):
                head = pl.ds(pl.multiple_of(t * pair_lanes + j * HEAD, HEAD), HEAD)
                cols = slice(j * pixels, (j + 1) * pixels)
                dq_t[head] = dot(kv_t[head, :], dsb[:, cols]) * HEAD ** (-0.5)
            dkv[b, :, lanes] = dot(dsb[...], qm[...]).astype(low_type)
            dkv[b, :, v_lanes] = dot(eb[...], dom[...]).astype(low_type)
            return 0

        lax.fori_loop(0, pairs, one_pair, 0)
        dq[b] = dq_t[...].T.astype(low_type)
        for n in range(4):
            rows = pl.ds(n * pixels, pixels)
            part[b, rows] = dot_nt(dkv[b, rows], jw[:, channels:]).astype(low_type)
        part[b, block(r)] = (
            part[b, block(r)].astype(float_type) + dot_nt(dq[b], jw[:, :channels])
        ).astype(low_type)
        for cp in sums_core(b):
            cp.start()

        @pl.when(b + 1 < images)
        def _():
            forward(b + 1)

        mixed = mix_t[b].T
        res_ref[b] = (mid_ref[b] + dot(mixed, ow[...]) + vec_ref[2:3]).astype(low_type)
        return 0

    lax.fori_loop(0, images, one_image, 0)
    pass_on(images - 1)
    ones = jnp.ones((16, whole), low_type)
    for b in range(images):
        att_t[b, 0:channels] = att[b].T
        att_t[b, channels:] = ones
    kv_sum = None
    q_sum = None
    o_sum = None
    for b in range(images):
        more = dot(att_t[b], dkv[b])
        kv_sum = more if kv_sum is None else kv_sum + more
        more = dot(att_t[b, :, block(r)], dq[b])
        q_sum = more if q_sum is None else q_sum + more
        more = dot(mix_t[b], cot_ref[b])
        o_sum = more if o_sum is None else o_sum + more
    gj_ref[:, :channels] = q_sum[:channels]
    gj_ref[:, channels:] = kv_sum[:channels]
    go_ref[...] = o_sum
    cot_sum = jnp.sum(jnp.sum(cot_ref[...].astype(float_type), axis=0), axis=0, keepdims=True)
    gs_ref[0:1] = q_sum[channels : channels + 1]
    gs_ref[1:2] = kv_sum[channels : channels + 1, channels:]
    gs_ref[2:3] = cot_sum
    for b in range(images):
        sum_x(b).wait_recv()
        ag_ref[b] += got_x[b].astype(float_type)
    for b in range(images):
        for cp in shares(b) + sums_core(b) + [sum_x(b)]:
            cp.wait_send()


def attention_call(att, middle, cot, vectors, joint_weight, output_weight):
    images, pixels, channels = att.shape
    whole = 4 * pixels
    vm = pl.BlockSpec(memory_space=pltpu.VMEM)
    hbm = pl.BlockSpec(memory_space=pl.ANY)

    def low(*shape):
        return pltpu.VMEM(shape, low_type)

    def wide(*shape):
        return pltpu.VMEM(shape, float_type)

    return pl.pallas_call(
        attention_kernel,
        out_shape=(
            jax.ShapeDtypeStruct(att.shape, low_type),
            jax.ShapeDtypeStruct(att.shape, float_type),
            jax.ShapeDtypeStruct(joint_weight.shape, float_type),
            jax.ShapeDtypeStruct(output_weight.shape, float_type),
            jax.ShapeDtypeStruct((8, channels), float_type),
        ),
        in_specs=[vm, vm, vm, vm, hbm, hbm],
        out_specs=(vm,) * 5,
        scratch_shapes=[
            low(channels, 3 * channels), low(channels, channels), low(images, whole, channels),
            low(images, channels + 16, whole), low(whole, 2 * channels), low(2 * channels, whole),
            low(pixels, channels), wide(channels, pixels), low(2 * pixels, 2 * HEAD),
            low(2 * pixels, 2 * HEAD), wide(whole, 2 * pixels), low(whole, 2 * pixels),
            low(whole, 2 * pixels), low(images, channels, pixels), wide(channels, pixels),
            low(images, pixels, channels), low(images, whole, 2 * channels),
            low(images, whole, channels), low(images, 2, pixels, channels),
            low(images, pixels, channels), low(images, pixels, channels),
            pltpu.SemaphoreType.DMA((2,)), pltpu.SemaphoreType.DMA((images, 3)),
            pltpu.SemaphoreType.DMA((images, 3)), pltpu.SemaphoreType.DMA((images, 3)),
            pltpu.SemaphoreType.DMA((images, 3)),
        ],
        compiler_params=pltpu.CompilerParams(
            collective_id=1, has_side_effects=True, vmem_limit_bytes=56 << 20
        ),
        name="attention",
    )(att, middle, cot, vectors, joint_weight, output_weight)


def backward_kernel(
    ag_ref, mid_ref, cot_ref, hid_ref, x_ref, act1_ref, act2_ref, st_ref, vec_ref, mod_ref,
    w1_any, w2_any,
    gx_ref, gw1_ref, gw2_ref, mg_ref, gs_ref,
    w1, w2, ones, grad1, grad2, act_t, skip, slope_grad, m1, m3, got, wsem, ssem, rsem,
):
    images, pixels, channels = x_ref.shape
    width = 32
    edge = pixels - width
    span = pixels + 2 * width
    rows_in = pixels // width
    entries = 4.0 * pixels * (channels // GROUPS)
    i, r, c, who = peers()
    loads = [
        pltpu.make_async_copy(w2_any, w2, wsem.at[0]),
        pltpu.make_async_copy(w1_any, w1, wsem.at[1]),
    ]
    for cp in loads:
        cp.start()
    barrier = pltpu.get_barrier_semaphore()
    for k in (1, 2, 3):
        pl.semaphore_signal(barrier, inc=1, device_id=who[k], device_id_type=MESH)
    ones[...] = block_ones(channels, channels // GROUPS)
    gs_ref[...] = jnp.zeros(gs_ref.shape, float_type)
    mg_ref[...] = jnp.zeros(mg_ref.shape, float_type)
    inner = pl.multiple_of(edge * (1 - c), width)
    outer = pl.multiple_of(edge * c, width)
    outer_live = jnp.logical_and(r > 0, r < 3)
    stat = pl.ds(0, 16)
    halo = pl.ds(16, width)
    half = math.sqrt(0.5)

    def stat_copies(p, b):
        return [
            pltpu.make_async_remote_copy(
                m1.at[p, b, stat], got.at[p, b, k - 1, stat], ssem.at[p, b, k - 1],
                rsem.at[p, b, k - 1], device_id=who[k], device_id_type=MESH,
            )
            for k in (1, 2, 3)
        ]

    def halo_copies(p, b):
        return [
            pltpu.make_async_remote_copy(
                src.at[p, b, halo], got.at[p, b, k - 1, halo], ssem.at[p, b, k + 2],
                rsem.at[p, b, k + 2], device_id=who[k], device_id_type=MESH,
            )
            for k, src in ((1, m1), (3, m3))
        ]

    def send_stats(p, b, first, second):
        m1[p, b, 0:16] = pack_stats(first, second)
        for cp in stat_copies(p, b):
            cp.start()

    def receive_stats(p, b):
        for cp in stat_copies(p, b):
            cp.wait_recv()
        parts = [m1[p, b, 0:16]] + [got[p, b, k, 0:16] for k in range(3)]
        return combine_stats(parts, ones[...], entries)

    def send_halo(p, b, buf):
        middle = slice(channels, 2 * channels)
        m1[p, b, 16:48] = buf[b, pl.ds(inner + width, width), middle]
        m3[p, b, 16:48] = buf[b, pl.ds(outer + width, width), middle]
        for cp in halo_copies(p, b):
            cp.start()

    def receive_halo(p, b, buf):
        for cp in halo_copies(p, b):
            cp.wait_recv()
        v = got[p, b, 0, 16:48].astype(float_type)
        fill_row(buf.at[b], pl.multiple_of((pixels + width) * (1 - c), width), v, channels, width)
        v = jnp.where(outer_live, got[p, b, 2, 16:48].astype(float_type), 0.0)
        fill_row(buf.at[b], pl.multiple_of((pixels + width) * c, width), v, channels, width)

    def data_grad(buf, b, w):
        total = None
        for dy in range(3):
            for dx in range(3):
                tap = 3 * dy + dx
                more = lax.dot_general(
                    buf[b, (2 - dy) * width : (2 - dy) * width + pixels,
                        (2 - dx) * channels : (3 - dx) * channels],
                    w[tap * channels : (tap + 1) * channels, :],
                    contract_cols, preferred_element_type=float_type,
                )
                total = more if total is None else total + more
        return total

    def kernel_grad(act_ref, buf, out_ref):
        for b in range(images):
            act_t[:, b * span : b * span + pixels] = act_ref[b].T
        reach = images * span - 2 * width
        flat = buf.reshape(images * span, 3 * channels)
        for dy in range(3):
            g = jnp.dot(
                act_t[:, 0:reach], flat[(2 - dy) * width : (2 - dy) * width + reach, :],
                preferred_element_type=float_type,
            )
            for dx in range(3):
                tap = 3 * dy + dx
                out_ref[tap * channels : (tap + 1) * channels, :] = g[
                    :, (2 - dx) * channels : (3 - dx) * channels
                ].astype(low_type)

    def vec(n):
        return vec_ref[n : n + 1, :]

    def col_sum(v):
        return jnp.sum(v, axis=0, keepdims=True)

    def slope_of(pre):
        s = 0.5 * jnp.tanh(0.5 * pre) + 0.5
        return s * (1.0 + pre * (1.0 - s))

    for b in range(images):
        act_t[:, b * span + pixels : (b + 1) * span] = jnp.zeros((channels, 2 * width), low_type)
    pl.semaphore_wait(barrier, 3)

    def step0(b, _):
        u = ag_ref[b]
        first = col_sum(u)
        second = col_sum(u * ((mid_ref[b] - st_ref[b, 4:5]) * st_ref[b, 5:6]))
        gs_ref[6:7] += second
        gs_ref[7:8] += first
        send_stats(0, b, first * vec(6), second * vec(6))
        return 0

    lax.fori_loop(0, images, step0, 0)

    def step1(b, _):
        first, second = receive_stats(0, b)
        centre, scaled = st_ref[b, 4:5], st_ref[b, 5:6]
        total = jnp.zeros((1, channels), float_type)
        for row in range(rows_in):
            rows = pl.ds(row * width, width)
            normed = (mid_ref[b, rows] - centre) * scaled
            back = scaled * (ag_ref[b, rows] * vec(6) - first - normed * second)
            v = (cot_ref[b, rows].astype(float_type) + back) * half
            skip[b, rows] = v
            v = v.astype(low_type).astype(float_type)
            fill_row(grad2.at[b], (row + 1) * width, v, channels, width)
            total += col_sum(v)
        gs_ref[5:6] += total
        send_halo(1, b, grad2)
        return 0

    lax.fori_loop(0, images, step1, 0)
    loads[0].wait()

    def step2(b, _):
        receive_halo(1, b, grad2)
        upstream = data_grad(grad2, b, w2)
        grow = 1.0 + mod_ref[b, 0:1]
        normed = (hid_ref[b] - st_ref[b, 2:3]) * st_ref[b, 3:4]
        pre = (normed * vec(3) + vec(4)) * grow + mod_ref[b, 1:2]
        v = upstream * slope_of(pre)
        slope_grad[b] = v
        first, second = col_sum(v), col_sum(v * normed)
        mg_ref[b, 0:1] = vec(3) * second + vec(4) * first
        mg_ref[b, 1:2] = first
        first, second = grow * first, grow * second
        gs_ref[3:4] += second
        gs_ref[4:5] += first
        send_stats(2, b, first * vec(3), second * vec(3))
        return 0

    lax.fori_loop(0, images, step2, 0)
    kernel_grad(act2_ref, grad2, gw2_ref)

    def step3(b, _):
        first, second = receive_stats(2, b)
        centre, scaled = st_ref[b, 2:3], st_ref[b, 3:4]
        gain = (1.0 + mod_ref[b, 0:1]) * vec(3)
        total = jnp.zeros((1, channels), float_type)
        for row in range(rows_in):
            rows = pl.ds(row * width, width)
            normed = (hid_ref[b, rows] - centre) * scaled
            v = scaled * (slope_grad[b, rows] * gain - first - normed * second)
            v = v.astype(low_type).astype(float_type)
            fill_row(grad1.at[b], (row + 1) * width, v, channels, width)
            total += col_sum(v)
        gs_ref[2:3] += total
        send_halo(3, b, grad1)
        return 0

    lax.fori_loop(0, images, step3, 0)
    loads[1].wait()

    def step4(b, _):
        receive_halo(3, b, grad1)
        return 0

    lax.fori_loop(0, images, step4, 0)
    kernel_grad(act1_ref, grad1, gw1_ref)

    def step5(b, _):
        upstream = data_grad(grad1, b, w1)
        normed = (x_ref[b].astype(float_type) - st_ref[b, 0:1]) * st_ref[b, 1:2]
        v = upstream * slope_of(normed * vec(0) + vec(1))
        slope_grad[b] = v
        first, second = col_sum(v), col_sum(v * normed)
        gs_ref[0:1] += second
        gs_ref[1:2] += first
        send_stats(4, b, first * vec(0), second * vec(0))
        return 0

    lax.fori_loop(0, images, step5, 0)

    def step6(b, _):
        first, second = receive_stats(4, b)
        scaled = st_ref[b, 1:2]
        normed = (x_ref[b].astype(float_type) - st_ref[b, 0:1]) * scaled
        gx_ref[b] = skip[b] + scaled * (slope_grad[b] * vec(0) - first - normed * second)
        for p in (0, 2, 4):
            for cp in stat_copies(p, b):
                cp.wait_send()
        for p in (1, 3):
            for cp in halo_copies(p, b):
                cp.wait_send()
        return 0

    lax.fori_loop(0, images, step6, 0)


def backward_call(ag, mid, cot, hid, x, act1, act2, stats, vectors, modulate, w1, w2):
    images, pixels, channels = x.shape
    span = pixels + 64
    vm = pl.BlockSpec(memory_space=pltpu.VMEM)
    hbm = pl.BlockSpec(memory_space=pl.ANY)

    def low(*shape):
        return pltpu.VMEM(shape, low_type)

    def wide(*shape):
        return pltpu.VMEM(shape, float_type)

    return pl.pallas_call(
        backward_kernel,
        out_shape=(
            jax.ShapeDtypeStruct(x.shape, float_type),
            jax.ShapeDtypeStruct(w1.shape, low_type),
            jax.ShapeDtypeStruct(w2.shape, low_type),
            jax.ShapeDtypeStruct((images, 8, channels), float_type),
            jax.ShapeDtypeStruct((16, channels), float_type),
        ),
        in_specs=[vm] * 10 + [hbm] * 2,
        out_specs=(vm,) * 5,
        scratch_shapes=[
            low(*w1.shape), low(*w2.shape), low(channels, channels),
            low(images, span, 3 * channels), low(images, span, 3 * channels),
            low(channels, images * span), wide(images, pixels, channels),
            wide(images, pixels, channels), low(5, images, 48, channels),
            low(5, images, 48, channels), low(5, images, 3, 48, channels),
            pltpu.SemaphoreType.DMA((2,)), pltpu.SemaphoreType.DMA((5, images, 6)),
            pltpu.SemaphoreType.DMA((5, images, 6)),
        ],
        compiler_params=pltpu.CompilerParams(
            collective_id=2, has_side_effects=True, vmem_limit_bytes=56 << 20
        ),
        name="backward",
    )(ag, mid, cot, hid, x, act1, act2, stats, vectors, modulate, w1, w2)


def shards(
    images,
    level_count,
    level_index,
    labels,
    first_gain,
    first_shift,
    first_kernel,
    first_offset,
    embed_weight,
    embed_offset,
    class_table,
    second_gain,
    second_shift,
    second_kernel,
    second_offset,
    third_gain,
    third_shift,
    joint_weight,
    joint_offset,
    output_weight,
    output_offset,
    cotangent,
):
    image_count, stripe_rows, image_width, channels = images.shape
    layout = (image_count, stripe_rows, image_width, channels)
    pixels = stripe_rows * image_width
    gain_one = first_gain.astype(float_type)
    shift_one = first_shift.astype(float_type)
    gain_two = second_gain.astype(float_type)
    shift_two = second_shift.astype(float_type)
    gain_three = third_gain.astype(float_type)
    features = noise_features(level_count, level_index)
    class_count = class_table.shape[0]
    one_hot = (labels[:, None] == jnp.arange(class_count, dtype=jnp.int32)[None, :]).astype(
        low_type
    )
    embedded = features + jnp.dot(one_hot, class_table, preferred_element_type=float_type)
    embed_act = jax.nn.silu(embedded).astype(low_type)
    modulate = jnp.dot(
        embed_act, embed_weight, preferred_element_type=float_type
    ) + embed_offset.astype(float_type)
    scale_part = modulate[:, :channels]
    vectors = jnp.stack(
        [
            first_gain, first_shift, first_offset, second_gain, second_shift, second_offset,
            third_gain, third_shift,
        ]
    ).astype(float_type)
    x = images.reshape(image_count, pixels, channels)
    hidden, middle, attend, act_one, act_two, stats = forward_call(
        x, vectors, modulate.reshape(image_count, 2, channels), first_kernel, second_kernel
    )
    attention_vectors = jnp.stack(
        [joint_offset[:channels], joint_offset[channels:], output_offset]
    ).astype(float_type)
    cot = cotangent.reshape(image_count, pixels, channels)
    result, attend_grad, joint_weight_grad, output_weight_grad, sums = attention_call(
        attend, middle, cot, attention_vectors, joint_weight, output_weight
    )
    result = result.reshape(layout)
    joint_offset_grad = jnp.concatenate([sums[0], sums[1]])
    output_offset_grad = sums[2]
    images_gradient, first_kernel_grad, second_kernel_grad, modulate_grad, sums = backward_call(
        attend_grad, middle, cot, hidden, x, act_one, act_two, stats, vectors,
        modulate.reshape(image_count, 2, channels), first_kernel, second_kernel,
    )
    images_gradient = images_gradient.reshape(layout)
    (
        first_gain_grad, first_shift_grad, first_offset_grad, second_gain_grad, second_shift_grad,
        second_offset_grad, third_gain_grad, third_shift_grad,
    ) = (sums[n] for n in range(8))
    modulate_grad = modulate_grad[:, :2].reshape(image_count, 2 * channels)
    modulate_grad = lax.psum(modulate_grad, "row")
    every_grad, every_embedded, every_label = lax.all_gather(
        (modulate_grad, embedded, labels), "img", axis=0, tiled=True
    )
    stripe_index = lax.axis_index("row")
    stripe_count = lax.axis_size("row")

    def own_rows(v, axis):
        size = v.shape[axis] // stripe_count
        return lax.dynamic_slice_in_dim(v, stripe_index * size, size, axis)

    every_act = jax.nn.silu(every_embedded).astype(low_type).astype(float_type)
    embed_weight_grad = lax.dot_general(
        own_rows(every_act, 1), every_grad, contract_rows, precision=highest
    )
    embed_offset_grad = own_rows(jnp.sum(every_grad, axis=0), 0)
    active_grad = lax.dot_general(
        every_grad, embed_weight.astype(float_type), contract_cols, precision=highest
    )
    embedded_grad = active_grad * silu_slope(every_embedded)
    own_classes = stripe_index * (class_count // stripe_count) + jnp.arange(
        class_count // stripe_count, dtype=jnp.int32
    )
    own_hot = (every_label[:, None] == own_classes[None, :]).astype(float_type)
    class_table_grad = lax.dot_general(own_hot, embedded_grad, contract_rows, precision=highest)

    def scattered(v):
        v = lax.psum_scatter(v.astype(low_type), "row", scatter_dimension=0, tiled=True)
        return lax.psum(v.astype(low_type), "img").astype(float_type)

    first_kernel_grad, second_kernel_grad, joint_weight_grad, output_weight_grad = (
        scattered(v)
        for v in (first_kernel_grad, second_kernel_grad, joint_weight_grad, output_weight_grad)
    )
    small = (
        first_gain_grad, first_shift_grad, first_offset_grad, second_gain_grad, second_shift_grad,
        second_offset_grad, third_gain_grad, third_shift_grad, joint_offset_grad,
        output_offset_grad,
    )
    summed = lax.psum(jnp.concatenate(small), ("img", "row"))
    pieces, at = [], 0
    for v in small:
        pieces.append(own_rows(summed[at : at + v.shape[0]], 0))
        at += v.shape[0]
    (
        first_gain_grad, first_shift_grad, first_offset_grad, second_gain_grad, second_shift_grad,
        second_offset_grad, third_gain_grad, third_shift_grad, joint_offset_grad,
        output_offset_grad,
    ) = pieces
    return (
        result, images_gradient, first_gain_grad, first_shift_grad, first_kernel_grad,
        first_offset_grad, embed_weight_grad, embed_offset_grad, class_table_grad,
        second_gain_grad, second_shift_grad, second_kernel_grad, second_offset_grad,
        third_gain_grad, third_shift_grad, joint_weight_grad, joint_offset_grad,
        output_weight_grad, output_offset_grad,
    )


def solution(mesh):
    in_specs = (
        (P("img", "row", None, None),) + (P("img"),) * 3 + (P(),) * 17
        + (P("img", "row", None, None),)
    )
    row, rows = P("row"), P("row", None)
    out_specs = (
        P("img", "row", None, None), P("img", "row", None, None), row, row, rows, row, rows, row,
        rows, row, row, rows, row, row, row, rows, row, rows, row,
    )
    return jax.shard_map(shards, mesh=mesh, in_specs=in_specs, out_specs=out_specs, check_vma=False)
```

```python
import math

import jax
import jax.numpy as jnp
from jax import lax
from jax.experimental import pallas as pl
from jax.experimental.pallas import tpu as pltpu
from jax.sharding import PartitionSpec as P

GROUPS = 32
HEAD = 64
EMB = 768
MESH = pl.DeviceIdType.MESH

norm_eps = 1e-05
sigma_least = 0.002
sigma_most = 80.0
sigma_power = 7.0
highest = lax.Precision.HIGHEST
float_type = jnp.float32
low_type = jnp.bfloat16
contract_rows = (((0,), (0,)), ((), ()))
contract_cols = (((1,), (1,)), ((), ()))


def noise_features(level_count, level_index):
    position = (level_index.astype(jnp.float32) + 1.0) / (level_count.astype(jnp.float32) - 1.0)
    low_root = sigma_least ** (1.0 / sigma_power)
    high_root = sigma_most ** (1.0 / sigma_power)
    noise_level = (low_root + position * (high_root - low_root)) ** sigma_power
    noise_time = 250.0 * jnp.log(noise_level)
    half_width = EMB // 2
    frequency = jnp.exp(-math.log(10000.0) * jnp.arange(half_width, dtype=jnp.float32) / half_width)
    angles = noise_time[:, None] * frequency[None, :]
    return jnp.concatenate([jnp.cos(angles), jnp.sin(angles)], axis=-1)


def silu_slope(values):
    sigmoid_part = jax.nn.sigmoid(values)
    return sigmoid_part * (1.0 + values * (1.0 - sigmoid_part))


def normalize(values, centre, scaled):
    return (values - centre) * scaled


def group_fold(v):
    return v.reshape(v.shape[:-1] + (GROUPS, v.shape[-1] // GROUPS))


def group_back(upstream, normed, scaled):
    image_count, pixels, channels = upstream.shape
    first_sum = jnp.sum(group_fold(jnp.sum(upstream, axis=1)), axis=-1)
    second_sum = jnp.sum(group_fold(jnp.sum(upstream * normed, axis=1)), axis=-1)
    first_sum, second_sum = lax.psum((first_sum, second_sum), "row")
    entries = pixels * lax.axis_size("row") * (channels // GROUPS)
    per = channels // GROUPS
    first_sum = jnp.repeat(first_sum / entries, per, axis=-1)
    second_sum = jnp.repeat(second_sum / entries, per, axis=-1)
    return scaled * (upstream - first_sum[:, None, :] - normed * second_sum[:, None, :])


def padded_grads(activity):
    size, length = lax.axis_size("row"), activity.shape[1]
    up = [(i, i + 1) for i in range(size - 1)]
    down = [(j, i) for i, j in up]
    last = lax.slice_in_dim(activity, length - 1, length, axis=1)
    initial = lax.slice_in_dim(activity, 0, 1, axis=1)
    before = lax.ppermute(last, "row", up)
    after = lax.ppermute(initial, "row", down)
    framed = jnp.concatenate([before, activity, after], axis=1)
    return jnp.pad(framed, ((0, 0), (0, 0), (1, 1), (0, 0)))


def backward_patches(framed, stripe_rows, image_width):
    pieces = [
        framed[
            :, 2 - row_tap : 2 - row_tap + stripe_rows, 2 - col_tap : 2 - col_tap + image_width, :
        ]
        for row_tap in range(3)
        for col_tap in range(3)
    ]
    joined = jnp.concatenate(pieces, axis=-1)
    return joined.reshape(-1, joined.shape[-1])


def transpose_product(columns, kernel):
    channels = kernel.shape[1]
    stacked = columns.reshape(columns.shape[0], 9, channels)
    kernel_taps = kernel.reshape(9, kernel.shape[0] // 9, channels)
    return lax.dot_general(
        stacked, kernel_taps, (((1, 2), (0, 2)), ((), ())), preferred_element_type=float_type
    )


def peers():
    i = lax.axis_index("img")
    r = lax.axis_index("row")
    c = lax.rem(r, 2)
    near = r + 1 - 2 * c
    return (i, r, c, {1: (i, near), 2: (i, lax.rem(r + 2, 4)), 3: (i, 3 - r)})


def half_silu(v):
    h = 0.5 * v
    return h * jnp.tanh(h) + h


def col_iota(n, width, channels):
    return lax.rem(lax.broadcasted_iota(jnp.int32, (n, channels), 0), width)


def fill_row(buf, start, act, channels, width):
    col = lax.broadcasted_iota(jnp.int32, (width, channels), 0)
    left = jnp.where(col == 0, 0.0, pltpu.roll(act, 1, 0))
    right = jnp.where(col == width - 1, 0.0, pltpu.roll(act, width - 1, 0))
    rows = pl.ds(start, width)
    buf[rows, 0:channels] = left.astype(low_type)
    buf[rows, channels : 2 * channels] = act.astype(low_type)
    buf[rows, 2 * channels : 3 * channels] = right.astype(low_type)


def pack_stats(first, second):
    channels = first.shape[1]
    row = lax.broadcasted_iota(jnp.int32, (8, channels), 0)

    def terms(v):
        a = v.astype(low_type).astype(float_type)
        b = (v - a).astype(low_type).astype(float_type)
        c = v - a - b
        return jnp.where(row == 0, a, jnp.where(row == 1, b, jnp.where(row == 2, c, 0.0)))

    return jnp.concatenate([terms(first), terms(second)], axis=0).astype(low_type)


def block_ones(channels, per):
    a = lax.broadcasted_iota(jnp.int32, (channels, channels), 0)
    b = lax.broadcasted_iota(jnp.int32, (channels, channels), 1)
    a = lax.shift_right_logical(a * 43691, 19)
    b = lax.shift_right_logical(b * 43691, 19)
    return jnp.where(a == b, 1.0, 0.0).astype(low_type)


def combine_stats(parts, ones, entries):
    total = jnp.dot(jnp.concatenate(parts, axis=0), ones, preferred_element_type=float_type)
    first = total[0:8] + total[16:24] + total[32:40] + total[48:56]
    second = total[8:16] + total[24:32] + total[40:48] + total[56:64]
    first = jnp.sum(first, axis=0, keepdims=True) * (1.0 / entries)
    second = jnp.sum(second, axis=0, keepdims=True) * (1.0 / entries)
    return first, second


def forward_kernel(
    x_ref, vec_ref, mod_ref, w1_any, w2_any,
    hid_ref, mid_ref, att_ref, act1_ref, act2_ref, st_ref,
    w1, w2, ones, abuf, m1, m3, got, wsem, ssem, rsem,
):
    images, pixels, channels = x_ref.shape
    width = 32
    edge = pixels - width
    entries = 4.0 * pixels * (channels // GROUPS)
    i, r, c, who = peers()
    load1 = pltpu.make_async_copy(w1_any, w1, wsem.at[0])
    load2 = pltpu.make_async_copy(w2_any, w2, wsem.at[1])
    load1.start()
    load2.start()
    barrier = pltpu.get_barrier_semaphore()
    for k in (1, 2, 3):
        pl.semaphore_signal(barrier, inc=1, device_id=who[k], device_id_type=MESH)
    ones[...] = block_ones(channels, channels // GROUPS)
    inner = pl.multiple_of(edge * (1 - c), width)
    outer = pl.multiple_of(edge * c, width)
    inner_live = None
    outer_live = jnp.logical_and(r > 0, r < 3)
    stat = pl.ds(0, 16)
    halo = pl.ds(16, width)

    def copies(p, b):
        full = p < 2
        rows = pl.ds(0, 48) if full else stat
        return [
            pltpu.make_async_remote_copy(
                src.at[p, b, rs], got.at[p, b, k - 1, rs], ssem.at[p, b, k - 1],
                rsem.at[p, b, k - 1], device_id=who[k], device_id_type=MESH,
            )
            for k, src, rs in ((1, m1, rows), (2, m1, stat), (3, m3, rows))
        ]

    def send(p, b, first, second, edges):
        packed = pack_stats(first, second)
        m1[p, b, 0:16] = packed
        m3[p, b, 0:16] = packed
        if edges is not None:
            m1[p, b, 16:48] = edges(inner)
            m3[p, b, 16:48] = edges(outer)
        for cp in copies(p, b):
            cp.start()

    def receive(p, b):
        for cp in copies(p, b):
            cp.wait_recv()
        parts = [m1[p, b, 0:16]] + [got[p, b, k, 0:16] for k in range(3)]
        first, second = combine_stats(parts, ones[...], entries)
        return first, lax.rsqrt(second - first * first + norm_eps)

    def expand(p, b, affine, own, keep):
        for row in range(pixels // width):
            a = half_silu(affine(own(row)))
            keep[b, pl.ds(row * width, width)] = a.astype(low_type)
            fill_row(abuf, (row + 1) * width, a, channels, width)
        a = half_silu(affine(got[p, b, 0, 16:48].astype(float_type)))
        fill_row(abuf, pl.multiple_of((pixels + width) * (1 - c), width), a, channels, width)
        a = half_silu(affine(got[p, b, 2, 16:48].astype(float_type)))
        a = jnp.where(outer_live, a, 0.0)
        fill_row(abuf, pl.multiple_of((pixels + width) * c, width), a, channels, width)

    def convolve(w):
        depth = 3 * channels
        return sum(
            jnp.dot(
                abuf[width * dy : width * dy + pixels, :],
                w[depth * dy : depth * (dy + 1), :],
                preferred_element_type=float_type,
            )
            for dy in range(3)
        )

    def vec(n):
        return vec_ref[n : n + 1, :]

    pl.semaphore_wait(barrier, 3)

    def step0(b, _):
        v = x_ref[b].astype(float_type)
        send(
            0, b, jnp.sum(v, axis=0, keepdims=True), jnp.sum(v * v, axis=0, keepdims=True),
            lambda at: x_ref[b, pl.ds(at, width)],
        )
        return 0

    lax.fori_loop(0, images, step0, 0)
    load1.wait()

    def step1(b, _):
        centre, scaled = receive(0, b)
        st_ref[b, 0:1] = centre
        st_ref[b, 1:2] = scaled
        slope = scaled * vec(0)
        shift = vec(1)
        expand(
            0, b, lambda v: (v - centre) * slope + shift,
            lambda row: x_ref[b, pl.ds(row * width, width)].astype(float_type), act1_ref,
        )
        hidden = convolve(w1) + vec(2)
        hid_ref[b] = hidden
        send(
            1, b, jnp.sum(hidden, axis=0, keepdims=True),
            jnp.sum(hidden * hidden, axis=0, keepdims=True),
            lambda at: hid_ref[b, pl.ds(at, width)].astype(low_type),
        )
        return 0

    lax.fori_loop(0, images, step1, 0)
    load2.wait()

    def step2(b, _):
        centre, scaled = receive(1, b)
        st_ref[b, 2:3] = centre
        st_ref[b, 3:4] = scaled
        grow = 1.0 + mod_ref[b, 0:1]
        slope = scaled * vec(3) * grow
        shift = vec(4) * grow + mod_ref[b, 1:2]
        expand(
            1, b, lambda v: (v - centre) * slope + shift,
            lambda row: hid_ref[b, pl.ds(row * width, width)], act2_ref,
        )
        middle = (convolve(w2) + vec(5) + x_ref[b].astype(float_type)) * math.sqrt(0.5)
        mid_ref[b] = middle
        send(
            2, b, jnp.sum(middle, axis=0, keepdims=True),
            jnp.sum(middle * middle, axis=0, keepdims=True), None,
        )
        return 0

    lax.fori_loop(0, images, step2, 0)

    def step3(b, _):
        centre, scaled = receive(2, b)
        st_ref[b, 4:5] = centre
        st_ref[b, 5:6] = scaled
        slope = scaled * vec(6)
        att_ref[b] = ((mid_ref[b] - centre) * slope + vec(7)).astype(low_type)
        for p in range(3):
            for cp in copies(p, b):
                cp.wait_send()
        return 0

    lax.fori_loop(0, images, step3, 0)


def forward_call(x, vectors, modulate, first_kernel, second_kernel):
    images, pixels, channels = x.shape
    depth = 9 * channels
    vm = pl.BlockSpec(memory_space=pltpu.VMEM)
    hbm = pl.BlockSpec(memory_space=pl.ANY)
    wide = jax.ShapeDtypeStruct(x.shape, float_type)
    low = jax.ShapeDtypeStruct(x.shape, low_type)
    return pl.pallas_call(
        forward_kernel,
        out_shape=(wide, wide, low, low, low, jax.ShapeDtypeStruct((images, 8, channels), float_type)),
        in_specs=[vm, vm, vm, hbm, hbm],
        out_specs=(vm,) * 6,
        scratch_shapes=[
            pltpu.VMEM((depth, channels), low_type),
            pltpu.VMEM((depth, channels), low_type),
            pltpu.VMEM((channels, channels), low_type),
            pltpu.VMEM((pixels + 64, 3 * channels), low_type),
            pltpu.VMEM((3, images, 48, channels), low_type),
            pltpu.VMEM((3, images, 48, channels), low_type),
            pltpu.VMEM((3, images, 3, 48, channels), low_type),
            pltpu.SemaphoreType.DMA((2,)),
            pltpu.SemaphoreType.DMA((3, images, 3)),
            pltpu.SemaphoreType.DMA((3, images, 3)),
        ],
        compiler_params=pltpu.CompilerParams(
            collective_id=0, has_side_effects=True, vmem_limit_bytes=56 << 20
        ),
        name="forward",
    )(x, vectors, modulate, first_kernel, second_kernel)


def attention_kernel(
    att_ref, mid_ref, cot_ref, vec_ref, jw_any, ow_any,
    res_ref, ag_ref, gjo_ref, gs_ref,
    jw, ow, att, att_t, kv, kv_t, q8, d_out_t, qm, dom, s_ref, eb, dsb, mix_t, dq_t, dq, dkv,
    part, got_core, to_x, got_x, wsem, gsem, hsem, asem, bsem,
):
    images, pixels, channels = att_ref.shape
    whole = 4 * pixels
    chunk = 128
    pair_lanes = 2 * HEAD
    pairs = channels // pair_lanes
    i, r, c, who = peers()
    loads = [
        pltpu.make_async_copy(jw_any, jw, wsem.at[0]),
        pltpu.make_async_copy(ow_any, ow, wsem.at[1]),
    ]
    for cp in loads:
        cp.start()
    barrier = pltpu.get_barrier_semaphore()
    for k in (1, 2):
        pl.semaphore_signal(barrier, inc=1, device_id=who[k], device_id_type=MESH)

    def block(n):
        return pl.ds(pl.multiple_of(n * pixels, pixels), pixels)

    def shares(b):
        own, far = block(r), block(lax.rem(r + 2, 4))
        return [
            pltpu.make_async_remote_copy(
                att.at[b, rows], att.at[b, rows], gsem.at[b, n], hsem.at[b, n],
                device_id=who[k], device_id_type=MESH,
            )
            for n, (rows, k) in enumerate(((own, 1), (own, 2), (far, 1)))
        ]

    def arrivals(b):
        mate = r + 1 - 2 * c
        rows = (block(mate), block(lax.rem(r + 2, 4)), block(lax.rem(mate + 2, 4)))
        return [
            pltpu.make_async_remote_copy(
                att.at[b, w], att.at[b, w], gsem.at[b, n], hsem.at[b, n],
                device_id=who[(1, 2, 1)[n]], device_id_type=MESH,
            )
            for n, w in enumerate(rows)
        ]

    def forward(b):
        arrivals(b)[1].wait_recv()
        shares(b)[2].start()

    def sums_core(b):
        return [
            pltpu.make_async_remote_copy(
                part.at[b, block(2 * n + 1 - c)], got_core.at[b, n], asem.at[b, n], bsem.at[b, n],
                device_id=who[1], device_id_type=MESH,
            )
            for n in range(2)
        ]

    def sum_x(b):
        return pltpu.make_async_remote_copy(
            to_x.at[b], got_x.at[b], asem.at[b, 2], bsem.at[b, 2],
            device_id=who[2], device_id_type=MESH,
        )

    def pass_on(b):
        x = lax.div(r, 2)
        for cp in sums_core(b):
            cp.wait_recv()
        far = 1 - x
        to_x[b] = (
            part[b, block(2 * far + c)].astype(float_type) + got_core[b, far].astype(float_type)
        ).astype(low_type)
        sum_x(b).start()
        ag_ref[b] = part[b, block(r)].astype(float_type) + got_core[b, x].astype(float_type)

    def keep_own(b, _):
        att[b, block(r)] = att_ref[b]
        return 0

    lax.fori_loop(0, images, keep_own, 0)
    pl.semaphore_wait(barrier, 2)
    for b in range(images):
        shares(b)[0].start()
        shares(b)[1].start()
    for cp in loads:
        cp.wait()
    forward(0)
    lane = lax.broadcasted_iota(jnp.int32, (pixels, pair_lanes), 1)

    def masked(v):
        return jnp.concatenate(
            [jnp.where(lane < HEAD, v, 0.0), jnp.where(lane >= HEAD, v, 0.0)], axis=0
        ).astype(low_type)

    def dot(a, b):
        return jnp.dot(a, b, preferred_element_type=float_type)

    def dot_nt(a, b):
        return lax.dot_general(a, b, contract_cols, preferred_element_type=float_type)

    def one_image(b, _):
        a = arrivals(b)
        a[0].wait_recv()
        a[2].wait_recv()
        bias = jnp.concatenate([jnp.zeros((1, channels), float_type), vec_ref[1:2]], axis=1)
        for n in range(4):
            rows = pl.ds(n * pixels, pixels)
            kv[rows] = (dot(att[b, rows], jw[:, channels:]) + bias).astype(low_type)
        for n in range(2 * channels // 128):
            cols = pl.ds(n * 128, 128)
            kv_t[cols, :] = kv[:, cols].T
        q = (dot(att_ref[b], jw[:, :channels]) + vec_ref[0:1]).astype(low_type)
        q8[...] = (q.astype(float_type) * HEAD ** (-0.5)).astype(low_type)
        d_out = dot_nt(cot_ref[b], ow[...]).astype(low_type).astype(float_type)
        d_out_t[...] = d_out.T

        @pl.when(b > 0)
        def _():
            pass_on(b - 1)

        def one_pair(t, _):
            lanes = pl.ds(pl.multiple_of(t * pair_lanes, pair_lanes), pair_lanes)
            v_lanes = pl.ds(pl.multiple_of(channels + t * pair_lanes, pair_lanes), pair_lanes)
            qm[...] = masked(q8[:, lanes].astype(float_type))
            peak = None
            for n in range(whole // chunk):
                rows = pl.ds(n * chunk, chunk)
                s = dot_nt(kv[rows, lanes], qm[...])
                s_ref[rows] = s
                top = jnp.max(s.reshape(chunk // 8, 8, 2 * pixels), axis=0)
                peak = top if peak is None else jnp.maximum(peak, top)
            peak = jnp.max(peak, axis=0, keepdims=True)
            total = None
            for n in range(whole // chunk):
                rows = pl.ds(n * chunk, chunk)
                e = jnp.exp(s_ref[rows] - peak)
                eb[rows] = e.astype(low_type)
                more = jnp.sum(e.reshape(chunk // 8, 8, 2 * pixels), axis=0)
                total = more if total is None else total + more
            over = 1.0 / jnp.sum(total, axis=0, keepdims=True)
            inner, scaled = [], []
            for j in range(2):
                head = pl.ds(pl.multiple_of(t * pair_lanes + j * HEAD, HEAD), HEAD)
                v_head = pl.ds(pl.multiple_of(channels + t * pair_lanes + j * HEAD, HEAD), HEAD)
                cols = slice(j * pixels, (j + 1) * pixels)
                mt = dot(kv_t[v_head, :], eb[:, cols]) * over[:, cols]
                mix_t[b, head] = mt.astype(low_type)
                g = (d_out_t[head] * over[:, cols]).astype(low_type).astype(float_type)
                inner.append(jnp.sum(g * mt, axis=0, keepdims=True))
                scaled.append(g)
            inner = jnp.concatenate(inner, axis=1)
            dom[...] = masked(jnp.concatenate(scaled, axis=0).T)
            for n in range(whole // chunk):
                rows = pl.ds(n * chunk, chunk)
                dp = dot_nt(kv[rows, v_lanes], dom[...])
                dsb[rows] = (eb[rows].astype(float_type) * (dp - inner)).astype(low_type)
            for j in range(2):
                head = pl.ds(pl.multiple_of(t * pair_lanes + j * HEAD, HEAD), HEAD)
                cols = slice(j * pixels, (j + 1) * pixels)
                dq_t[head] = dot(kv_t[head, :], dsb[:, cols]) * HEAD ** (-0.5)
            dkv[b, :, lanes] = dot(dsb[...], qm[...]).astype(low_type)
            dkv[b, :, v_lanes] = dot(eb[...], dom[...]).astype(low_type)
            return 0

        lax.fori_loop(0, pairs, one_pair, 0)
        dq[b] = dq_t[...].T.astype(low_type)
        for n in range(4):
            rows = pl.ds(n * pixels, pixels)
            part[b, rows] = dot_nt(dkv[b, rows], jw[:, channels:]).astype(low_type)
        part[b, block(r)] = (
            part[b, block(r)].astype(float_type) + dot_nt(dq[b], jw[:, :channels])
        ).astype(low_type)
        for cp in sums_core(b):
            cp.start()

        @pl.when(b + 1 < images)
        def _():
            forward(b + 1)

        mixed = mix_t[b].T
        res_ref[b] = (mid_ref[b] + dot(mixed, ow[...]) + vec_ref[2:3]).astype(low_type)
        return 0

    lax.fori_loop(0, images, one_image, 0)
    pass_on(images - 1)
    ones = jnp.ones((16, whole), low_type)
    for b in range(images):
        att_t[b, 0:channels] = att[b].T
        att_t[b, channels:] = ones
    kv_sum = None
    q_sum = None
    o_sum = None
    for b in range(images):
        more = dot(att_t[b], dkv[b])
        kv_sum = more if kv_sum is None else kv_sum + more
        more = dot(att_t[b, :, block(r)], dq[b])
        q_sum = more if q_sum is None else q_sum + more
        more = dot(mix_t[b], cot_ref[b])
        o_sum = more if o_sum is None else o_sum + more
    part_rows = channels // 4
    every = (q_sum, kv_sum[:, :channels], kv_sum[:, channels:], o_sum)
    for n, v in enumerate(every):
        for m in range(4):
            gjo_ref[m, n * part_rows : (n + 1) * part_rows] = v[
                m * part_rows : (m + 1) * part_rows
            ].astype(low_type)
    cot_sum = jnp.sum(jnp.sum(cot_ref[...].astype(float_type), axis=0), axis=0, keepdims=True)
    gs_ref[0:1] = q_sum[channels : channels + 1]
    gs_ref[1:2] = kv_sum[channels : channels + 1, channels:]
    gs_ref[2:3] = cot_sum
    for b in range(images):
        sum_x(b).wait_recv()
        ag_ref[b] += got_x[b].astype(float_type)
    for b in range(images):
        for cp in shares(b) + sums_core(b) + [sum_x(b)]:
            cp.wait_send()


def attention_call(att, middle, cot, vectors, joint_weight, output_weight):
    images, pixels, channels = att.shape
    whole = 4 * pixels
    vm = pl.BlockSpec(memory_space=pltpu.VMEM)
    hbm = pl.BlockSpec(memory_space=pl.ANY)

    def low(*shape):
        return pltpu.VMEM(shape, low_type)

    def wide(*shape):
        return pltpu.VMEM(shape, float_type)

    return pl.pallas_call(
        attention_kernel,
        out_shape=(
            jax.ShapeDtypeStruct(att.shape, low_type),
            jax.ShapeDtypeStruct(att.shape, float_type),
            jax.ShapeDtypeStruct((4, channels, channels), low_type),
            jax.ShapeDtypeStruct((8, channels), float_type),
        ),
        in_specs=[vm, vm, vm, vm, hbm, hbm],
        out_specs=(vm,) * 4,
        scratch_shapes=[
            low(channels, 3 * channels), low(channels, channels), low(images, whole, channels),
            low(images, channels + 16, whole), low(whole, 2 * channels), low(2 * channels, whole),
            low(pixels, channels), wide(channels, pixels), low(2 * pixels, 2 * HEAD),
            low(2 * pixels, 2 * HEAD), wide(whole, 2 * pixels), low(whole, 2 * pixels),
            low(whole, 2 * pixels), low(images, channels, pixels), wide(channels, pixels),
            low(images, pixels, channels), low(images, whole, 2 * channels),
            low(images, whole, channels), low(images, 2, pixels, channels),
            low(images, pixels, channels), low(images, pixels, channels),
            pltpu.SemaphoreType.DMA((2,)), pltpu.SemaphoreType.DMA((images, 3)),
            pltpu.SemaphoreType.DMA((images, 3)), pltpu.SemaphoreType.DMA((images, 3)),
            pltpu.SemaphoreType.DMA((images, 3)),
        ],
        compiler_params=pltpu.CompilerParams(
            collective_id=1, has_side_effects=True, vmem_limit_bytes=56 << 20
        ),
        name="attention",
    )(att, middle, cot, vectors, joint_weight, output_weight)


def chip_peers(i, r):
    size = lax.axis_size("img")
    z = lax.rem(lax.div(i, 2), 4)
    e = lax.div(i, 8)
    others = (z + 1 - 2 * lax.rem(z, 2), lax.rem(z + 2, 4), 3 - z)
    more = size // 8
    return {
        "y": [(i + 1 - 2 * lax.rem(i, 2), r)],
        "z": [(i + 2 * (n - z), r) for n in others],
        "e": [(i + 8 * (lax.rem(e + k, more) - e), r) for k in range(1, more)],
        "at": (lax.rem(i, 2), z),
        "pieces": others,
    }


class Reduction:
    def __init__(self, out, lanes, n, q, refs, who, place, cs, cr, es, er):
        if n is not None:
            refs = (refs[0].at[n],) + tuple(ref.at[n] for ref in refs[1:])
        (self.grad, self.got_core, self.to_x, self.got_x, self.own, self.to_y, self.got_y,
         self.to_z, self.got_z, self.got_e) = refs
        self.out, self.lanes, self.q, self.who = out, lanes, q, who
        self.c, self.x, self.chips = place
        self.y, self.z = self.chips["at"]
        self.sems = (cs, cr, es, er)
        self.size = self.own.shape[0]

    def copy(self, src, dst, n, at, extra=False):
        send, recv = self.sems[2:] if extra else self.sems[:2]
        return pltpu.make_async_remote_copy(
            src, dst, send.at[self.q, n], recv.at[self.q, n], device_id=at, device_id_type=MESH
        )

    def half(self, y):
        size = self.size // 2
        return pl.ds(pl.multiple_of(y * size, size), size)

    def piece(self, z, y=0):
        size = self.size // 8
        return pl.ds(pl.multiple_of(y * (self.size // 2) + z * size, size), size)

    def core_copies(self):
        return [
            self.copy(self.grad.at[2 * n + 1 - self.c], self.got_core.at[n], n, self.who[1])
            for n in range(2)
        ]

    def x_copies(self):
        return [self.copy(self.to_x, self.got_x, 2, self.who[2])]

    def y_copies(self):
        return [self.copy(self.to_y, self.got_y, 3, self.chips["y"][0])]

    def z_copies(self):
        return [
            self.copy(self.to_z.at[self.piece(p)], self.got_z.at[n], 4 + n, at)
            for n, (p, at) in enumerate(zip(self.chips["pieces"], self.chips["z"]))
        ]

    def extra_copies(self):
        src = self.to_z.at[self.piece(self.z)]
        return [
            self.copy(src, self.got_e.at[n], n, at, True) for n, at in enumerate(self.chips["e"])
        ]

    def back_z_copies(self):
        part = self.out.at[self.piece(self.z, self.y), self.lanes]
        return [self.copy(part, part, 7 + n, at) for n, at in enumerate(self.chips["z"])]

    def back_y_copies(self):
        part = self.out.at[self.half(self.y), self.lanes]
        return [self.copy(part, part, 10, self.chips["y"][0])]

    def core(self):
        for cp in self.core_copies():
            cp.start()

    def across_x(self):
        for cp in self.core_copies():
            cp.wait_recv()
        far = 1 - self.x
        self.to_x[...] = (
            self.grad[2 * far + self.c].astype(float_type) + self.got_core[far].astype(float_type)
        ).astype(low_type)
        self.x_copies()[0].start()
        self.own[...] = self.grad[2 * self.x + self.c].astype(float_type) + self.got_core[
            self.x
        ].astype(float_type)

    def across_y(self):
        self.x_copies()[0].wait_recv()
        self.own[...] += self.got_x[...].astype(float_type)
        self.to_y[...] = self.own[self.half(1 - self.y)].astype(low_type)
        self.y_copies()[0].start()

    def across_z(self):
        self.y_copies()[0].wait_recv()
        rows = self.half(self.y)
        v = self.own[rows] + self.got_y[...].astype(float_type)
        self.own[rows] = v
        self.to_z[...] = v.astype(low_type)
        for cp in self.z_copies():
            cp.start()

    def back_z(self):
        for cp in self.z_copies():
            cp.wait_recv()
        rows = self.piece(self.z, self.y)
        v = self.own[rows]
        for n in range(3):
            v = v + self.got_z[n].astype(float_type)
        if self.chips["e"]:
            self.to_z[self.piece(self.z)] = v.astype(low_type)
            for cp in self.extra_copies():
                cp.start()
            for n, cp in enumerate(self.extra_copies()):
                cp.wait_recv()
                v = v + self.got_e[n].astype(float_type)
        self.out[rows, self.lanes] = v.astype(low_type)
        for cp in self.back_z_copies():
            cp.start()

    def back_y(self):
        for cp in self.back_z_copies():
            cp.wait_recv()
        self.back_y_copies()[0].start()

    def end(self):
        self.back_y_copies()[0].wait_recv()

    def drain(self):
        for cp in (
            self.core_copies() + self.x_copies() + self.y_copies() + self.z_copies()
            + self.extra_copies() + self.back_z_copies() + self.back_y_copies()
        ):
            cp.wait_send()


def backward_kernel(
    ag_ref, mid_ref, cot_ref, hid_ref, x_ref, act1_ref, act2_ref, st_ref, vec_ref, mod_ref,
    gjo_ref, sums_ref, emb_ref, w1_any, w2_any, ew_any,
    gx_ref, gw1_ref, gw2_ref, go_ref, gv_ref, ge_ref, gc_ref, geo_ref,
    w1, w2, ew, ones, grad1, grad2, act_t, skip, slope_grad, m1, m3, got, gs_ref, mg_ref,
    gw, w_core, w_to_x, w_got_x, w_own, w_to_y, w_got_y, w_to_z, w_got_z, w_got_e,
    o_core, o_to_x, o_got_x, o_own, o_to_y, o_got_y, o_to_z, o_got_z, o_got_e,
    v_own, v_row, v_one, v_y, v_two, v_z, v_three, v_e, g_row, gat, left, hot,
    wsem, ssem, rsem, cs, cr, es, er, vs, vr, gsem, hsem,
):
    images, pixels, channels = x_ref.shape
    width = 32
    edge = pixels - width
    span = pixels + 2 * width
    rows_in = pixels // width
    entries = 4.0 * pixels * (channels // GROUPS)
    i, r, c, who = peers()
    loads = [
        pltpu.make_async_copy(w2_any, w2, wsem.at[0]),
        pltpu.make_async_copy(w1_any, w1, wsem.at[1]),
        pltpu.make_async_copy(ew_any, ew, wsem.at[2]),
    ]
    for cp in loads:
        cp.start()
    barrier = pltpu.get_barrier_semaphore()
    chips = chip_peers(i, r)
    greeted = list(who.values()) + chips["y"] + chips["z"] + chips["e"]
    for at in greeted:
        pl.semaphore_signal(barrier, inc=1, device_id=at, device_id_type=MESH)
    place = (c, lax.div(r, 2), chips)
    ones[...] = block_ones(channels, channels // GROUPS)
    gs_ref[...] = jnp.zeros(gs_ref.shape, float_type)
    quarter = 9 * channels // 4
    padded = gw.shape[2]
    mg_ref[...] = jnp.zeros(mg_ref.shape, float_type)
    for n in range(6):
        for m in range(4):
            gw[n, m, quarter:padded] = jnp.zeros((padded - quarter, 128), low_type)
    inner = pl.multiple_of(edge * (1 - c), width)
    outer = pl.multiple_of(edge * c, width)
    outer_live = jnp.logical_and(r > 0, r < 3)
    stat = pl.ds(0, 16)
    halo = pl.ds(16, width)
    half = math.sqrt(0.5)

    def chunk(out, lanes, n, q, refs):
        return Reduction(out, lanes, n, q, refs, who, place, cs, cr, es, er)

    refs = (gw, w_core, w_to_x, w_got_x, w_own, w_to_y, w_got_y, w_to_z, w_got_z, w_got_e)
    red2 = [chunk(gw2_ref, slice(128 * n, 128 * n + 128), n, n, refs) for n in range(3)]
    red1 = [chunk(gw1_ref, slice(128 * n, 128 * n + 128), n + 3, n + 3, refs) for n in range(3)]
    refs = (gjo_ref, o_core, o_to_x, o_got_x, o_own, o_to_y, o_got_y, o_to_z, o_got_z, o_got_e)
    red0 = chunk(go_ref, slice(0, channels), None, 6, refs)

    def stat_copies(p, b):
        return [
            pltpu.make_async_remote_copy(
                m1.at[p, b, stat], got.at[p, b, k - 1, stat], ssem.at[p, b, k - 1],
                rsem.at[p, b, k - 1], device_id=who[k], device_id_type=MESH,
            )
            for k in (1, 2, 3)
        ]

    def halo_copies(p, b):
        return [
            pltpu.make_async_remote_copy(
                src.at[p, b, halo], got.at[p, b, k - 1, halo], ssem.at[p, b, k + 2],
                rsem.at[p, b, k + 2], device_id=who[k], device_id_type=MESH,
            )
            for k, src in ((1, m1), (3, m3))
        ]

    def send_stats(p, b, first, second):
        m1[p, b, 0:16] = pack_stats(first, second)
        for cp in stat_copies(p, b):
            cp.start()

    def receive_stats(p, b):
        for cp in stat_copies(p, b):
            cp.wait_recv()
        parts = [m1[p, b, 0:16]] + [got[p, b, k, 0:16] for k in range(3)]
        return combine_stats(parts, ones[...], entries)

    def send_halo(p, b, buf):
        middle = slice(channels, 2 * channels)
        m1[p, b, 16:48] = buf[b, pl.ds(inner + width, width), middle]
        m3[p, b, 16:48] = buf[b, pl.ds(outer + width, width), middle]
        for cp in halo_copies(p, b):
            cp.start()

    def receive_halo(p, b, buf):
        for cp in halo_copies(p, b):
            cp.wait_recv()
        v = got[p, b, 0, 16:48].astype(float_type)
        fill_row(buf.at[b], pl.multiple_of((pixels + width) * (1 - c), width), v, channels, width)
        v = jnp.where(outer_live, got[p, b, 2, 16:48].astype(float_type), 0.0)
        fill_row(buf.at[b], pl.multiple_of((pixels + width) * c, width), v, channels, width)

    def data_grad(buf, b, w):
        total = None
        for dy in range(3):
            for dx in range(3):
                tap = 3 * dy + dx
                more = lax.dot_general(
                    buf[b, (2 - dy) * width : (2 - dy) * width + pixels,
                        (2 - dx) * channels : (3 - dx) * channels],
                    w[tap * channels : (tap + 1) * channels, :],
                    contract_cols, preferred_element_type=float_type,
                )
                total = more if total is None else total + more
        return total

    def kernel_grad(act_ref, buf, base):
        for b in range(images):
            act_t[:, b * span : b * span + pixels] = act_ref[b].T
        reach = images * span - 2 * width
        flat = buf.reshape(images * span, 3 * channels)
        for dy in range(3):
            g = jnp.dot(
                act_t[:, 0:reach], flat[(2 - dy) * width : (2 - dy) * width + reach, :],
                preferred_element_type=float_type,
            )
            for dx in range(3):
                tap = 3 * dy + dx
                at = (2 - dx) * channels
                for m in range(4):
                    lo = max(tap * channels, m * quarter)
                    hi = min((tap + 1) * channels, (m + 1) * quarter)
                    for n in range(3 if lo < hi else 0):
                        gw[base + n, m, lo - m * quarter : hi - m * quarter] = g[
                            lo - tap * channels : hi - tap * channels,
                            at + 128 * n : at + 128 * n + 128,
                        ].astype(low_type)

    def remote(src, dst, send, recv, at):
        return pltpu.make_async_remote_copy(
            src, dst, send, recv, device_id=at, device_id_type=MESH
        )

    def start(copies):
        for cp in copies:
            cp.start()

    def arrived(copies):
        for cp in copies:
            cp.wait_recv()

    zs, extras = chips["z"], chips["e"]

    def small_row_copies(s):
        return [
            remote(v_own.at[s], v_row.at[s, k - 1], vs.at[s, k - 1], vr.at[s, k - 1], who[k])
            for k in (1, 2, 3)
        ]

    def small_y_copies(s):
        return [remote(v_one.at[s], v_y.at[s], vs.at[s, 3], vr.at[s, 3], chips["y"][0])]

    def small_z_copies(s):
        return [
            remote(v_two.at[s], v_z.at[s, n], vs.at[s, 4 + n], vr.at[s, 4 + n], at)
            for n, at in enumerate(zs)
        ]

    def small_e_copies(s):
        return [
            remote(v_three.at[s], v_e.at[s, n], vs.at[s, 7 + n], vr.at[s, 7 + n], at)
            for n, at in enumerate(extras)
        ]

    def small_row(s):
        v_own[s] = gs_ref[...]
        start(small_row_copies(s))

    def small_y(s):
        arrived(small_row_copies(s))
        v_one[s] = v_own[s] + v_row[s, 0] + v_row[s, 1] + v_row[s, 2]
        start(small_y_copies(s))

    def small_z(s):
        arrived(small_y_copies(s))
        v_two[s] = v_one[s] + v_y[s]
        start(small_z_copies(s))

    def small_end(s):
        arrived(small_z_copies(s))
        v_three[s] = v_two[s] + v_z[s, 0] + v_z[s, 1] + v_z[s, 2]
        total = v_three[s]
        if extras:
            start(small_e_copies(s))
            arrived(small_e_copies(s))
            for n in range(len(extras)):
                total = total + v_e[s, n]
        gv_ref[s] = total

    def gather_row_copies():
        return [
            remote(mg_ref, g_row.at[k - 1], gsem.at[k - 1], hsem.at[k - 1], who[k])
            for k in (1, 2, 3)
        ]

    def gather_copies():
        blocks = [pl.ds(i, 1), pl.ds(pl.multiple_of(i - lax.rem(i, 2), 2), 2)]
        blocks.append(pl.ds(pl.multiple_of(i - lax.rem(i, 8), 8), 8))
        found = []
        for rows, places in zip(blocks, (chips["y"], zs, extras)):
            for at in places:
                n = 3 + len(found)
                found.append(remote(gat.at[rows], gat.at[rows], gsem.at[n], hsem.at[n], at))
        return found

    def gather_row():
        start(gather_row_copies())

    def gather_y():
        arrived(gather_row_copies())
        gat[i] = emb_ref[...] + mg_ref[...] + g_row[0] + g_row[1] + g_row[2]
        start(gather_copies()[:1])

    def gather_z():
        arrived(gather_copies()[:1])
        start(gather_copies()[1:4])

    def gather_end():
        arrived(gather_copies()[1:4])
        start(gather_copies()[4:])
        arrived(gather_copies()[4:])

    def three_terms(v):
        a = v.astype(low_type)
        b = (v - a.astype(float_type)).astype(low_type)
        d = (v - a.astype(float_type) - b.astype(float_type)).astype(low_type)
        return jnp.concatenate([a, b, d], axis=0)

    def embedding():
        ge_ref[...] = jnp.zeros(ge_ref.shape, float_type)
        gc_ref[...] = jnp.zeros(gc_ref.shape, float_type)
        geo_ref[...] = jnp.zeros(geo_ref.shape, float_type)
        lax.fori_loop(0, gat.shape[0] // 8, embedding_part, 0)

    def embedding_part(part_of, _):
        every = 64
        full = gat[pl.ds(pl.multiple_of(part_of * 8, 8), 8)].reshape(every, 2 * channels)
        place_of = lax.rem(lax.broadcasted_iota(jnp.int32, (every, 2 * channels), 0), 8)
        live = place_of < images
        grad = jnp.where(live, full, 0.0)
        held = jnp.where(live, pltpu.roll(full, every - images, 0), 0.0)
        act = jnp.where(live, half_silu(held), 0.0).astype(low_type)
        left[...] = jnp.concatenate([act, act, act], axis=0).T
        terms = three_terms(grad)
        size = 2 * channels // 4
        own = pl.ds(pl.multiple_of(r * size, size), size)
        ge_ref[...] += jnp.dot(left[own, :], terms, preferred_element_type=float_type)
        geo_ref[...] += jnp.broadcast_to(jnp.sum(grad, axis=0, keepdims=True), geo_ref.shape)
        active = lax.dot_general(terms, ew[...], contract_cols, preferred_element_type=float_type)
        active = active[0:every] + active[every : 2 * every] + active[2 * every :]
        back = jnp.where(live, active * slope_of(held), 0.0)
        classes = gc_ref.shape[0]
        row_of = lax.rem(lax.broadcasted_iota(jnp.int32, (every, 128), 0), 8)
        label = jnp.full((every, 128), -1.0, float_type)
        for b in range(images):
            rolled = pltpu.roll(full[:, 256 * b : 256 * b + 128], every - 2 * images + b, 0)
            label = jnp.where(row_of == b, rolled, label)
        for n in range(hot.shape[0] // 128):
            kind = lax.broadcasted_iota(jnp.int32, (every, 128), 1) + 128 * n + r * classes
            hit = jnp.where(label == kind.astype(float_type), 1.0, 0.0).astype(low_type)
            hot[128 * n : 128 * (n + 1), :] = jnp.concatenate([hit, hit, hit], axis=0).T
        found = jnp.dot(hot[...], three_terms(back), preferred_element_type=float_type)
        gc_ref[...] += found[0:classes]
        return 0

    def vec(n):
        return vec_ref[n : n + 1, :]

    def col_sum(v):
        return jnp.sum(v, axis=0, keepdims=True)

    def slope_of(pre):
        s = 0.5 * jnp.tanh(0.5 * pre) + 0.5
        return s * (1.0 + pre * (1.0 - s))

    for b in range(images):
        act_t[:, b * span + pixels : (b + 1) * span] = jnp.zeros((channels, 2 * width), low_type)
    pl.semaphore_wait(barrier, len(greeted))
    red0.core()

    def step0(b, _):
        u = ag_ref[b]
        first = col_sum(u)
        second = col_sum(u * ((mid_ref[b] - st_ref[b, 4:5]) * st_ref[b, 5:6]))
        gs_ref[6:7] += second
        gs_ref[7:8] += first
        send_stats(0, b, first * vec(6), second * vec(6))
        return 0

    lax.fori_loop(0, images, step0, 0)
    red0.across_x()

    def step1(b, _):
        first, second = receive_stats(0, b)
        centre, scaled = st_ref[b, 4:5], st_ref[b, 5:6]
        total = jnp.zeros((1, channels), float_type)
        for row in range(rows_in):
            rows = pl.ds(row * width, width)
            normed = (mid_ref[b, rows] - centre) * scaled
            back = scaled * (ag_ref[b, rows] * vec(6) - first - normed * second)
            v = (cot_ref[b, rows].astype(float_type) + back) * half
            skip[b, rows] = v
            v = v.astype(low_type).astype(float_type)
            fill_row(grad2.at[b], (row + 1) * width, v, channels, width)
            total += col_sum(v)
        gs_ref[5:6] += total
        send_halo(1, b, grad2)
        return 0

    lax.fori_loop(0, images, step1, 0)
    loads[0].wait()

    def step2(b, _):
        receive_halo(1, b, grad2)
        upstream = data_grad(grad2, b, w2)
        grow = 1.0 + mod_ref[b, 0:1]
        normed = (hid_ref[b] - st_ref[b, 2:3]) * st_ref[b, 3:4]
        pre = (normed * vec(3) + vec(4)) * grow + mod_ref[b, 1:2]
        v = upstream * slope_of(pre)
        slope_grad[b] = v
        first, second = col_sum(v), col_sum(v * normed)
        mg_ref[pl.ds(b, 1), 0:channels] = vec(3) * second + vec(4) * first
        mg_ref[pl.ds(b, 1), channels:] = first
        first, second = grow * first, grow * second
        gs_ref[3:4] += second
        gs_ref[4:5] += first
        send_stats(2, b, first * vec(3), second * vec(3))
        return 0

    lax.fori_loop(0, images, step2, 0)
    red0.across_y()
    kernel_grad(act2_ref, grad2, 0)
    for n in range(3):
        red2[n].core()
    gs_ref[8:11] = sums_ref[0:3]
    small_row(0)
    gather_row()
    for n in range(3):
        red2[n].across_x()
    red0.across_z()
    small_y(0)
    gather_y()

    def step3(b, _):
        first, second = receive_stats(2, b)
        centre, scaled = st_ref[b, 2:3], st_ref[b, 3:4]
        gain = (1.0 + mod_ref[b, 0:1]) * vec(3)
        total = jnp.zeros((1, channels), float_type)
        for row in range(rows_in):
            rows = pl.ds(row * width, width)
            normed = (hid_ref[b, rows] - centre) * scaled
            v = scaled * (slope_grad[b, rows] * gain - first - normed * second)
            v = v.astype(low_type).astype(float_type)
            fill_row(grad1.at[b], (row + 1) * width, v, channels, width)
            total += col_sum(v)
        gs_ref[2:3] += total
        send_halo(3, b, grad1)
        return 0

    lax.fori_loop(0, images, step3, 0)
    loads[1].wait()

    def step4(b, _):
        receive_halo(3, b, grad1)
        return 0

    lax.fori_loop(0, images, step4, 0)
    kernel_grad(act1_ref, grad1, 3)
    for n in range(3):
        red1[n].core()
    small_z(0)
    gather_z()
    red0.back_z()
    red2[0].across_y()
    for n in range(3):
        red1[n].across_x()

    def step5(b, _):
        upstream = data_grad(grad1, b, w1)
        normed = (x_ref[b].astype(float_type) - st_ref[b, 0:1]) * st_ref[b, 1:2]
        v = upstream * slope_of(normed * vec(0) + vec(1))
        slope_grad[b] = v
        first, second = col_sum(v), col_sum(v * normed)
        gs_ref[0:1] += second
        gs_ref[1:2] += first
        send_stats(4, b, first * vec(0), second * vec(0))
        return 0

    lax.fori_loop(0, images, step5, 0)
    small_row(1)
    red0.back_y()
    red2[1].across_y()
    red2[0].across_z()

    def step6(b, _):
        first, second = receive_stats(4, b)
        scaled = st_ref[b, 1:2]
        normed = (x_ref[b].astype(float_type) - st_ref[b, 0:1]) * scaled
        gx_ref[b] = skip[b] + scaled * (slope_grad[b] * vec(0) - first - normed * second)
        for p in (0, 2, 4):
            for cp in stat_copies(p, b):
                cp.wait_send()
        for p in (1, 3):
            for cp in halo_copies(p, b):
                cp.wait_send()
        return 0

    lax.fori_loop(0, images, step6, 0)
    small_y(1)
    small_end(0)
    gather_end()
    loads[2].wait()
    embedding()
    red0.end()
    red2[2].across_y()
    red2[1].across_z()
    red2[0].back_z()
    small_z(1)
    red1[0].across_y()
    red2[2].across_z()
    red2[1].back_z()
    red2[0].back_y()
    red1[1].across_y()
    red1[0].across_z()
    red2[2].back_z()
    red2[1].back_y()
    red2[0].end()
    red1[2].across_y()
    red1[1].across_z()
    red1[0].back_z()
    red2[2].back_y()
    red2[1].end()
    red1[2].across_z()
    red1[1].back_z()
    red1[0].back_y()
    red2[2].end()
    red1[2].back_z()
    red1[1].back_y()
    red1[0].end()
    red1[2].back_y()
    red1[1].end()
    red1[2].end()
    small_end(1)
    for red in [red0] + red1 + red2:
        red.drain()
    for s in range(2):
        for cp in small_row_copies(s) + small_y_copies(s) + small_z_copies(s) + small_e_copies(s):
            cp.wait_send()
    for cp in gather_row_copies() + gather_copies():
        cp.wait_send()


def backward_call(
    ag, mid, cot, hid, x, act1, act2, stats, vectors, modulate, joint, sums, emb, w1, w2, ew, classes
):
    images, pixels, channels = x.shape
    span = pixels + 64
    padded = -(-9 * channels // 4 // 128) * 128
    every = lax.axis_size("img")
    more = every // 8
    some = max(more - 1, 1)
    vm = pl.BlockSpec(memory_space=pltpu.VMEM)
    hbm = pl.BlockSpec(memory_space=pl.ANY)

    def low(*shape):
        return pltpu.VMEM(shape, low_type)

    def wide(*shape):
        return pltpu.VMEM(shape, float_type)

    return pl.pallas_call(
        backward_kernel,
        out_shape=(
            jax.ShapeDtypeStruct(x.shape, float_type),
            jax.ShapeDtypeStruct((padded, channels), low_type),
            jax.ShapeDtypeStruct((padded, channels), low_type),
            jax.ShapeDtypeStruct((channels, channels), low_type),
            jax.ShapeDtypeStruct((2, 16, channels), float_type),
            jax.ShapeDtypeStruct((2 * channels // 4, 2 * channels), float_type),
            jax.ShapeDtypeStruct((classes // 4, 2 * channels), float_type),
            jax.ShapeDtypeStruct((8, 2 * channels), float_type),
        ),
        in_specs=[vm] * 13 + [hbm] * 3,
        out_specs=(vm,) * 8,
        scratch_shapes=[
            low(*w1.shape), low(*w2.shape), low(*ew.shape), low(channels, channels),
            low(images, span, 3 * channels), low(images, span, 3 * channels),
            low(channels, images * span), wide(images, pixels, channels),
            wide(images, pixels, channels), low(5, images, 48, channels),
            low(5, images, 48, channels), low(5, images, 3, 48, channels),
            wide(16, channels), wide(8, 2 * channels),
            low(6, 4, padded, 128), low(6, 2, padded, 128), low(6, padded, 128),
            low(6, padded, 128), wide(6, padded, 128), low(6, padded // 2, 128),
            low(6, padded // 2, 128), low(6, padded // 2, 128), low(6, 3, padded // 8, 128),
            low(6, some, padded // 8, 128),
            low(2, channels, channels), low(channels, channels), low(channels, channels),
            wide(channels, channels), low(channels // 2, channels), low(channels // 2, channels),
            low(channels // 2, channels), low(3, channels // 8, channels),
            low(some, channels // 8, channels),
            wide(2, 16, channels), wide(2, 3, 16, channels), wide(2, 16, channels),
            wide(2, 16, channels),
            wide(2, 16, channels), wide(2, 3, 16, channels), wide(2, 16, channels),
            wide(2, some, 16, channels), wide(3, 8, 2 * channels), wide(every, 8, 2 * channels),
            low(2 * channels, 192), low(256, 192),
            pltpu.SemaphoreType.DMA((3,)), pltpu.SemaphoreType.DMA((5, images, 6)),
            pltpu.SemaphoreType.DMA((5, images, 6)), pltpu.SemaphoreType.DMA((7, 11)),
            pltpu.SemaphoreType.DMA((7, 11)), pltpu.SemaphoreType.DMA((7, some)),
            pltpu.SemaphoreType.DMA((7, some)), pltpu.SemaphoreType.DMA((2, 6 + more)),
            pltpu.SemaphoreType.DMA((2, 6 + more)), pltpu.SemaphoreType.DMA((6 + more,)),
            pltpu.SemaphoreType.DMA((6 + more,)),
        ],
        compiler_params=pltpu.CompilerParams(
            collective_id=2, has_side_effects=True, vmem_limit_bytes=56 << 20
        ),
        name="backward",
    )(
        ag, mid, cot, hid, x, act1, act2, stats, vectors, modulate, joint, sums, emb, w1, w2, ew
    )


def shards(
    images,
    level_count,
    level_index,
    labels,
    first_gain,
    first_shift,
    first_kernel,
    first_offset,
    embed_weight,
    embed_offset,
    class_table,
    second_gain,
    second_shift,
    second_kernel,
    second_offset,
    third_gain,
    third_shift,
    joint_weight,
    joint_offset,
    output_weight,
    output_offset,
    cotangent,
):
    image_count, stripe_rows, image_width, channels = images.shape
    layout = (image_count, stripe_rows, image_width, channels)
    pixels = stripe_rows * image_width
    gain_one = first_gain.astype(float_type)
    shift_one = first_shift.astype(float_type)
    gain_two = second_gain.astype(float_type)
    shift_two = second_shift.astype(float_type)
    gain_three = third_gain.astype(float_type)
    features = noise_features(level_count, level_index)
    class_count = class_table.shape[0]
    one_hot = (labels[:, None] == jnp.arange(class_count, dtype=jnp.int32)[None, :]).astype(
        low_type
    )
    embedded = features + jnp.dot(one_hot, class_table, preferred_element_type=float_type)
    embed_act = jax.nn.silu(embedded).astype(low_type)
    modulate = jnp.dot(
        embed_act, embed_weight, preferred_element_type=float_type
    ) + embed_offset.astype(float_type)
    scale_part = modulate[:, :channels]
    vectors = jnp.stack(
        [
            first_gain, first_shift, first_offset, second_gain, second_shift, second_offset,
            third_gain, third_shift,
        ]
    ).astype(float_type)
    x = images.reshape(image_count, pixels, channels)
    hidden, middle, attend, act_one, act_two, stats = forward_call(
        x, vectors, modulate.reshape(image_count, 2, channels), first_kernel, second_kernel
    )
    attention_vectors = jnp.stack(
        [joint_offset[:channels], joint_offset[channels:], output_offset]
    ).astype(float_type)
    cot = cotangent.reshape(image_count, pixels, channels)
    result, attend_grad, joint_blocks, offset_sums = attention_call(
        attend, middle, cot, attention_vectors, joint_weight, output_weight
    )
    marks = jnp.repeat(labels.astype(float_type), 2 * channels // image_count)[None]
    rows = jnp.concatenate([jnp.zeros_like(embedded), embedded, marks, jnp.zeros_like(marks)])
    (
        images_gradient, first_block, second_block, joint_block, sums, embed_weight_grad,
        class_table_grad, embed_offset_grad,
    ) = backward_call(
        attend_grad, middle, cot, hidden, x, act_one, act_two, stats, vectors,
        modulate.reshape(image_count, 2, channels), joint_blocks, offset_sums, rows,
        first_kernel, second_kernel, embed_weight, class_count,
    )
    stripe = lax.axis_index("row")
    size = channels // 4
    own = lax.dynamic_slice_in_dim(sums, stripe * size, size, 2)
    both = lax.dynamic_slice_in_dim(
        jnp.concatenate([sums[0, 8], sums[0, 9]]), stripe * 2 * size, 2 * size, 0
    )
    embed_offset_grad = lax.dynamic_slice_in_dim(
        embed_offset_grad[0], stripe * 2 * size, 2 * size, 0
    )
    quarter = 9 * channels // 4
    joint_weight_grad = jnp.concatenate(
        [joint_block[n * size : (n + 1) * size] for n in range(3)], axis=1
    ).astype(float_type)
    return (
        result.reshape(layout), images_gradient.reshape(layout), own[1, 0], own[1, 1],
        first_block[:quarter].astype(float_type), own[1, 2], embed_weight_grad,
        embed_offset_grad, class_table_grad, own[0, 3], own[0, 4],
        second_block[:quarter].astype(float_type), own[0, 5], own[0, 6], own[0, 7],
        joint_weight_grad, both, joint_block[3 * size :].astype(float_type), own[0, 10],
    )


def solution(mesh):
    in_specs = (
        (P("img", "row", None, None),) + (P("img"),) * 3 + (P(),) * 17
        + (P("img", "row", None, None),)
    )
    row, rows = P("row"), P("row", None)
    out_specs = (
        P("img", "row", None, None), P("img", "row", None, None), row, row, rows, row, rows, row,
        rows, row, row, rows, row, row, row, rows, row, rows, row,
    )
    return jax.shard_map(shards, mesh=mesh, in_specs=in_specs, out_specs=out_specs, check_vma=False)
```

```python
import math

import jax
import jax.numpy as jnp
from jax import lax
from jax.experimental import pallas as pl
from jax.experimental.pallas import tpu as pltpu
from jax.sharding import PartitionSpec as P

GROUPS = 32
HEAD = 64
MESH = pl.DeviceIdType.MESH

norm_eps = 1e-05
sigma_least = 0.002
sigma_most = 80.0
sigma_power = 7.0
float_type = jnp.float32
low_type = jnp.bfloat16
contract_cols = (((1,), (1,)), ((), ()))


def peers():
    i = lax.axis_index("img")
    r = lax.axis_index("row")
    c = lax.rem(r, 2)
    near = r + 1 - 2 * c
    return (i, r, c, {1: (i, near), 2: (i, lax.rem(r + 2, 4)), 3: (i, 3 - r)})


def half_silu(v):
    h = 0.5 * v
    return h * jnp.tanh(h) + h


def fill_row(buf, start, act, channels, width):
    col = lax.broadcasted_iota(jnp.int32, (width, channels), 0)
    left = jnp.where(col == 0, 0.0, pltpu.roll(act, 1, 0))
    right = jnp.where(col == width - 1, 0.0, pltpu.roll(act, width - 1, 0))
    rows = pl.ds(start, width)
    buf[rows, 0:channels] = left.astype(low_type)
    buf[rows, channels : 2 * channels] = act.astype(low_type)
    buf[rows, 2 * channels : 3 * channels] = right.astype(low_type)


def pack_stats(first, second):
    channels = first.shape[1]
    row = lax.broadcasted_iota(jnp.int32, (8, channels), 0)

    def terms(v):
        a = v.astype(low_type).astype(float_type)
        b = (v - a).astype(low_type).astype(float_type)
        c = v - a - b
        return jnp.where(row == 0, a, jnp.where(row == 1, b, jnp.where(row == 2, c, 0.0)))

    return jnp.concatenate([terms(first), terms(second)], axis=0).astype(low_type)


def block_ones(channels, per):
    a = lax.broadcasted_iota(jnp.int32, (channels, channels), 0)
    b = lax.broadcasted_iota(jnp.int32, (channels, channels), 1)
    a = lax.shift_right_logical(a * 43691, 19)
    b = lax.shift_right_logical(b * 43691, 19)
    return jnp.where(a == b, 1.0, 0.0).astype(low_type)


def combine_stats(parts, ones, entries):
    total = jnp.dot(jnp.concatenate(parts, axis=0), ones, preferred_element_type=float_type)
    first = total[0:8] + total[16:24] + total[32:40] + total[48:56]
    second = total[8:16] + total[24:32] + total[40:48] + total[56:64]
    first = jnp.sum(first, axis=0, keepdims=True) * (1.0 / entries)
    second = jnp.sum(second, axis=0, keepdims=True) * (1.0 / entries)
    return first, second


def chip_peers(i, r):
    size = lax.axis_size("img")
    z = lax.rem(lax.div(i, 2), 4)
    e = lax.div(i, 8)
    others = (z + 1 - 2 * lax.rem(z, 2), lax.rem(z + 2, 4), 3 - z)
    more = size // 8
    return {
        "y": [(i + 1 - 2 * lax.rem(i, 2), r)],
        "z": [(i + 2 * (n - z), r) for n in others],
        "e": [(i + 8 * (lax.rem(e + k, more) - e), r) for k in range(1, more)],
        "at": (lax.rem(i, 2), z),
        "pieces": others,
    }


class Reduction:
    def __init__(self, out, lanes, n, q, refs, who, place, cs, cr, es, er):
        if n is not None:
            refs = (refs[0].at[n],) + tuple(ref.at[n] for ref in refs[1:])
        self.grad, self.got_core, self.got_x, self.own, self.got_y, self.got_z, self.got_e = refs
        self.out, self.lanes, self.q, self.who = out, lanes, q, who
        self.c, self.x, self.chips = place
        self.y, self.z = self.chips["at"]
        self.sems = (cs, cr, es, er)
        self.size = self.got_x.shape[0]

    def copy(self, src, dst, n, at, extra=False):
        send, recv = self.sems[2:] if extra else self.sems[:2]
        return pltpu.make_async_remote_copy(
            src, dst, send.at[self.q, n], recv.at[self.q, n], device_id=at, device_id_type=MESH
        )

    def half(self, y):
        size = self.size // 2
        return pl.ds(pl.multiple_of(y * size, size), size)

    def piece(self, z, y=0):
        size = self.size // 8
        return pl.ds(pl.multiple_of(y * (self.size // 2) + z * size, size), size)

    def core_copies(self):
        return [
            self.copy(self.grad.at[2 * n + 1 - self.c], self.got_core.at[n], n, self.who[1])
            for n in range(2)
        ]

    def x_copies(self):
        return [self.copy(self.grad.at[2 * (1 - self.x) + self.c], self.got_x, 2, self.who[2])]

    def y_copies(self):
        return [self.copy(self.got_x.at[self.half(1 - self.y)], self.got_y, 3, self.chips["y"][0])]

    def z_copies(self):
        return [
            self.copy(self.got_x.at[self.piece(p, self.y)], self.got_z.at[n], 4 + n, at)
            for n, (p, at) in enumerate(zip(self.chips["pieces"], self.chips["z"]))
        ]

    def extra_copies(self):
        src = self.got_x.at[self.piece(self.z, self.y)]
        return [
            self.copy(src, self.got_e.at[n], n, at, True) for n, at in enumerate(self.chips["e"])
        ]

    def back_z_copies(self):
        part = self.out.at[self.piece(self.z, self.y), self.lanes]
        return [self.copy(part, part, 7 + n, at) for n, at in enumerate(self.chips["z"])]

    def back_y_copies(self):
        part = self.out.at[self.half(self.y), self.lanes]
        return [self.copy(part, part, 10, self.chips["y"][0])]

    def core(self):
        for cp in self.core_copies():
            cp.start()

    def across_x(self):
        for cp in self.core_copies():
            cp.wait_recv()
        far = 1 - self.x
        block = 2 * far + self.c
        self.grad[block] = (
            self.grad[block].astype(float_type) + self.got_core[far].astype(float_type)
        ).astype(low_type)
        self.x_copies()[0].start()

    def chip_sum(self, rows):
        return (
            self.grad[2 * self.x + self.c, rows].astype(float_type)
            + self.got_core[self.x, rows].astype(float_type)
            + self.got_x[rows].astype(float_type)
        )

    def across_y(self):
        self.x_copies()[0].wait_recv()
        rows = self.half(1 - self.y)
        self.got_x[rows] = self.chip_sum(rows).astype(low_type)
        self.y_copies()[0].start()
        self.own[...] = self.chip_sum(self.half(self.y))

    def across_z(self):
        self.y_copies()[0].wait_recv()
        v = self.own[...] + self.got_y[...].astype(float_type)
        self.own[...] = v
        self.got_x[self.half(self.y)] = v.astype(low_type)
        for cp in self.z_copies():
            cp.start()

    def back_z(self):
        for cp in self.z_copies():
            cp.wait_recv()
        v = self.own[self.piece(self.z)]
        for n in range(3):
            v = v + self.got_z[n].astype(float_type)
        if self.chips["e"]:
            self.got_x[self.piece(self.z, self.y)] = v.astype(low_type)
            for cp in self.extra_copies():
                cp.start()
            for n, cp in enumerate(self.extra_copies()):
                cp.wait_recv()
                v = v + self.got_e[n].astype(float_type)
        self.out[self.piece(self.z, self.y), self.lanes] = v.astype(low_type)
        for cp in self.back_z_copies():
            cp.start()

    def back_y(self):
        for cp in self.back_z_copies():
            cp.wait_recv()
        self.back_y_copies()[0].start()

    def end(self):
        self.back_y_copies()[0].wait_recv()

    def drain(self):
        for cp in (
            self.core_copies() + self.x_copies() + self.y_copies() + self.z_copies()
            + self.extra_copies() + self.back_z_copies() + self.back_y_copies()
        ):
            cp.wait_send()


def block_kernel(
    x_ref, cot_ref, *rest,
):
    lines, rest = rest[:11], rest[11:]
    count_ref, index_ref, label_ref = rest[:3]
    (w1_any, w2_any, jw_any, ow_any, ew_any, ct_any,
    res_ref, gx_ref, gw1_ref, gw2_ref, go_ref, gv_ref, ge_ref, gc_ref, geo_ref,
    w1, w2, jw, ow, ew, ct, ones, hid, mid, mod, emb, act1_t, act2_t, st, m1, m3, got,
    att, att_t, kv, kv_t, q8, d_out_t, qm, dom, s_ref, eb, dsb, mix_t, dq_t, dq, dkv,
    got_core, got_x, ag, q_sum, kv_sum, o_sum, gjo,
    grad, slope_grad, gs, mg,
    gw, w_core, w_got_x, w_own, w_got_y, w_got_z, w_got_e,
    o_core, o_got_x, o_own, o_got_y, o_got_z, o_got_e,
    v_own, v_row, v_one, v_y, v_two, v_z, v_three, v_e, g_row, gat, left, hot,
    vec_ref, prep_ref, wsem, ssem, rsem, gsend, grecv, asem, bsem, cs, cr, es, er, vs, vr, gsem,
    hsem) = rest[3:]
    images, pixels, channels = x_ref.shape
    width = 32
    edge = pixels - width
    rows_in = pixels // width
    whole = 4 * pixels
    entries = float(whole * (channels // GROUPS))
    half = math.sqrt(0.5)
    quarter = 9 * channels // 4
    padded = gw.shape[2]
    chunk = 128
    pair_lanes = 2 * HEAD
    pairs = channels // pair_lanes
    i, r, c, who = peers()
    chips = chip_peers(i, r)
    place = (c, lax.div(r, 2), chips)
    inner = pl.multiple_of(edge * (1 - c), width)
    outer = pl.multiple_of(edge * c, width)
    inner_halo = pl.multiple_of((pixels + width) * (1 - c), width)
    outer_halo = pl.multiple_of((pixels + width) * c, width)
    outer_live = jnp.logical_and(r > 0, r < 3)
    loads = {
        name: pltpu.make_async_copy(src, dst, wsem.at[n])
        for n, (name, src, dst) in enumerate((
            ("ct", ct_any, ct), ("ew", ew_any, ew), ("w1", w1_any, w1), ("w2", w2_any, w2),
            ("jw", jw_any, jw), ("ow", ow_any, ow),
        ))
    }
    for cp in loads.values():
        cp.start()
    barrier = pltpu.get_barrier_semaphore()
    greeted = list(who.values()) + chips["y"] + chips["z"] + chips["e"]
    for at in greeted:
        pl.semaphore_signal(barrier, inc=1, device_id=at, device_id_type=MESH)

    abuf = grad.at[0]

    def dot(a, b):
        return jnp.dot(a, b, preferred_element_type=float_type)

    def dot_nt(a, b):
        return lax.dot_general(a, b, contract_cols, preferred_element_type=float_type)

    def vec(n):
        return vec_ref[n : n + 1, :]

    def col_sum(v):
        return jnp.sum(v, axis=0, keepdims=True)

    def slope_of(pre):
        s = 0.5 * jnp.tanh(0.5 * pre) + 0.5
        return s * (1.0 + pre * (1.0 - s))

    def remote(src, dst, send, recv, at):
        return pltpu.make_async_remote_copy(
            src, dst, send, recv, device_id=at, device_id_type=MESH
        )

    def start(copies):
        for cp in copies:
            cp.start()

    def arrived(copies):
        for cp in copies:
            cp.wait_recv()

    def some_images(step, first, last):
        def run(b, _):
            step(b)
            return 0

        lax.fori_loop(first, last, run, 0)

    def each_image(step):
        some_images(step, 0, images)

    message_rows = (48, 48, 48, 48, 48, 16, 48)

    def copies(p, b):
        full, stat = pl.ds(0, message_rows[p]), pl.ds(0, 16)
        return [
            remote(
                src.at[p, b, rows], got.at[p, b, k - 1, rows], ssem.at[p, b, k - 1],
                rsem.at[p, b, k - 1], who[k],
            )
            for k, src, rs in ((1, m1, full), (2, m1, stat), (3, m3, full))
            for rows in (rs,)
        ]

    def fill_message(p, b, first, second, edges=None):
        packed = pack_stats(first, second)
        m1[p, b, 0:16] = packed
        m3[p, b, 0:16] = packed
        if edges is not None:
            m1[p, b, 16:48] = edges(inner).astype(low_type)
            m3[p, b, 16:48] = edges(outer).astype(low_type)

    def send(p, b, first, second, edges=None):
        fill_message(p, b, first, second, edges)
        start(copies(p, b))

    def receive(p, b):
        arrived(copies(p, b))
        parts = [m1[p, b, 0:16]] + [got[p, b, k, 0:16] for k in range(3)]
        return combine_stats(parts, ones[...], entries)

    def receive_scale(p, b):
        first, second = receive(p, b)
        scaled = lax.rsqrt(second - first * first + norm_eps)
        st[b, 2 * p : 2 * p + 1] = first
        st[b, 2 * p + 1 : 2 * p + 2] = scaled
        return first, scaled

    def far_rows(p, b, k):
        return got[p, b, k, 16:48].astype(float_type)

    def fill_halo(buf, value):
        fill_row(buf, inner_halo, value(0), channels, width)
        fill_row(buf, outer_halo, jnp.where(outer_live, value(2), 0.0), channels, width)

    def convolve(w):
        depth = 3 * channels
        return sum(
            dot(abuf[width * dy : width * dy + pixels, :], w[depth * dy : depth * (dy + 1), :])
            for dy in range(3)
        )

    def data_grad(buf, b, w):
        total = None
        for dy in range(3):
            for dx in range(3):
                tap = 3 * dy + dx
                more = dot_nt(
                    buf[b, (2 - dy) * width : (2 - dy) * width + pixels,
                        (2 - dx) * channels : (3 - dx) * channels],
                    w[tap * channels : (tap + 1) * channels, :],
                )
                total = more if total is None else total + more
        return total

    def kernel_grad(act_t, buf, base):
        for dy in range(3):
            for dx in range(3):
                tap = 3 * dy + dx
                at = (2 - dx) * channels
                g = None
                for b in range(images):
                    more = dot(
                        act_t[:, b * pixels : (b + 1) * pixels],
                        buf[b, (2 - dy) * width : (2 - dy) * width + pixels, at : at + channels],
                    )
                    g = more if g is None else g + more
                g = g.astype(low_type)
                for m in range(4):
                    lo = max(tap * channels, m * quarter)
                    hi = min((tap + 1) * channels, (m + 1) * quarter)
                    for n in range(3 if lo < hi else 0):
                        gw[base + n, m, lo - m * quarter : hi - m * quarter] = g[
                            lo - tap * channels : hi - tap * channels, 128 * n : 128 * n + 128
                        ]

    def reduction(out, lanes, n, q, refs):
        return Reduction(out, lanes, n, q, refs, who, place, cs, cr, es, er)

    refs = (gw, w_core, w_got_x, w_own, w_got_y, w_got_z, w_got_e)
    red2 = [reduction(gw2_ref, slice(128 * n, 128 * n + 128), n, n, refs) for n in range(3)]
    red1 = [reduction(gw1_ref, slice(128 * n, 128 * n + 128), n + 3, n + 3, refs) for n in range(3)]
    refs = (gjo, o_core, o_got_x, o_own, o_got_y, o_got_z, o_got_e)
    red0 = reduction(go_ref, slice(0, channels), None, 6, refs)
    zs, extras = chips["z"], chips["e"]

    def small_row_copies(s):
        return [
            remote(v_own.at[s], v_row.at[s, k - 1], vs.at[s, k - 1], vr.at[s, k - 1], who[k])
            for k in (1, 2, 3)
        ]

    def small_y_copies(s):
        return [remote(v_one.at[s], v_y.at[s], vs.at[s, 3], vr.at[s, 3], chips["y"][0])]

    def small_z_copies(s):
        return [
            remote(v_two.at[s], v_z.at[s, n], vs.at[s, 4 + n], vr.at[s, 4 + n], at)
            for n, at in enumerate(zs)
        ]

    def small_e_copies(s):
        return [
            remote(v_three.at[s], v_e.at[s, n], vs.at[s, 7 + n], vr.at[s, 7 + n], at)
            for n, at in enumerate(extras)
        ]

    def small_row(s):
        v_own[s] = gs[...]
        start(small_row_copies(s))

    def small_y(s):
        arrived(small_row_copies(s))
        v_one[s] = v_own[s] + v_row[s, 0] + v_row[s, 1] + v_row[s, 2]
        start(small_y_copies(s))

    def small_z(s):
        arrived(small_y_copies(s))
        v_two[s] = v_one[s] + v_y[s]
        start(small_z_copies(s))

    def small_end(s):
        arrived(small_z_copies(s))
        v_three[s] = v_two[s] + v_z[s, 0] + v_z[s, 1] + v_z[s, 2]
        total = v_three[s]
        if extras:
            start(small_e_copies(s))
            arrived(small_e_copies(s))
            for n in range(len(extras)):
                total = total + v_e[s, n]
        gv_ref[s] = total

    def gather_row_copies():
        return [
            remote(mg, g_row.at[k - 1], gsem.at[k - 1], hsem.at[k - 1], who[k])
            for k in (1, 2, 3)
        ]

    def gather_copies():
        blocks = [pl.ds(i, 1), pl.ds(pl.multiple_of(i - lax.rem(i, 2), 2), 2)]
        blocks.append(pl.ds(pl.multiple_of(i - lax.rem(i, 8), 8), 8))
        found = []
        for rows, places in zip(blocks, (chips["y"], zs, extras)):
            for at in places:
                n = 3 + len(found)
                found.append(remote(gat.at[rows], gat.at[rows], gsem.at[n], hsem.at[n], at))
        return found

    def gather_row():
        start(gather_row_copies())

    def gather_y():
        arrived(gather_row_copies())
        gat[i] = emb[...] + mg[...] + g_row[0] + g_row[1] + g_row[2]
        start(gather_copies()[:1])

    def gather_z():
        arrived(gather_copies()[:1])
        start(gather_copies()[1:4])

    def gather_end():
        arrived(gather_copies()[1:4])
        start(gather_copies()[4:])
        arrived(gather_copies()[4:])

    def three_terms(v):
        a = v.astype(low_type)
        b = (v - a.astype(float_type)).astype(low_type)
        d = (v - a.astype(float_type) - b.astype(float_type)).astype(low_type)
        return jnp.concatenate([a, b, d], axis=0)

    def embedding():
        ge_ref[...] = jnp.zeros(ge_ref.shape, float_type)
        gc_ref[...] = jnp.zeros(gc_ref.shape, float_type)
        geo_ref[...] = jnp.zeros(geo_ref.shape, float_type)
        lax.fori_loop(0, gat.shape[0] // 8, embedding_part, 0)

    def embedding_part(part_of, _):
        every = 64
        full = gat[pl.ds(pl.multiple_of(part_of * 8, 8), 8)].reshape(every, 2 * channels)
        place_of = lax.rem(lax.broadcasted_iota(jnp.int32, (every, 2 * channels), 0), 8)
        live = place_of < images
        grad = jnp.where(live, full, 0.0)
        held = jnp.where(live, pltpu.roll(full, every - images, 0), 0.0)
        act = jnp.where(live, half_silu(held), 0.0).astype(low_type)
        left[...] = jnp.concatenate([act, act, act], axis=0).T
        terms = three_terms(grad)
        size = 2 * channels // 4
        own = pl.ds(pl.multiple_of(r * size, size), size)
        ge_ref[...] += jnp.dot(left[own, :], terms, preferred_element_type=float_type)
        geo_ref[...] += jnp.broadcast_to(jnp.sum(grad, axis=0, keepdims=True), geo_ref.shape)
        active = lax.dot_general(terms, ew[...], contract_cols, preferred_element_type=float_type)
        active = active[0:every] + active[every : 2 * every] + active[2 * every :]
        back = jnp.where(live, active * slope_of(held), 0.0)
        classes = gc_ref.shape[0]
        row_of = lax.rem(lax.broadcasted_iota(jnp.int32, (every, 128), 0), 8)
        label = jnp.full((every, 128), -1.0, float_type)
        for b in range(images):
            rolled = pltpu.roll(full[:, 256 * b : 256 * b + 128], every - 2 * images + b, 0)
            label = jnp.where(row_of == b, rolled, label)
        for n in range(hot.shape[0] // 128):
            kind = lax.broadcasted_iota(jnp.int32, (every, 128), 1) + 128 * n + r * classes
            hit = jnp.where(label == kind.astype(float_type), 1.0, 0.0).astype(low_type)
            hot[128 * n : 128 * (n + 1), :] = jnp.concatenate([hit, hit, hit], axis=0).T
        found = jnp.dot(hot[...], three_terms(back), preferred_element_type=float_type)
        gc_ref[...] += found[0:classes]
        return 0

    def embed_forward():
        row = lax.broadcasted_iota(jnp.int32, (8, 2 * channels), 0)
        lane_of = lax.broadcasted_iota(jnp.int32, (8, channels), 1).astype(float_type)

        def spread(ref, other):
            v = jnp.full((8, channels), other, float_type)
            for b in range(images):
                v = jnp.where(row[:, :channels] == b, ref[b].astype(float_type), v)
            return v

        position = (spread(index_ref, 0.0) + 1.0) / (spread(count_ref, 2.0) - 1.0)
        low_root = sigma_least ** (1.0 / sigma_power)
        high_root = sigma_most ** (1.0 / sigma_power)
        root = low_root + position * (high_root - low_root)
        square = root * root
        noise_time = 250.0 * jnp.log(square * square * square * root)
        angles = noise_time * jnp.exp(lane_of * (-math.log(10000.0) / channels))
        features = jnp.concatenate([jnp.cos(angles), jnp.sin(angles)], axis=1)
        count = ct.shape[0]
        label = spread(label_ref, -1.0)[:, 0:1]
        kinds = lax.broadcasted_iota(jnp.int32, (8, count), 1).astype(float_type)
        one_hot = jnp.where(label == kinds, 1.0, 0.0).astype(low_type)
        loads["ct"].wait()
        embedded = features + dot(one_hot, ct[...])
        live = row < images
        embed_act = half_silu(embedded).astype(low_type)
        loads["ew"].wait()
        offset = jnp.concatenate([vec(11), vec(12)], axis=1)
        mod[...] = dot(embed_act, ew[...]) + offset
        rows = pltpu.roll(jnp.where(live, embedded, 0.0), images, 0)
        part_of = lax.broadcasted_iota(jnp.int32, (8, 2 * channels), 1)
        marks = jnp.zeros((8, 2 * channels), float_type)
        for b in range(images):
            here = jnp.logical_and(row == 2 * images, part_of >= 256 * b)
            marks = jnp.where(here, label_ref[b].astype(float_type), marks)
        emb[...] = rows + marks

    at = 0
    for line in lines:
        v = line[...].astype(float_type).reshape(1, line.shape[0])
        for n in range(line.shape[0] // channels):
            vec_ref[at : at + 1] = v[:, n * channels : (n + 1) * channels]
            at += 1
    ones[...] = block_ones(channels, channels // GROUPS)
    gs[...] = jnp.zeros(gs.shape, float_type)
    mg[...] = jnp.zeros(mg.shape, float_type)

    def clear(n, _):
        for m in range(4):
            gw[n, m, quarter:padded] = jnp.zeros((padded - quarter, 128), low_type)
        return 0

    lax.fori_loop(0, 6, clear, 0)

    @each_image
    def _(b):
        v = x_ref[b].astype(float_type)
        fill_message(0, b, col_sum(v), col_sum(v * v), lambda at: x_ref[b, pl.ds(at, width)])
        none = jnp.zeros((1, channels), float_type)
        fill_message(6, b, none, none, lambda at: cot_ref[b, pl.ds(at, width)])

    embed_forward()
    pl.semaphore_wait(barrier, len(greeted))

    @each_image
    def _(b):
        start(copies(0, b))

    @each_image
    def _(b):
        start(copies(6, b))

    loads["ow"].wait()

    @each_image
    def _(b):
        d_out_t[b] = dot_nt(cot_ref[b], ow[...]).T.astype(low_type)

    loads["w1"].wait()

    @each_image
    def _(b):
        centre, scaled = receive_scale(0, b)
        slope = scaled * vec(0)
        shift = vec(1)

        def activate(v):
            return half_silu((v - centre) * slope + shift)

        for row in range(rows_in):
            v = activate(x_ref[b, row * width : (row + 1) * width].astype(float_type))
            fill_row(abuf, (row + 1) * width, v, channels, width)
        fill_halo(abuf, lambda k: activate(far_rows(0, b, k)))
        hidden = convolve(w1) + vec(2)
        hid[b] = hidden
        send(
            1, b, col_sum(hidden), col_sum(hidden * hidden),
            lambda at: hid[b, pl.ds(at, width)],
        )
        own = pl.ds(pl.multiple_of(b * pixels, pixels), pixels)
        act1_t[:, own] = abuf[width : width + pixels, channels : 2 * channels].T

    def block(n):
        return pl.ds(pl.multiple_of(n * pixels, pixels), pixels)

    mate = r + 1 - 2 * c
    across = lax.rem(r + 2, 4)

    def gather(b, n, rows):
        return remote(
            att.at[b, rows], att.at[b, rows], gsend.at[b, n], grecv.at[b, n], who[(1, 2, 1)[n]]
        )

    def shares(b):
        return [gather(b, n, block(rows)) for n, rows in enumerate((r, r, across))]

    def arrivals(b):
        rows = (mate, across, lax.rem(mate + 2, 4))
        return [gather(b, n, block(w)) for n, w in enumerate(rows)]

    def share(b):
        centre, scaled = receive_scale(2, b)
        slope = scaled * vec(6)
        att[b, block(r)] = ((mid[b] - centre) * slope + vec(7)).astype(low_type)
        start(shares(b)[:2])

    loads["w2"].wait()
    loads["jw"].wait()

    @each_image
    def _(b):
        @pl.when(b == images - 1)
        def _():
            share(0)

        centre, scaled = receive_scale(1, b)
        grow = 1.0 + mod[pl.ds(b, 1), 0:channels]
        slope = scaled * vec(3) * grow
        shift = vec(4) * grow + mod[pl.ds(b, 1), channels:]

        def activate(v):
            return half_silu((v - centre) * slope + shift)

        for row in range(rows_in):
            v = activate(hid[b, row * width : (row + 1) * width])
            fill_row(abuf, (row + 1) * width, v, channels, width)
        fill_halo(abuf, lambda k: activate(far_rows(1, b, k)))
        middle = (convolve(w2) + vec(5) + x_ref[b].astype(float_type)) * half
        mid[b] = middle
        send(
            2, b, col_sum(middle), col_sum(middle * middle),
            lambda at: mid[b, pl.ds(at, width)],
        )
        own = pl.ds(pl.multiple_of(b * pixels, pixels), pixels)
        act2_t[:, own] = abuf[width : width + pixels, channels : 2 * channels].T

    part = att

    def forward(b):
        arrivals(b)[1].wait_recv()
        shares(b)[2].start()

    def sums_core(b):
        return [
            remote(
                part.at[b, block(2 * n + 1 - c)], got_core.at[b, n], asem.at[b, n],
                bsem.at[b, n], who[1],
            )
            for n in range(2)
        ]

    def sum_x(b):
        far = block(2 * (1 - lax.div(r, 2)) + c)
        return remote(part.at[b, far], got_x.at[b], asem.at[b, 2], bsem.at[b, 2], who[2])

    def pass_on(b):
        x = lax.div(r, 2)
        arrived(sums_core(b))
        far = 1 - x
        rows = block(2 * far + c)
        part[b, rows] = (
            part[b, rows].astype(float_type) + got_core[b, far].astype(float_type)
        ).astype(low_type)
        sum_x(b).start()
        ag[b] = part[b, block(r)].astype(float_type) + got_core[b, x].astype(float_type)

    def queries(b):
        q = (dot(att[b, block(r)], jw[:, :channels]) + vec(8)).astype(low_type)
        q8[b] = (q.astype(float_type) * HEAD ** (-0.5)).astype(low_type)

    some_images(share, 1, images)
    each_image(queries)
    lane = lax.broadcasted_iota(jnp.int32, (pixels, pair_lanes), 1)

    def masked(v):
        return jnp.concatenate(
            [jnp.where(lane < HEAD, v, 0.0), jnp.where(lane >= HEAD, v, 0.0)], axis=0
        ).astype(low_type)

    q_sum[...] = jnp.zeros(q_sum.shape, float_type)
    kv_sum[...] = jnp.zeros(kv_sum.shape, float_type)
    o_sum[...] = jnp.zeros(o_sum.shape, float_type)
    att_t[channels:] = jnp.ones((16, whole), low_type)
    forward(0)

    @each_image
    def _(b):
        a = arrivals(b)
        a[0].wait_recv()
        a[2].wait_recv()
        bias = jnp.concatenate([jnp.zeros((1, channels), float_type), vec(9)], axis=1)
        for n in range(4):
            rows = pl.ds(n * pixels, pixels)
            kv[rows] = (dot(att[b, rows], jw[:, channels:]) + bias).astype(low_type)
        for n in range(2 * channels // 128):
            cols = pl.ds(n * 128, 128)
            kv_t[cols, :] = kv[:, cols].T

        @pl.when(b > 0)
        def _():
            pass_on(b - 1)

        def one_pair(t, _):
            lanes = pl.ds(pl.multiple_of(t * pair_lanes, pair_lanes), pair_lanes)
            v_lanes = pl.ds(pl.multiple_of(channels + t * pair_lanes, pair_lanes), pair_lanes)
            qm[...] = masked(q8[b, :, lanes].astype(float_type))
            peak = None
            for n in range(whole // chunk):
                rows = pl.ds(n * chunk, chunk)
                s = dot_nt(kv[rows, lanes], qm[...])
                s_ref[rows] = s
                top = jnp.max(s.reshape(chunk // 8, 8, 2 * pixels), axis=0)
                peak = top if peak is None else jnp.maximum(peak, top)
            peak = jnp.max(peak, axis=0, keepdims=True)
            total = None
            for n in range(whole // chunk):
                rows = pl.ds(n * chunk, chunk)
                e = jnp.exp(s_ref[rows] - peak)
                eb[rows] = e.astype(low_type)
                more = jnp.sum(e.reshape(chunk // 8, 8, 2 * pixels), axis=0)
                total = more if total is None else total + more
            over = 1.0 / jnp.sum(total, axis=0, keepdims=True)
            inner_of, scaled = [], []
            for j in range(2):
                head = pl.ds(pl.multiple_of(t * pair_lanes + j * HEAD, HEAD), HEAD)
                v_head = pl.ds(pl.multiple_of(channels + t * pair_lanes + j * HEAD, HEAD), HEAD)
                cols = slice(j * pixels, (j + 1) * pixels)
                mt = dot(kv_t[v_head, :], eb[:, cols]) * over[:, cols]
                mix_t[head] = mt.astype(low_type)
                g = (d_out_t[b, head].astype(float_type) * over[:, cols]).astype(low_type).astype(float_type)
                inner_of.append(col_sum(g * mt))
                scaled.append(g)
            inner_of = jnp.concatenate(inner_of, axis=1)
            dom[...] = masked(jnp.concatenate(scaled, axis=0).T)
            for n in range(whole // chunk):
                rows = pl.ds(n * chunk, chunk)
                dp = dot_nt(kv[rows, v_lanes], dom[...])
                dsb[rows] = (eb[rows].astype(float_type) * (dp - inner_of)).astype(low_type)
            for j in range(2):
                head = pl.ds(pl.multiple_of(t * pair_lanes + j * HEAD, HEAD), HEAD)
                cols = slice(j * pixels, (j + 1) * pixels)
                dq_t[head] = dot(kv_t[head, :], dsb[:, cols]) * HEAD ** (-0.5)
            dkv[:, lanes] = dot(dsb[...], qm[...]).astype(low_type)
            dkv[:, v_lanes] = dot(eb[...], dom[...]).astype(low_type)
            return 0

        lax.fori_loop(0, pairs, one_pair, 0)

        @pl.when(b + 1 < images)
        def _():
            forward(b + 1)

        dq[...] = dq_t[...].T.astype(low_type)
        att_t[0:channels] = att[b].T
        for cp in shares(b):
            cp.wait_send()
        for n in range(4):
            rows = pl.ds(n * pixels, pixels)
            part[b, rows] = dot_nt(dkv[rows], jw[:, channels:]).astype(low_type)
        part[b, block(r)] = (
            part[b, block(r)].astype(float_type) + dot_nt(dq[...], jw[:, :channels])
        ).astype(low_type)
        start(sums_core(b))
        q_sum[...] += dot(att_t[:, block(r)], dq[...])
        kv_sum[...] += dot(att_t[...], dkv[...])
        o_sum[...] += dot(mix_t[...], cot_ref[b])
        mixed = mix_t[...].T
        res_ref[b] = (mid[b] + dot(mixed, ow[...]) + vec(10)).astype(low_type)

    def pack_weights():
        part_rows = channels // 4
        every = (q_sum[0:channels], kv_sum[0:channels, :channels], kv_sum[0:channels, channels:], o_sum[...])
        for n, v in enumerate(every):
            for m in range(4):
                gjo[m, n * part_rows : (n + 1) * part_rows] = v[
                    m * part_rows : (m + 1) * part_rows
                ].astype(low_type)
        gs[8:9] = q_sum[channels : channels + 1]
        gs[9:10] = kv_sum[channels : channels + 1, channels:]
        gs[10:11] = col_sum(jnp.sum(cot_ref[...].astype(float_type), axis=0))

    def attend_sums(b):
        sum_x(b).wait_recv()
        u = ag[b] + got_x[b].astype(float_type)
        ag[b] = u
        first = col_sum(u)
        second = col_sum(u * ((mid[b] - st[b, 4:5]) * st[b, 5:6]))
        gs[6:7] += second
        gs[7:8] += first
        send(3, b, first * vec(6), second * vec(6), lambda at: ag[b, pl.ds(at, width)])

    def branch_grad(b):
        first, second = receive(3, b)
        arrived(copies(6, b))
        centre, scaled = st[b, 4:5], st[b, 5:6]

        def grad_of(cot, u, v):
            return (cot + scaled * (u * vec(6) - first - (v - centre) * scaled * second)) * half

        total = jnp.zeros((1, channels), float_type)
        for row in range(rows_in):
            rows = pl.ds(row * width, width)
            v = grad_of(cot_ref[b, rows].astype(float_type), ag[b, rows], mid[b, rows])
            ag[b, rows] = v
            v = v.astype(low_type).astype(float_type)
            fill_row(grad.at[b], (row + 1) * width, v, channels, width)
            total += col_sum(v)
        gs[5:6] += total
        fill_halo(
            grad.at[b],
            lambda k: grad_of(far_rows(6, b, k), far_rows(3, b, k), far_rows(2, b, k)),
        )

    def branch_back(b):
        upstream = data_grad(grad, b, w2)
        grow = 1.0 + mod[pl.ds(b, 1), 0:channels]
        normed = (hid[b] - st[b, 2:3]) * st[b, 3:4]
        pre = (normed * vec(3) + vec(4)) * grow + mod[pl.ds(b, 1), channels:]
        v = upstream * slope_of(pre)
        slope_grad[b] = v
        first, second = col_sum(v), col_sum(v * normed)
        mg[pl.ds(b, 1), 0:channels] = vec(3) * second + vec(4) * first
        mg[pl.ds(b, 1), channels:] = first
        first, second = grow * first, grow * second
        gs[3:4] += second
        gs[4:5] += first
        send(
            4, b, first * vec(3), second * vec(3),
            lambda at: slope_grad[b, pl.ds(at, width)],
        )

    def hidden_grad(b):
        first, second = receive(4, b)
        centre, scaled = st[b, 2:3], st[b, 3:4]
        gain = (1.0 + mod[pl.ds(b, 1), 0:channels]) * vec(3)

        def grad_of(u, v):
            return scaled * (u * gain - first - (v - centre) * scaled * second)

        total = jnp.zeros((1, channels), float_type)
        for row in range(rows_in):
            rows = pl.ds(row * width, width)
            v = grad_of(slope_grad[b, rows], hid[b, rows]).astype(low_type).astype(float_type)
            fill_row(grad.at[b], (row + 1) * width, v, channels, width)
            total += col_sum(v)
        gs[2:3] += total
        fill_halo(grad.at[b], lambda k: grad_of(far_rows(4, b, k), far_rows(1, b, k)))

    def hidden_back(b):
        upstream = data_grad(grad, b, w1)
        normed = (x_ref[b].astype(float_type) - st[b, 0:1]) * st[b, 1:2]
        v = upstream * slope_of(normed * vec(0) + vec(1))
        slope_grad[b] = v
        first, second = col_sum(v), col_sum(v * normed)
        gs[0:1] += second
        gs[1:2] += first
        send(5, b, first * vec(0), second * vec(0))

    def images_grad(b):
        first, second = receive(5, b)
        scaled = st[b, 1:2]
        normed = (x_ref[b].astype(float_type) - st[b, 0:1]) * scaled
        gx_ref[b] = ag[b] + scaled * (slope_grad[b] * vec(0) - first - normed * second)

    pass_on(images - 1)
    some_images(attend_sums, 0, images - 1)
    pack_weights()
    red0.core()
    some_images(attend_sums, images - 1, images)
    red0.across_x()
    some_images(branch_grad, 0, images - 1)
    some_images(branch_back, 0, images - 1)
    some_images(branch_grad, images - 1, images)
    kernel_grad(act2_t, grad, 0)
    red2[1].core()
    some_images(branch_back, images - 1, images)
    small_row(0)
    gather_row()
    red0.across_y()
    some_images(hidden_grad, 0, images - 1)
    red2[1].across_x()
    red2[0].core()
    red2[2].core()
    some_images(hidden_grad, images - 1, images)
    red2[0].across_x()
    kernel_grad(act1_t, grad, 3)
    red0.across_z()
    small_y(0)
    gather_y()
    red1[1].core()
    red2[2].across_x()
    red1[0].core()
    red1[2].core()
    some_images(hidden_back, 0, images - 1)
    red1[0].across_x()
    red1[1].across_x()
    red2[1].across_y()
    some_images(hidden_back, images - 1, images)
    red1[2].across_x()
    small_z(0)
    gather_z()
    small_row(1)
    red0.back_z()
    red2[0].across_y()
    red2[1].across_z()
    small_end(0)
    gather_end()
    embedding()
    red2[2].across_y()
    red0.back_y()
    red2[0].across_z()
    red2[1].back_z()
    red2[2].across_z()
    red1[0].across_y()
    red2[0].back_z()
    red2[1].back_y()
    red0.end()
    red1[1].across_y()
    red2[2].back_z()
    each_image(images_grad)
    red1[0].across_z()
    red2[0].back_y()
    red2[1].end()
    red1[2].across_y()
    red1[1].across_z()
    red2[2].back_y()
    small_y(1)
    red2[0].end()
    red1[0].back_z()
    red1[2].across_z()
    red1[1].back_z()
    red2[2].end()
    red1[0].back_y()
    small_z(1)
    red1[2].back_z()
    red1[1].back_y()
    red1[0].end()
    small_end(1)
    red1[2].back_y()
    red1[1].end()
    red1[2].end()

    @each_image
    def _(b):
        sent = sums_core(b) + [sum_x(b)]
        for p in range(7):
            sent += copies(p, b)
        for cp in sent:
            cp.wait_send()

    for red in [red0] + red1 + red2:
        red.drain()
    for s in range(2):
        for cp in small_row_copies(s) + small_y_copies(s) + small_z_copies(s) + small_e_copies(s):
            cp.wait_send()
    for cp in gather_row_copies() + gather_copies():
        cp.wait_send()


def block_call(x, cot, lines, scalars, w1, w2, jw, ow, ew, ct):
    images, pixels, channels = x.shape
    span = pixels + 64
    whole = 4 * pixels
    padded = -(-9 * channels // 4 // 128) * 128
    every = lax.axis_size("img")
    more = every // 8
    some = max(more - 1, 1)
    classes = ct.shape[0]
    vm = pl.BlockSpec(memory_space=pltpu.VMEM)
    hbm = pl.BlockSpec(memory_space=pl.ANY)

    def low(*shape):
        return pltpu.VMEM(shape, low_type)

    def wide(*shape):
        return pltpu.VMEM(shape, float_type)

    def dma(*shape):
        return pltpu.SemaphoreType.DMA(shape)

    def out(*shape, kind=float_type):
        return jax.ShapeDtypeStruct(shape, kind)

    return pl.pallas_call(
        block_kernel,
        out_shape=(
            out(*x.shape, kind=low_type), out(*x.shape), out(padded, channels, kind=low_type),
            out(padded, channels, kind=low_type), out(channels, channels, kind=low_type),
            out(2, 16, channels), out(2 * channels // 4, 2 * channels),
            out(classes // 4, 2 * channels), out(8, 2 * channels),
        ),
        in_specs=[vm] * (2 + len(lines)) + [pl.BlockSpec(memory_space=pltpu.SMEM)] * 3 + [hbm] * 6,
        out_specs=(vm,) * 9,
        scratch_shapes=[
            low(*w1.shape), low(*w2.shape), low(*jw.shape), low(*ow.shape), low(*ew.shape),
            low(*ct.shape), low(channels, channels), wide(*x.shape), wide(*x.shape),
            wide(8, 2 * channels), wide(8, 2 * channels),
            low(channels, images * pixels), low(channels, images * pixels),
            wide(images, 8, channels), low(7, images, 48, channels), low(7, images, 48, channels),
            low(7, images, 3, 48, channels),
            low(images, whole, channels), low(channels + 16, whole), low(whole, 2 * channels),
            low(2 * channels, whole), low(*x.shape), low(images, channels, pixels),
            low(2 * pixels, 2 * HEAD), low(2 * pixels, 2 * HEAD), wide(whole, 2 * pixels),
            low(whole, 2 * pixels), low(whole, 2 * pixels), low(channels, pixels),
            wide(channels, pixels), low(pixels, channels), low(whole, 2 * channels),
            low(images, 2, pixels, channels), low(*x.shape), wide(*x.shape),
            wide(channels + 16, channels),
            wide(channels + 16, 2 * channels), wide(channels, channels), low(4, channels, channels),
            low(images, span, 3 * channels), wide(*x.shape), wide(16, channels), wide(8, 2 * channels),
            low(6, 4, padded, 128), low(6, 2, padded, 128), low(6, padded, 128),
            wide(6, padded // 2, 128), low(6, padded // 2, 128), low(6, 3, padded // 8, 128),
            low(6, some, padded // 8, 128),
            low(2, channels, channels), low(channels, channels), wide(channels // 2, channels),
            low(channels // 2, channels), low(3, channels // 8, channels),
            low(some, channels // 8, channels),
            wide(2, 16, channels), wide(2, 3, 16, channels), wide(2, 16, channels),
            wide(2, 16, channels), wide(2, 16, channels), wide(2, 3, 16, channels),
            wide(2, 16, channels), wide(2, some, 16, channels), wide(3, 8, 2 * channels),
            wide(every, 8, 2 * channels), low(2 * channels, 192), low(256, 192), wide(16, channels), wide(8, 2 * channels),
            dma(6), dma(7, images, 3), dma(7, images, 3), dma(images, 3), dma(images, 3),
            dma(images, 3), dma(images, 3), dma(7, 11), dma(7, 11), dma(7, some), dma(7, some),
            dma(2, 6 + more), dma(2, 6 + more), dma(6 + more), dma(6 + more),
        ],
        compiler_params=pltpu.CompilerParams(
            collective_id=0, has_side_effects=True, vmem_limit_bytes=62 << 20
        ),
        name="block",
    )(x, cot, *lines, *scalars, w1, w2, jw, ow, ew, ct)


def finish_kernel(
    res, gx, gw1, gw2, go, gv, ge, gc, geo,
    res_out, gx_out, first_gain, first_shift, first_kernel, first_offset, embed_weight,
    embed_offset, class_table, second_gain, second_shift, second_kernel, second_offset,
    third_gain, third_shift, joint_weight, joint_offset, output_weight, output_offset, sems,
):
    r = lax.axis_index("row")
    moves = [
        pltpu.make_async_copy(src, dst, sems.at[n])
        for n, (src, dst) in enumerate(
            ((res, res_out), (gx, gx_out), (ge, embed_weight), (gc, class_table))
        )
    ]
    for cp in moves:
        cp.start()
    first_kernel[...] = gw1[0 : first_kernel.shape[0]].astype(float_type)
    second_kernel[...] = gw2[0 : second_kernel.shape[0]].astype(float_type)
    rows, channels = output_weight.shape
    for n in range(3):
        joint_weight[:, n * channels : (n + 1) * channels] = go[n * rows : (n + 1) * rows].astype(
            float_type
        )
    output_weight[...] = go[3 * rows :].astype(float_type)

    def own(v, size, place):
        width = v.shape[1]
        return pltpu.roll(v, lax.rem(width - place * size, width), 1)

    late = own(gv[1], rows, r)
    early = own(gv[0], rows, r)
    for n, ref in enumerate((first_gain, first_shift, first_offset)):
        ref[...] = late[n, 0:rows]
    for n, ref in (
        (3, second_gain), (4, second_shift), (5, second_offset), (6, third_gain),
        (7, third_shift), (10, output_offset),
    ):
        ref[...] = early[n, 0:rows]
    pair = own(gv[0], 2 * rows, lax.rem(r, 2))
    joint_offset[...] = jnp.where(r < 2, pair[8:9, 0 : 2 * rows], pair[9:10, 0 : 2 * rows]).reshape(
        2 * rows
    )
    embed_offset[...] = own(geo[...], 2 * rows, r)[0, 0 : 2 * rows]
    for cp in moves:
        cp.wait()


def finish_call(res, gx, gw1, gw2, go, gv, ge, gc, geo):
    channels = go.shape[0]
    rows = channels // 4
    vm = pl.BlockSpec(memory_space=pltpu.VMEM)
    hbm = pl.BlockSpec(memory_space=pl.ANY)

    def out(*shape, kind=float_type):
        return jax.ShapeDtypeStruct(shape, kind)

    kernel = out(9 * rows, channels)
    line = out(rows)
    return pl.pallas_call(
        finish_kernel,
        out_shape=(
            out(*res.shape, kind=low_type), out(*gx.shape), line, line, kernel, line,
            out(*ge.shape), out(2 * rows), out(*gc.shape), line, line, kernel, line, line, line,
            out(rows, 3 * channels), out(2 * rows), out(rows, channels), line,
        ),
        in_specs=[hbm, hbm, vm, vm, vm, vm, hbm, hbm, vm],
        out_specs=(hbm, hbm, vm, vm, vm, vm, hbm, vm, hbm) + (vm,) * 10,
        scratch_shapes=[pltpu.SemaphoreType.DMA((4,))],
        compiler_params=pltpu.CompilerParams(vmem_limit_bytes=32 << 20),
        name="finish",
    )(res, gx, gw1, gw2, go, gv, ge, gc, geo)


def shards(
    images,
    level_count,
    level_index,
    labels,
    first_gain,
    first_shift,
    first_kernel,
    first_offset,
    embed_weight,
    embed_offset,
    class_table,
    second_gain,
    second_shift,
    second_kernel,
    second_offset,
    third_gain,
    third_shift,
    joint_weight,
    joint_offset,
    output_weight,
    output_offset,
    cotangent,
):
    image_count, stripe_rows, image_width, channels = images.shape
    pixels = stripe_rows * image_width
    x = images.reshape(image_count, pixels, channels)
    cot = cotangent.reshape(image_count, pixels, channels)
    lines = (
        first_gain, first_shift, first_offset, second_gain, second_shift, second_offset,
        third_gain, third_shift, joint_offset, output_offset, embed_offset,
    )
    found = block_call(
        x, cot, lines, (level_count, level_index, labels), first_kernel, second_kernel,
        joint_weight, output_weight, embed_weight, class_table,
    )
    outs = finish_call(*found)
    return (outs[0].reshape(images.shape), outs[1].reshape(images.shape)) + tuple(outs[2:])


def solution(mesh):
    in_specs = (
        (P("img", "row", None, None),) + (P("img"),) * 3 + (P(),) * 17
        + (P("img", "row", None, None),)
    )
    row, rows = P("row"), P("row", None)
    out_specs = (
        P("img", "row", None, None), P("img", "row", None, None), row, row, rows, row, rows, row,
        rows, row, row, rows, row, row, row, rows, row, rows, row,
    )
    return jax.shard_map(shards, mesh=mesh, in_specs=in_specs, out_specs=out_specs, check_vma=False)
```

```python
import math

import jax
import jax.numpy as jnp
from jax import lax
from jax.experimental import pallas as pl
from jax.experimental.pallas import tpu as pltpu
from jax.sharding import PartitionSpec as P

GROUPS = 32
HEAD = 64
MESH = pl.DeviceIdType.MESH

norm_eps = 1e-05
sigma_least = 0.002
sigma_most = 80.0
sigma_power = 7.0
float_type = jnp.float32
low_type = jnp.bfloat16
contract_cols = (((1,), (1,)), ((), ()))


def peers():
    i = lax.axis_index("img")
    r = lax.axis_index("row")
    c = lax.rem(r, 2)
    near = r + 1 - 2 * c
    return (i, r, c, {1: (i, near), 2: (i, lax.rem(r + 2, 4)), 3: (i, 3 - r)})


def half_silu(v):
    h = 0.5 * v
    return h * jnp.tanh(h) + h


def fill_row(buf, start, act, channels, width):
    col = lax.broadcasted_iota(jnp.int32, (width, channels), 0)
    left = jnp.where(col == 0, 0.0, pltpu.roll(act, 1, 0))
    right = jnp.where(col == width - 1, 0.0, pltpu.roll(act, width - 1, 0))
    rows = pl.ds(start, width)
    buf[rows, 0:channels] = left.astype(low_type)
    buf[rows, channels : 2 * channels] = act.astype(low_type)
    buf[rows, 2 * channels : 3 * channels] = right.astype(low_type)


def pack_stats(first, second):
    channels = first.shape[1]
    row = lax.broadcasted_iota(jnp.int32, (8, channels), 0)

    def terms(v):
        a = v.astype(low_type).astype(float_type)
        b = (v - a).astype(low_type).astype(float_type)
        c = v - a - b
        return jnp.where(row == 0, a, jnp.where(row == 1, b, jnp.where(row == 2, c, 0.0)))

    return jnp.concatenate([terms(first), terms(second)], axis=0).astype(low_type)


def block_ones(channels, per):
    a = lax.broadcasted_iota(jnp.int32, (channels, channels), 0)
    b = lax.broadcasted_iota(jnp.int32, (channels, channels), 1)
    a = lax.shift_right_logical(a * 43691, 19)
    b = lax.shift_right_logical(b * 43691, 19)
    return jnp.where(a == b, 1.0, 0.0).astype(low_type)


def combine_stats(parts, ones, entries):
    total = jnp.dot(jnp.concatenate(parts, axis=0), ones, preferred_element_type=float_type)
    first = total[0:8] + total[16:24] + total[32:40] + total[48:56]
    second = total[8:16] + total[24:32] + total[40:48] + total[56:64]
    first = jnp.sum(first, axis=0, keepdims=True) * (1.0 / entries)
    second = jnp.sum(second, axis=0, keepdims=True) * (1.0 / entries)
    return first, second


def chip_peers(i, r):
    size = lax.axis_size("img")
    z = lax.rem(lax.div(i, 2), 4)
    e = lax.div(i, 8)
    others = (z + 1 - 2 * lax.rem(z, 2), lax.rem(z + 2, 4), 3 - z)
    more = size // 8
    return {
        "y": [(i + 1 - 2 * lax.rem(i, 2), r)],
        "z": [(i + 2 * (n - z), r) for n in others],
        "e": [(i + 8 * (lax.rem(e + k, more) - e), r) for k in range(1, more)],
        "at": (lax.rem(i, 2), z),
        "pieces": others,
    }


class Reduction:
    def __init__(self, out, lanes, n, q, refs, who, place, cs, cr, es, er):
        if n is not None:
            refs = (refs[0].at[n],) + tuple(ref.at[n] for ref in refs[1:])
        self.grad, self.got_core, self.got_x, self.own, self.got_y, self.got_z, self.got_e = refs
        self.out, self.lanes, self.q, self.who = out, lanes, q, who
        self.c, self.x, self.chips = place
        self.y, self.z = self.chips["at"]
        self.sems = (cs, cr, es, er)
        self.size = self.got_x.shape[0]

    def copy(self, src, dst, n, at, extra=False):
        send, recv = self.sems[2:] if extra else self.sems[:2]
        return pltpu.make_async_remote_copy(
            src, dst, send.at[self.q, n], recv.at[self.q, n], device_id=at, device_id_type=MESH
        )

    def half(self, y):
        size = self.size // 2
        return pl.ds(pl.multiple_of(y * size, size), size)

    def piece(self, z, y=0):
        size = self.size // 8
        return pl.ds(pl.multiple_of(y * (self.size // 2) + z * size, size), size)

    def core_copies(self):
        return [
            self.copy(self.grad.at[2 * n + 1 - self.c], self.got_core.at[n], n, self.who[1])
            for n in range(2)
        ]

    def x_copies(self):
        return [self.copy(self.grad.at[2 * (1 - self.x) + self.c], self.got_x, 2, self.who[2])]

    def y_copies(self):
        return [self.copy(self.got_x.at[self.half(1 - self.y)], self.got_y, 3, self.chips["y"][0])]

    def z_copies(self):
        return [
            self.copy(self.got_x.at[self.piece(p, self.y)], self.got_z.at[n], 4 + n, at)
            for n, (p, at) in enumerate(zip(self.chips["pieces"], self.chips["z"]))
        ]

    def extra_copies(self):
        src = self.got_x.at[self.piece(self.z, self.y)]
        return [
            self.copy(src, self.got_e.at[n], n, at, True) for n, at in enumerate(self.chips["e"])
        ]

    def back_z_copies(self):
        part = self.out.at[self.piece(self.z, self.y), self.lanes]
        return [self.copy(part, part, 7 + n, at) for n, at in enumerate(self.chips["z"])]

    def back_y_copies(self):
        part = self.out.at[self.half(self.y), self.lanes]
        return [self.copy(part, part, 10, self.chips["y"][0])]

    def core(self):
        for cp in self.core_copies():
            cp.start()

    def across_x(self):
        for cp in self.core_copies():
            cp.wait_recv()
        far = 1 - self.x
        block = 2 * far + self.c
        self.grad[block] = (
            self.grad[block].astype(float_type) + self.got_core[far].astype(float_type)
        ).astype(low_type)
        self.x_copies()[0].start()

    def chip_sum(self, rows):
        return (
            self.grad[2 * self.x + self.c, rows].astype(float_type)
            + self.got_core[self.x, rows].astype(float_type)
            + self.got_x[rows].astype(float_type)
        )

    def across_y(self):
        self.x_copies()[0].wait_recv()
        rows = self.half(1 - self.y)
        self.got_x[rows] = self.chip_sum(rows).astype(low_type)
        self.y_copies()[0].start()
        self.own[...] = self.chip_sum(self.half(self.y))

    def across_z(self):
        self.y_copies()[0].wait_recv()
        v = self.own[...] + self.got_y[...].astype(float_type)
        self.own[...] = v
        self.got_x[self.half(self.y)] = v.astype(low_type)
        for cp in self.z_copies():
            cp.start()

    def back_z(self):
        for cp in self.z_copies():
            cp.wait_recv()
        v = self.own[self.piece(self.z)]
        for n in range(3):
            v = v + self.got_z[n].astype(float_type)
        if self.chips["e"]:
            self.got_x[self.piece(self.z, self.y)] = v.astype(low_type)
            for cp in self.extra_copies():
                cp.start()
            for n, cp in enumerate(self.extra_copies()):
                cp.wait_recv()
                v = v + self.got_e[n].astype(float_type)
        self.out[self.piece(self.z, self.y), self.lanes] = v.astype(low_type)
        for cp in self.back_z_copies():
            cp.start()

    def back_y(self):
        for cp in self.back_z_copies():
            cp.wait_recv()
        self.back_y_copies()[0].start()

    def end(self):
        self.back_y_copies()[0].wait_recv()

    def drain(self):
        for cp in (
            self.core_copies() + self.x_copies() + self.y_copies() + self.z_copies()
            + self.extra_copies() + self.back_z_copies() + self.back_y_copies()
        ):
            cp.wait_send()


def out_rows(pixels, channels, classes):
    def laid(sizes):
        found, at = {}, 0
        for name, size in sizes:
            found[name] = (at, size)
            at += size
        return found

    padded = -(-9 * channels // 4 // 128) * 128
    rows = -(-classes // 4 // 16) * 16
    low_at = laid((("result", pixels), ("w1", padded), ("w2", padded), ("jo", channels)))
    wide_at = laid((
        ("images", pixels), ("lines", 32), ("embed", channels), ("classes", 2 * rows),
        ("offset", 16),
    ))
    return low_at, wide_at


def block_kernel(
    x_ref, cot_ref, *rest,
):
    lines, rest = rest[:11], rest[11:]
    count_ref, index_ref, label_ref = rest[:3]
    (w1_any, w2_any, jw_any, ow_any, ew_any, ct_any,
    low_out, wide_out,
    w1, w2, jw, ow, ew, ct, ones, hid, mid, mod, emb, act1_t, act2_t, st, m1, m3, got,
    att, att_t, kv, kv_t, q8, d_out_t, qm, dom, s_ref, eb, dsb, mix_t, dq_t, dq, dkv,
    got_core, to_x, got_x, ag, q_sum, kv_sum, o_sum, gjo,
    grad, slope_grad, gs, mg,
    gw, w_core, w_got_x, w_own, w_got_y, w_got_z, w_got_e,
    o_core, o_got_x, o_own, o_got_y, o_got_z, o_got_e,
    v_own, v_row, v_one, v_y, v_two, v_z, v_three, v_e, g_row, gat, left, hot,
    vec_ref, prep_ref, wsem, ssem, rsem, gsend, grecv, asem, bsem, cs, cr, es, er, vs, vr, gsem,
    hsem) = rest[3:]
    images, pixels, channels = x_ref.shape
    width = 32
    edge = pixels - width
    rows_in = pixels // width
    whole = 4 * pixels
    entries = float(whole * (channels // GROUPS))
    half = math.sqrt(0.5)
    quarter = 9 * channels // 4
    padded = gw.shape[2]
    chunk = 128
    pair_lanes = 2 * HEAD
    pairs = channels // pair_lanes
    i, r, c, who = peers()
    chips = chip_peers(i, r)
    place = (c, lax.div(r, 2), chips)
    inner = pl.multiple_of(edge * (1 - c), width)
    outer = pl.multiple_of(edge * c, width)
    inner_halo = pl.multiple_of((pixels + width) * (1 - c), width)
    outer_halo = pl.multiple_of((pixels + width) * c, width)
    outer_live = jnp.logical_and(r > 0, r < 3)
    loads = {
        name: pltpu.make_async_copy(src, dst, wsem.at[n])
        for n, (name, src, dst) in enumerate((
            ("ct", ct_any, ct), ("ew", ew_any, ew), ("w1", w1_any, w1), ("w2", w2_any, w2),
            ("jw", jw_any, jw), ("ow", ow_any, ow),
        ))
    }
    for cp in loads.values():
        cp.start()
    barrier = pltpu.get_barrier_semaphore()
    greeted = list(who.values()) + chips["y"] + chips["z"] + chips["e"]
    for at in greeted:
        pl.semaphore_signal(barrier, inc=1, device_id=at, device_id_type=MESH)

    abuf = grad.at[0]
    low_at, wide_at = out_rows(images * pixels, channels, ct.shape[0])
    gw1_ref, gw2_ref, go_ref = (low_out.at[pl.ds(*low_at[n])] for n in ("w1", "w2", "jo"))
    gv_ref, ge_ref, gc_ref, geo_ref = (
        wide_out.at[pl.ds(*wide_at[n])] for n in ("lines", "embed", "classes", "offset")
    )

    def dot(a, b):
        return jnp.dot(a, b, preferred_element_type=float_type)

    def dot_nt(a, b):
        return lax.dot_general(a, b, contract_cols, preferred_element_type=float_type)

    def vec(n):
        return vec_ref[n : n + 1, :]

    def col_sum(v):
        return jnp.sum(v, axis=0, keepdims=True)

    def slope_of(pre):
        s = 0.5 * jnp.tanh(0.5 * pre) + 0.5
        return s * (1.0 + pre * (1.0 - s))

    def remote(src, dst, send, recv, at):
        return pltpu.make_async_remote_copy(
            src, dst, send, recv, device_id=at, device_id_type=MESH
        )

    def start(copies):
        for cp in copies:
            cp.start()

    def arrived(copies):
        for cp in copies:
            cp.wait_recv()

    def some_images(step, first, last):
        def run(b, _):
            step(b)
            return 0

        lax.fori_loop(first, last, run, 0)

    def each_image(step):
        some_images(step, 0, images)

    message_rows = (48, 48, 48, 16, 48, 16, 48)

    def copies(p, b):
        full, stat = pl.ds(0, message_rows[p]), pl.ds(0, 16)
        return [
            remote(
                src.at[p, b, rows], got.at[p, b, k - 1, rows], ssem.at[p, b, k - 1],
                rsem.at[p, b, k - 1], who[k],
            )
            for k, src, rs in ((1, m1, full), (2, m1, stat), (3, m3, full))
            for rows in (rs,)
        ]

    def fill_message(p, b, first, second, edges=None):
        packed = pack_stats(first, second)
        m1[p, b, 0:16] = packed
        m3[p, b, 0:16] = packed
        if edges is not None:
            m1[p, b, 16:48] = edges(inner).astype(low_type)
            m3[p, b, 16:48] = edges(outer).astype(low_type)

    def send(p, b, first, second, edges=None):
        fill_message(p, b, first, second, edges)
        start(copies(p, b))

    def receive(p, b):
        arrived(copies(p, b))
        parts = [m1[p, b, 0:16]] + [got[p, b, k, 0:16] for k in range(3)]
        return combine_stats(parts, ones[...], entries)

    def receive_scale(p, b):
        first, second = receive(p, b)
        scaled = lax.rsqrt(second - first * first + norm_eps)
        st[b, 2 * p : 2 * p + 1] = first
        st[b, 2 * p + 1 : 2 * p + 2] = scaled
        return first, scaled

    def far_rows(p, b, k):
        return got[p, b, k, 16:48].astype(float_type)

    def fill_halo(buf, value):
        fill_row(buf, inner_halo, value(0), channels, width)
        fill_row(buf, outer_halo, jnp.where(outer_live, value(2), 0.0), channels, width)

    def convolve(w):
        depth = 3 * channels
        return sum(
            dot(abuf[width * dy : width * dy + pixels, :], w[depth * dy : depth * (dy + 1), :])
            for dy in range(3)
        )

    def data_grad(buf, b, w):
        total = None
        for dy in range(3):
            for dx in range(3):
                tap = 3 * dy + dx
                more = dot_nt(
                    buf[b, (2 - dy) * width : (2 - dy) * width + pixels,
                        (2 - dx) * channels : (3 - dx) * channels],
                    w[tap * channels : (tap + 1) * channels, :],
                )
                total = more if total is None else total + more
        return total

    def kernel_grad(act_t, buf, base):
        for dy in range(3):
            for dx in range(3):
                tap = 3 * dy + dx
                at = (2 - dx) * channels
                g = None
                for b in range(images):
                    more = dot(
                        act_t[:, b * pixels : (b + 1) * pixels],
                        buf[b, (2 - dy) * width : (2 - dy) * width + pixels, at : at + channels],
                    )
                    g = more if g is None else g + more
                g = g.astype(low_type)
                for m in range(4):
                    lo = max(tap * channels, m * quarter)
                    hi = min((tap + 1) * channels, (m + 1) * quarter)
                    for n in range(3 if lo < hi else 0):
                        gw[base + n, m, lo - m * quarter : hi - m * quarter] = g[
                            lo - tap * channels : hi - tap * channels, 128 * n : 128 * n + 128
                        ]

    def reduction(out, lanes, n, q, refs):
        return Reduction(out, lanes, n, q, refs, who, place, cs, cr, es, er)

    refs = (gw, w_core, w_got_x, w_own, w_got_y, w_got_z, w_got_e)
    red2 = [reduction(gw2_ref, slice(128 * n, 128 * n + 128), n, n, refs) for n in range(3)]
    red1 = [reduction(gw1_ref, slice(128 * n, 128 * n + 128), n + 3, n + 3, refs) for n in range(3)]
    refs = (gjo, o_core, o_got_x, o_own, o_got_y, o_got_z, o_got_e)
    red0 = reduction(go_ref, slice(0, channels), None, 6, refs)
    zs, extras = chips["z"], chips["e"]

    def small_row_copies(s):
        return [
            remote(v_own.at[s], v_row.at[s, k - 1], vs.at[s, k - 1], vr.at[s, k - 1], who[k])
            for k in (1, 2, 3)
        ]

    def small_y_copies(s):
        return [remote(v_one.at[s], v_y.at[s], vs.at[s, 3], vr.at[s, 3], chips["y"][0])]

    def small_z_copies(s):
        return [
            remote(v_two.at[s], v_z.at[s, n], vs.at[s, 4 + n], vr.at[s, 4 + n], at)
            for n, at in enumerate(zs)
        ]

    def small_e_copies(s):
        return [
            remote(v_three.at[s], v_e.at[s, n], vs.at[s, 7 + n], vr.at[s, 7 + n], at)
            for n, at in enumerate(extras)
        ]

    def small_row(s):
        v_own[s] = gs[...]
        start(small_row_copies(s))

    def small_y(s):
        arrived(small_row_copies(s))
        v = v_own[s] + v_row[s, 0] + v_row[s, 1] + v_row[s, 2]
        quarter_of = channels // 4
        v = pltpu.roll(v, lax.rem(channels - r * quarter_of, channels), 1)
        v_one[s] = v[:, 0:128]
        if s == 0:
            double = lax.rem(r, 2) * 2 * quarter_of
            pair = jnp.where(r < 2, v_own[0, 8:9], v_own[0, 9:10])
            for k in range(3):
                pair = pair + jnp.where(r < 2, v_row[0, k, 8:9], v_row[0, k, 9:10])
            pair = pltpu.roll(pair, lax.rem(channels - double, channels), 1)
            v_one[0, 8:9] = pair[:, 0:128]
            v_one[0, 9:10] = pltpu.roll(pair, channels - 128, 1)[:, 0:128]
        start(small_y_copies(s))

    def small_z(s):
        arrived(small_y_copies(s))
        v_two[s] = v_one[s] + v_y[s]
        start(small_z_copies(s))

    def small_end(s):
        arrived(small_z_copies(s))
        v_three[s] = v_two[s] + v_z[s, 0] + v_z[s, 1] + v_z[s, 2]
        total = v_three[s]
        if extras:
            start(small_e_copies(s))
            arrived(small_e_copies(s))
            for n in range(len(extras)):
                total = total + v_e[s, n]
        gv_ref[pl.ds(16 * s, 16), 0:128] = total

    def gather_row_copies():
        return [
            remote(mg, g_row.at[k - 1], gsem.at[k - 1], hsem.at[k - 1], who[k])
            for k in (1, 2, 3)
        ]

    def gather_copies():
        blocks = [pl.ds(i, 1), pl.ds(pl.multiple_of(i - lax.rem(i, 2), 2), 2)]
        blocks.append(pl.ds(pl.multiple_of(i - lax.rem(i, 8), 8), 8))
        found = []
        for rows, places in zip(blocks, (chips["y"], zs, extras)):
            for at in places:
                n = 3 + len(found)
                part_of = gat.at[c, rows]
                found.append(remote(part_of, part_of, gsem.at[n], hsem.at[n], at))
        return found

    def gather_core_copies():
        n = 7 + len(extras)
        return [remote(gat.at[c], gat.at[c], gsem.at[n], hsem.at[n], who[1])]

    def gather_row():
        start(gather_row_copies())

    def gather_y():
        arrived(gather_row_copies())
        v = emb[...] + mg[...] + g_row[0] + g_row[1] + g_row[2]
        gat[c, i] = jnp.where(c == 0, v[:, :channels], v[:, channels:])
        start(gather_copies()[:1])

    def gather_z():
        arrived(gather_copies()[:1])
        start(gather_copies()[1:4])

    def gather_end():
        arrived(gather_copies()[1:4])
        start(gather_copies()[4:])
        arrived(gather_copies()[4:])
        start(gather_core_copies())

    def gather_core():
        other = gat.at[1 - c]
        n = 7 + len(extras)
        remote(other, other, gsem.at[n], hsem.at[n], who[1]).wait_recv()

    def three_terms(v):
        a = v.astype(low_type)
        b = (v - a.astype(float_type)).astype(low_type)
        d = (v - a.astype(float_type) - b.astype(float_type)).astype(low_type)
        return jnp.concatenate([a, b, d], axis=0)

    def embedding():
        for ref in (ge_ref, gc_ref, geo_ref):
            ref[...] = jnp.zeros(ref.shape, float_type)
        lax.fori_loop(0, gat.shape[1] // 8, embedding_part, 0)

    def embedding_part(part_of, _):
        every = 64
        groups = pl.ds(pl.multiple_of(part_of * 8, 8), 8)
        full = jnp.concatenate(
            [gat[n, groups].reshape(every, channels) for n in range(2)], axis=1
        )
        place_of = lax.rem(lax.broadcasted_iota(jnp.int32, (every, 2 * channels), 0), 8)
        live = place_of < images
        grad = jnp.where(live, full, 0.0)
        held = jnp.where(live, pltpu.roll(full, every - images, 0), 0.0)
        act = jnp.where(live, half_silu(held), 0.0).astype(low_type)
        left[...] = jnp.concatenate([act, act, act], axis=0).T
        terms = three_terms(grad)
        size = 2 * channels // 4
        own = pl.ds(pl.multiple_of(r * size, size), size)
        v = jnp.dot(left[own, :], terms, preferred_element_type=float_type)
        ge_ref[0:size] += v[:, :channels]
        ge_ref[size : 2 * size] += v[:, channels:]
        v = jnp.sum(grad, axis=0, keepdims=True)
        geo_ref[0:1] += v[:, :channels]
        geo_ref[8:9] += v[:, channels:]
        active = lax.dot_general(terms, ew[...], contract_cols, preferred_element_type=float_type)
        active = active[0:every] + active[every : 2 * every] + active[2 * every :]
        back = jnp.where(live, active * slope_of(held), 0.0)
        classes = ct.shape[0] // 4
        row_of = lax.rem(lax.broadcasted_iota(jnp.int32, (every, 128), 0), 8)
        label = jnp.full((every, 128), -1.0, float_type)
        for b in range(images):
            rolled = pltpu.roll(full[:, 256 * b : 256 * b + 128], every - 2 * images + b, 0)
            label = jnp.where(row_of == b, rolled, label)
        for n in range(hot.shape[0] // 128):
            kind = lax.broadcasted_iota(jnp.int32, (every, 128), 1) + 128 * n + r * classes
            hit = jnp.where(label == kind.astype(float_type), 1.0, 0.0).astype(low_type)
            hot[128 * n : 128 * (n + 1), :] = jnp.concatenate([hit, hit, hit], axis=0).T
        found = jnp.dot(hot[...], three_terms(back), preferred_element_type=float_type)
        height = gc_ref.shape[0] // 2
        gc_ref[0:height] += found[0:height, :channels]
        gc_ref[height:] += found[0:height, channels:]
        return 0

    def embed_forward():
        row = lax.broadcasted_iota(jnp.int32, (8, 2 * channels), 0)
        lane_of = lax.broadcasted_iota(jnp.int32, (8, channels), 1).astype(float_type)

        def spread(ref, other):
            v = jnp.full((8, channels), other, float_type)
            for b in range(images):
                v = jnp.where(row[:, :channels] == b, ref[b].astype(float_type), v)
            return v

        position = (spread(index_ref, 0.0) + 1.0) / (spread(count_ref, 2.0) - 1.0)
        low_root = sigma_least ** (1.0 / sigma_power)
        high_root = sigma_most ** (1.0 / sigma_power)
        root = low_root + position * (high_root - low_root)
        square = root * root
        noise_time = 250.0 * jnp.log(square * square * square * root)
        angles = noise_time * jnp.exp(lane_of * (-math.log(10000.0) / channels))
        features = jnp.concatenate([jnp.cos(angles), jnp.sin(angles)], axis=1)
        count = ct.shape[0]
        label = spread(label_ref, -1.0)[:, 0:1]
        kinds = lax.broadcasted_iota(jnp.int32, (8, count), 1).astype(float_type)
        one_hot = jnp.where(label == kinds, 1.0, 0.0).astype(low_type)
        loads["ct"].wait()
        embedded = features + dot(one_hot, ct[...])
        live = row < images
        embed_act = half_silu(embedded).astype(low_type)
        loads["ew"].wait()
        offset = jnp.concatenate([vec(11), vec(12)], axis=1)
        mod[...] = dot(embed_act, ew[...]) + offset
        rows = pltpu.roll(jnp.where(live, embedded, 0.0), images, 0)
        part_of = lax.broadcasted_iota(jnp.int32, (8, 2 * channels), 1)
        marks = jnp.zeros((8, 2 * channels), float_type)
        for b in range(images):
            here = jnp.logical_and(row == 2 * images, part_of >= 256 * b)
            marks = jnp.where(here, label_ref[b].astype(float_type), marks)
        emb[...] = rows + marks

    at = 0
    for line in lines:
        v = line[...].astype(float_type).reshape(1, line.shape[0])
        for n in range(line.shape[0] // channels):
            vec_ref[at : at + 1] = v[:, n * channels : (n + 1) * channels]
            at += 1
    ones[...] = block_ones(channels, channels // GROUPS)
    gs[...] = jnp.zeros(gs.shape, float_type)
    mg[...] = jnp.zeros(mg.shape, float_type)

    def clear(n, _):
        for m in range(4):
            gw[n, m, quarter:padded] = jnp.zeros((padded - quarter, 128), low_type)
        return 0

    lax.fori_loop(0, 6, clear, 0)

    @each_image
    def _(b):
        v = x_ref[b].astype(float_type)
        fill_message(0, b, col_sum(v), col_sum(v * v), lambda at: x_ref[b, pl.ds(at, width)])
        none = jnp.zeros((1, channels), float_type)
        fill_message(6, b, none, none, lambda at: cot_ref[b, pl.ds(at, width)])

    embed_forward()
    pl.semaphore_wait(barrier, len(greeted))

    @each_image
    def _(b):
        start(copies(0, b))

    @each_image
    def _(b):
        start(copies(6, b))

    loads["ow"].wait()

    @each_image
    def _(b):
        d_out_t[b] = dot_nt(cot_ref[b], ow[...]).T.astype(low_type)

    def first_convolution(b):
        centre, scaled = receive_scale(0, b)
        slope = scaled * vec(0)
        shift = vec(1)

        def activate(v):
            return half_silu((v - centre) * slope + shift)

        for row in range(rows_in):
            v = activate(x_ref[b, row * width : (row + 1) * width].astype(float_type))
            fill_row(abuf, (row + 1) * width, v, channels, width)
        fill_halo(abuf, lambda k: activate(far_rows(0, b, k)))
        hidden = convolve(w1) + vec(2)
        hid[b] = hidden
        send(
            1, b, col_sum(hidden), col_sum(hidden * hidden),
            lambda at: hid[b, pl.ds(at, width)],
        )
        own = pl.ds(pl.multiple_of(b * pixels, pixels), pixels)
        act1_t[:, own] = abuf[width : width + pixels, channels : 2 * channels].T

    def block(n):
        return pl.ds(pl.multiple_of(width + n * pixels, width), pixels)

    def wide_block(n):
        return pl.ds(pl.multiple_of(n * pixels, width), pixels + 2 * width)

    def span_of(n):
        return pl.ds(pl.multiple_of(n * pixels, pixels), pixels)

    mate = r + 1 - 2 * c
    across = lax.rem(r + 2, 4)

    def gather(b, n, rows):
        return remote(
            att.at[b, rows], att.at[b, rows], gsend.at[b, n], grecv.at[b, n], who[(1, 2, 1)[n]]
        )

    def shares(b):
        return [gather(b, n, block(rows)) for n, rows in enumerate((r, r, across))]

    def arrivals(b):
        rows = (mate, across, lax.rem(mate + 2, 4))
        return [gather(b, n, block(w)) for n, w in enumerate(rows)]

    def share(b):
        centre, scaled = receive_scale(2, b)
        slope = scaled * vec(6)
        att[b, block(r)] = ((mid[b] - centre) * slope + vec(7)).astype(low_type)
        start(shares(b)[:2])

    def second_convolution(b):
        centre, scaled = receive_scale(1, b)
        grow = 1.0 + mod[pl.ds(b, 1), 0:channels]
        slope = scaled * vec(3) * grow
        shift = vec(4) * grow + mod[pl.ds(b, 1), channels:]

        def activate(v):
            return half_silu((v - centre) * slope + shift)

        for row in range(rows_in):
            v = activate(hid[b, row * width : (row + 1) * width])
            fill_row(abuf, (row + 1) * width, v, channels, width)
        fill_halo(abuf, lambda k: activate(far_rows(1, b, k)))
        middle = (convolve(w2) + vec(5) + x_ref[b].astype(float_type)) * half
        mid[b] = middle
        send(
            2, b, col_sum(middle), col_sum(middle * middle),
            lambda at: mid[b, pl.ds(at, width)],
        )
        own = pl.ds(pl.multiple_of(b * pixels, pixels), pixels)
        act2_t[:, own] = abuf[width : width + pixels, channels : 2 * channels].T

    loads["w1"].wait()
    loads["w2"].wait()
    loads["jw"].wait()
    some_images(first_convolution, 0, 2)
    some_images(second_convolution, 0, 1)
    some_images(first_convolution, 2, images)
    share(0)
    some_images(second_convolution, 1, images)

    part = att

    def forward(b):
        arrivals(b)[1].wait_recv()
        shares(b)[2].start()

    def sums_core(b):
        return [
            remote(
                part.at[b, wide_block(2 * n + 1 - c)], got_core.at[b, n], asem.at[b, n],
                bsem.at[b, n], who[1],
            )
            for n in range(2)
        ]

    def sum_x(b):
        return remote(to_x, got_x.at[b], asem.at[b, 2], bsem.at[b, 2], who[2])

    def pass_on(b):
        x = lax.div(r, 2)
        arrived(sums_core(b))

        @pl.when(b > 0)
        def _():
            sum_x(b - 1).wait_send()

        far = 1 - x
        to_x[...] = (
            part[b, wide_block(2 * far + c)].astype(float_type)
            + got_core[b, far].astype(float_type)
        ).astype(low_type)
        sum_x(b).start()
        ag[b] = part[b, wide_block(r)].astype(float_type) + got_core[b, x].astype(float_type)

    def queries(b):
        q = (dot(att[b, block(r)], jw[:, :channels]) + vec(8)).astype(low_type)
        q8[...] = (q.astype(float_type) * HEAD ** (-0.5)).astype(low_type)

    lane = lax.broadcasted_iota(jnp.int32, (pixels, pair_lanes), 1)

    def masked(v):
        return jnp.concatenate(
            [jnp.where(lane < HEAD, v, 0.0), jnp.where(lane >= HEAD, v, 0.0)], axis=0
        ).astype(low_type)

    q_sum[...] = jnp.zeros(q_sum.shape, float_type)
    kv_sum[...] = jnp.zeros(kv_sum.shape, float_type)
    o_sum[...] = jnp.zeros(o_sum.shape, float_type)
    att_t[channels:] = jnp.ones((16, whole), low_type)
    none = jnp.zeros((width, channels), low_type)
    for b in range(images):
        att[b, 0:width] = none
        att[b, width + whole :] = none

    @each_image
    def _(b):
        a = arrivals(b)
        bias = jnp.concatenate([jnp.zeros((1, channels), float_type), vec(9)], axis=1)

        def project(x):
            rows = pl.ds(pl.multiple_of(width + 2 * x * pixels, width), 2 * pixels)
            to = pl.ds(pl.multiple_of(2 * x * pixels, 2 * pixels), 2 * pixels)
            kv[to] = (dot(att[b, rows], jw[:, channels:]) + bias).astype(low_type)

        queries(b)
        a[0].wait_recv()
        project(lax.div(r, 2))

        @pl.when(b == 0)
        def _():
            forward(0)

        a[2].wait_recv()
        project(1 - lax.div(r, 2))

        @pl.when(b == 0)
        def _():
            some_images(share, 1, images)

        for n in range(2 * channels // 128):
            cols = pl.ds(n * 128, 128)
            kv_t[cols, :] = kv[:, cols].T

        @pl.when(b > 0)
        def _():
            pass_on(b - 1)

        def one_pair(t, _):
            lanes = pl.ds(pl.multiple_of(t * pair_lanes, pair_lanes), pair_lanes)
            v_lanes = pl.ds(pl.multiple_of(channels + t * pair_lanes, pair_lanes), pair_lanes)
            qm[...] = masked(q8[:, lanes].astype(float_type))
            peak = None
            for n in range(whole // chunk):
                rows = pl.ds(n * chunk, chunk)
                s = dot_nt(kv[rows, lanes], qm[...])
                s_ref[rows] = s
                top = jnp.max(s.reshape(chunk // 8, 8, 2 * pixels), axis=0)
                peak = top if peak is None else jnp.maximum(peak, top)
            peak = jnp.max(peak, axis=0, keepdims=True)
            total = None
            for n in range(whole // chunk):
                rows = pl.ds(n * chunk, chunk)
                e = jnp.exp(s_ref[rows] - peak)
                eb[rows] = e.astype(low_type)
                more = jnp.sum(e.reshape(chunk // 8, 8, 2 * pixels), axis=0)
                total = more if total is None else total + more
            over = 1.0 / jnp.sum(total, axis=0, keepdims=True)
            inner_of, scaled = [], []
            for j in range(2):
                head = pl.ds(pl.multiple_of(t * pair_lanes + j * HEAD, HEAD), HEAD)
                v_head = pl.ds(pl.multiple_of(channels + t * pair_lanes + j * HEAD, HEAD), HEAD)
                cols = slice(j * pixels, (j + 1) * pixels)
                mt = dot(kv_t[v_head, :], eb[:, cols]) * over[:, cols]
                mix_t[head] = mt.astype(low_type)
                g = (d_out_t[b, head].astype(float_type) * over[:, cols]).astype(low_type).astype(float_type)
                inner_of.append(col_sum(g * mt))
                scaled.append(g)
            inner_of = jnp.concatenate(inner_of, axis=1)
            dom[...] = masked(jnp.concatenate(scaled, axis=0).T)
            for n in range(whole // chunk):
                rows = pl.ds(n * chunk, chunk)
                dp = dot_nt(kv[rows, v_lanes], dom[...])
                dsb[rows] = (eb[rows].astype(float_type) * (dp - inner_of)).astype(low_type)
            for j in range(2):
                head = pl.ds(pl.multiple_of(t * pair_lanes + j * HEAD, HEAD), HEAD)
                cols = slice(j * pixels, (j + 1) * pixels)
                dq_t[head] = dot(kv_t[head, :], dsb[:, cols]) * HEAD ** (-0.5)
            dkv[:, lanes] = dot(dsb[...], qm[...]).astype(low_type)
            dkv[:, v_lanes] = dot(eb[...], dom[...]).astype(low_type)
            return 0

        lax.fori_loop(0, pairs, one_pair, 0)

        @pl.when(b + 1 < images)
        def _():
            forward(b + 1)

        dq[...] = dq_t[...].T.astype(low_type)
        att_t[0:channels] = att[b, width : width + whole].T
        for cp in shares(b):
            cp.wait_send()
        own = dot_nt(dq[...], jw[:, :channels])
        first = col_sum(own)
        second = col_sum(own * att[b, block(r)].astype(float_type))
        for n in range(4):
            rows = pl.ds(width + n * pixels, pixels)
            v = dot_nt(dkv[n * pixels : (n + 1) * pixels], jw[:, channels:])
            first += col_sum(v)
            second += col_sum(v * att[b, rows].astype(float_type))
            part[b, rows] = v.astype(low_type)
        part[b, block(r)] = (part[b, block(r)].astype(float_type) + own).astype(low_type)
        start(sums_core(b))
        second = (second - vec(7) * first) / vec(6)
        gs[6:7] += second
        gs[7:8] += first
        send(3, b, first * vec(6), second * vec(6))
        q_sum[...] += dot(att_t[:, span_of(r)], dq[...])
        kv_sum[...] += dot(att_t[...], dkv[...])

        @pl.when(b == images - 1)
        def _():
            pass_on(b)

        o_sum[...] += dot(mix_t[...], cot_ref[b])
        low_out[span_of(b)] = mix_t[...].T

    def pack_weights():
        part_rows = channels // 4
        every = (q_sum[0:channels], kv_sum[0:channels, :channels], kv_sum[0:channels, channels:], o_sum[...])
        for n, v in enumerate(every):
            for m in range(4):
                gjo[m, n * part_rows : (n + 1) * part_rows] = v[
                    m * part_rows : (m + 1) * part_rows
                ].astype(low_type)
        gs[8:9] = q_sum[channels : channels + 1]
        gs[9:10] = kv_sum[channels : channels + 1, channels:]
        gs[10:11] = col_sum(jnp.sum(cot_ref[...].astype(float_type), axis=0))

    def result(b):
        v = mid[b] + dot(low_out[span_of(b)], ow[...]) + vec(10)
        low_out[span_of(b)] = v.astype(low_type)

    def branch_grad(b):
        first, second = receive(3, b)
        arrived(copies(6, b))
        sum_x(b).wait_recv()
        centre, scaled = st[b, 4:5], st[b, 5:6]

        def grad_of(cot, rows, v):
            u = ag[b, rows] + got_x[b, rows].astype(float_type)
            return (cot + scaled * (u * vec(6) - first - (v - centre) * scaled * second)) * half

        total = jnp.zeros((1, channels), float_type)
        for row in range(rows_in):
            rows = pl.ds(row * width, width)
            inside = pl.ds((row + 1) * width, width)
            v = grad_of(cot_ref[b, rows].astype(float_type), inside, mid[b, rows])
            ag[b, inside] = v
            v = v.astype(low_type).astype(float_type)
            fill_row(grad.at[b], (row + 1) * width, v, channels, width)
            total += col_sum(v)
        gs[5:6] += total
        places = {0: pl.ds(inner_halo, width), 2: pl.ds(outer_halo, width)}
        fill_halo(grad.at[b], lambda k: grad_of(far_rows(6, b, k), places[k], far_rows(2, b, k)))

    def branch_back(b):
        upstream = data_grad(grad, b, w2)
        grow = 1.0 + mod[pl.ds(b, 1), 0:channels]
        normed = (hid[b] - st[b, 2:3]) * st[b, 3:4]
        pre = (normed * vec(3) + vec(4)) * grow + mod[pl.ds(b, 1), channels:]
        v = upstream * slope_of(pre)
        slope_grad[b] = v
        first, second = col_sum(v), col_sum(v * normed)
        mg[pl.ds(b, 1), 0:channels] = vec(3) * second + vec(4) * first
        mg[pl.ds(b, 1), channels:] = first
        first, second = grow * first, grow * second
        gs[3:4] += second
        gs[4:5] += first
        send(
            4, b, first * vec(3), second * vec(3),
            lambda at: slope_grad[b, pl.ds(at, width)],
        )

    def hidden_grad(b):
        first, second = receive(4, b)
        centre, scaled = st[b, 2:3], st[b, 3:4]
        gain = (1.0 + mod[pl.ds(b, 1), 0:channels]) * vec(3)

        def grad_of(u, v):
            return scaled * (u * gain - first - (v - centre) * scaled * second)

        total = jnp.zeros((1, channels), float_type)
        for row in range(rows_in):
            rows = pl.ds(row * width, width)
            v = grad_of(slope_grad[b, rows], hid[b, rows]).astype(low_type).astype(float_type)
            fill_row(grad.at[b], (row + 1) * width, v, channels, width)
            total += col_sum(v)
        gs[2:3] += total
        fill_halo(grad.at[b], lambda k: grad_of(far_rows(4, b, k), far_rows(1, b, k)))

    def hidden_back(b):
        upstream = data_grad(grad, b, w1)
        normed = (x_ref[b].astype(float_type) - st[b, 0:1]) * st[b, 1:2]
        v = upstream * slope_of(normed * vec(0) + vec(1))
        slope_grad[b] = v
        first, second = col_sum(v), col_sum(v * normed)
        gs[0:1] += second
        gs[1:2] += first
        send(5, b, first * vec(0), second * vec(0))

    def images_grad(b):
        first, second = receive(5, b)
        scaled = st[b, 1:2]
        normed = (x_ref[b].astype(float_type) - st[b, 0:1]) * scaled
        v = scaled * (slope_grad[b] * vec(0) - first - normed * second)
        wide_out[span_of(b)] = ag[b, width : width + pixels] + v

    pack_weights()
    some_images(branch_grad, 0, images - 1)
    red0.core()
    red0.across_x()
    some_images(branch_back, 0, images - 1)
    some_images(branch_grad, images - 1, images)
    some_images(branch_back, images - 1, images)
    small_row(0)
    gather_row()
    kernel_grad(act2_t, grad, 0)
    red2[0].core()
    red0.across_y()
    red2[1].core()
    red2[2].core()
    red2[0].across_x()
    each_image(result)
    some_images(hidden_grad, 0, images - 1)
    red2[2].across_x()
    red2[1].across_x()
    small_y(0)
    gather_y()
    some_images(hidden_grad, images - 1, images)
    red0.across_z()
    red2[0].across_y()
    small_z(0)
    gather_z()
    kernel_grad(act1_t, grad, 3)
    red1[2].core()
    red0.back_z()
    red1[0].core()
    red2[0].across_z()
    red1[2].across_x()
    red2[2].across_y()
    red1[1].core()
    red2[1].across_y()
    red2[2].across_z()
    red1[1].across_x()
    red1[0].across_x()
    some_images(hidden_back, images - 1, images)
    red2[0].back_z()
    red1[2].across_y()
    red2[1].across_z()
    red2[2].back_z()
    some_images(hidden_back, 0, images - 1)
    red1[1].across_y()
    small_end(0)
    gather_end()
    red1[2].across_z()
    red2[0].back_y()
    red2[1].back_z()
    red1[0].across_y()
    red0.back_y()
    red1[1].across_z()
    small_row(1)
    red2[2].back_y()
    each_image(images_grad)
    red2[0].end()
    red1[2].back_z()
    red1[0].across_z()
    red1[1].back_z()
    red1[2].back_y()
    gather_core()
    embedding()
    red1[0].back_z()
    red2[1].back_y()
    small_y(1)
    red1[1].back_y()
    red1[0].back_y()
    red2[2].end()
    red0.end()
    red1[2].end()
    small_z(1)
    small_end(1)
    red1[1].end()
    red2[1].end()
    red1[0].end()

    @each_image
    def _(b):
        sent = sums_core(b)
        for p in range(7):
            sent += copies(p, b)
        for cp in sent:
            cp.wait_send()

    sum_x(images - 1).wait_send()

    for red in [red0] + red1 + red2:
        red.drain()
    for s in range(2):
        for cp in small_row_copies(s) + small_y_copies(s) + small_z_copies(s) + small_e_copies(s):
            cp.wait_send()
    for cp in gather_row_copies() + gather_copies() + gather_core_copies():
        cp.wait_send()


def block_call(x, cot, lines, scalars, w1, w2, jw, ow, ew, ct):
    images, pixels, channels = x.shape
    span = pixels + 64
    whole = 4 * pixels
    padded = -(-9 * channels // 4 // 128) * 128
    every = lax.axis_size("img")
    more = every // 8
    some = max(more - 1, 1)
    low_at, wide_at = out_rows(images * pixels, channels, ct.shape[0])
    vm = pl.BlockSpec(memory_space=pltpu.VMEM)
    hbm = pl.BlockSpec(memory_space=pl.ANY)

    def low(*shape):
        return pltpu.VMEM(shape, low_type)

    def wide(*shape):
        return pltpu.VMEM(shape, float_type)

    def dma(*shape):
        return pltpu.SemaphoreType.DMA(shape)

    def out(*shape, kind=float_type):
        return jax.ShapeDtypeStruct(shape, kind)

    return pl.pallas_call(
        block_kernel,
        out_shape=(
            out(sum(low_at["jo"]), channels, kind=low_type), out(sum(wide_at["offset"]), channels),
        ),
        in_specs=[vm] * (2 + len(lines)) + [pl.BlockSpec(memory_space=pltpu.SMEM)] * 3 + [hbm] * 6,
        out_specs=(vm,) * 2,
        scratch_shapes=[
            low(*w1.shape), low(*w2.shape), low(*jw.shape), low(*ow.shape), low(*ew.shape),
            low(*ct.shape), low(channels, channels), wide(*x.shape), wide(*x.shape),
            wide(8, 2 * channels), wide(8, 2 * channels),
            low(channels, images * pixels), low(channels, images * pixels),
            wide(images, 8, channels), low(7, images, 48, channels), low(7, images, 48, channels),
            low(7, images, 3, 48, channels),
            low(images, whole + 64, channels), low(channels + 16, whole), low(whole, 2 * channels),
            low(2 * channels, whole), low(pixels, channels), low(images, channels, pixels),
            low(2 * pixels, 2 * HEAD), low(2 * pixels, 2 * HEAD), wide(whole, 2 * pixels),
            low(whole, 2 * pixels), low(whole, 2 * pixels), low(channels, pixels),
            wide(channels, pixels), low(pixels, channels), low(whole, 2 * channels),
            low(images, 2, span, channels), low(span, channels), low(images, span, channels),
            wide(images, span, channels),
            wide(channels + 16, channels),
            wide(channels + 16, 2 * channels), wide(channels, channels), low(4, channels, channels),
            low(images, span, 3 * channels), wide(*x.shape), wide(16, channels), wide(8, 2 * channels),
            low(6, 4, padded, 128), low(6, 2, padded, 128), low(6, padded, 128),
            wide(6, padded // 2, 128), low(6, padded // 2, 128), low(6, 3, padded // 8, 128),
            low(6, some, padded // 8, 128),
            low(2, channels, channels), low(channels, channels), wide(channels // 2, channels),
            low(channels // 2, channels), low(3, channels // 8, channels),
            low(some, channels // 8, channels),
            wide(2, 16, channels), wide(2, 3, 16, channels), wide(2, 16, 128),
            wide(2, 16, 128), wide(2, 16, 128), wide(2, 3, 16, 128), wide(2, 16, 128),
            wide(2, some, 16, 128), wide(3, 8, 2 * channels), wide(2, every, 8, channels),
            low(2 * channels, 192), low(256, 192), wide(16, channels), wide(8, 2 * channels),
            dma(6), dma(7, images, 3), dma(7, images, 3), dma(images, 3), dma(images, 3),
            dma(images, 3), dma(images, 3), dma(7, 11), dma(7, 11), dma(7, some), dma(7, some),
            dma(2, 6 + more), dma(2, 6 + more), dma(7 + more), dma(7 + more),
        ],
        compiler_params=pltpu.CompilerParams(
            collective_id=0, has_side_effects=True, vmem_limit_bytes=62 << 20
        ),
        name="block",
    )(x, cot, *lines, *scalars, w1, w2, jw, ow, ew, ct)


def finish_kernel(
    low_any, wide_any,
    result, images, first_gain, first_shift, first_kernel, first_offset, embed_weight,
    embed_offset, class_table, second_gain, second_shift, second_kernel, second_offset,
    third_gain, third_shift, joint_weight, joint_offset, output_weight, output_offset,
    low_in, wide_in, sems,
):
    r = lax.axis_index("row")
    rows, channels = output_weight.shape
    pixels = result.shape[0]
    low_at, wide_at = out_rows(pixels, channels, 4 * class_table.shape[0])
    moves = [
        pltpu.make_async_copy(src, dst, sems.at[n])
        for n, (src, dst) in enumerate((
            (low_any, low_in), (wide_any, wide_in), (low_in.at[pl.ds(0, pixels)], result),
            (wide_in.at[pl.ds(0, pixels)], images),
        ))
    ]
    moves[0].start()
    moves[1].start()

    def low_rows(name, start, size):
        at = low_at[name][0] + start
        return low_in[at : at + size].astype(float_type)

    def wide_rows(name, start, size):
        at = wide_at[name][0] + start
        return wide_in[at : at + size]

    moves[0].wait()
    moves[2].start()
    first_kernel[...] = low_rows("w1", 0, 9 * rows)
    second_kernel[...] = low_rows("w2", 0, 9 * rows)
    for n in range(3):
        joint_weight[:, n * channels : (n + 1) * channels] = low_rows("jo", n * rows, rows)
    output_weight[...] = low_rows("jo", 3 * rows, rows)
    moves[1].wait()
    moves[3].start()
    lines = wide_rows("lines", 0, 32)
    for n, ref in (
        (16, first_gain), (17, first_shift), (18, first_offset), (3, second_gain),
        (4, second_shift), (5, second_offset), (6, third_gain), (7, third_shift),
        (10, output_offset),
    ):
        ref[...] = lines[n, 0:rows]
    joint_offset[...] = jnp.concatenate([lines[8:9, 0:128], lines[9:10, 0:128]], axis=1)[
        0, 0 : 2 * rows
    ]
    size = 2 * rows
    classes = class_table.shape[0]
    reach = wide_at["classes"][1] // 2
    for n in range(2):
        cols = slice(n * channels, (n + 1) * channels)
        embed_weight[:, cols] = wide_rows("embed", n * size, size)
        class_table[:, cols] = wide_rows("classes", n * reach, reach)[0:classes]
    whole = jnp.concatenate([wide_rows("offset", 0, 8), wide_rows("offset", 8, 8)], axis=1)
    turn = lax.rem(2 * channels - r * size, 2 * channels)
    embed_offset[...] = pltpu.roll(whole, turn, 1)[0, 0:size]
    for cp in moves[2:]:
        cp.wait()


def finish_call(low, wide, pixels, classes):
    channels = low.shape[1]
    rows = channels // 4
    vm = pl.BlockSpec(memory_space=pltpu.VMEM)
    hbm = pl.BlockSpec(memory_space=pl.ANY)

    def out(*shape, kind=float_type):
        return jax.ShapeDtypeStruct(shape, kind)

    kernel = out(9 * rows, channels)
    line = out(rows)
    return pl.pallas_call(
        finish_kernel,
        out_shape=(
            out(pixels, channels, kind=low_type), out(pixels, channels), line, line, kernel, line,
            out(2 * rows, 2 * channels), out(2 * rows), out(classes // 4, 2 * channels), line, line,
            kernel, line, line, line, out(rows, 3 * channels), out(2 * rows), out(rows, channels),
            line,
        ),
        in_specs=[hbm] * 2,
        out_specs=(hbm, hbm) + (vm,) * 17,
        scratch_shapes=[
            pltpu.VMEM(low.shape, low_type),
            pltpu.VMEM(wide.shape, float_type),
            pltpu.SemaphoreType.DMA((4,)),
        ],
        compiler_params=pltpu.CompilerParams(vmem_limit_bytes=60 << 20),
        name="finish",
    )(low, wide)


def shards(
    images,
    level_count,
    level_index,
    labels,
    first_gain,
    first_shift,
    first_kernel,
    first_offset,
    embed_weight,
    embed_offset,
    class_table,
    second_gain,
    second_shift,
    second_kernel,
    second_offset,
    third_gain,
    third_shift,
    joint_weight,
    joint_offset,
    output_weight,
    output_offset,
    cotangent,
):
    image_count, stripe_rows, image_width, channels = images.shape
    pixels = stripe_rows * image_width
    x = images.reshape(image_count, pixels, channels)
    cot = cotangent.reshape(image_count, pixels, channels)
    lines = (
        first_gain, first_shift, first_offset, second_gain, second_shift, second_offset,
        third_gain, third_shift, joint_offset, output_offset, embed_offset,
    )
    found = block_call(
        x, cot, lines, (level_count, level_index, labels), first_kernel, second_kernel,
        joint_weight, output_weight, embed_weight, class_table,
    )
    outs = finish_call(*found, image_count * pixels, class_table.shape[0])
    return (outs[0].reshape(images.shape), outs[1].reshape(images.shape)) + tuple(outs[2:])


def solution(mesh):
    in_specs = (
        (P("img", "row", None, None),) + (P("img"),) * 3 + (P(),) * 17
        + (P("img", "row", None, None),)
    )
    row, rows = P("row"), P("row", None)
    out_specs = (
        P("img", "row", None, None), P("img", "row", None, None), row, row, rows, row, rows, row,
        rows, row, row, rows, row, row, row, rows, row, rows, row,
    )
    return jax.shard_map(shards, mesh=mesh, in_specs=in_specs, out_specs=out_specs, check_vma=False)
```

```python
import math

import jax
import jax.numpy as jnp
from jax import lax
from jax.experimental import pallas as pl
from jax.experimental.pallas import tpu as pltpu
from jax.sharding import PartitionSpec as P

GROUPS = 32
HEAD = 64
MESH = pl.DeviceIdType.MESH

norm_eps = 1e-05
sigma_least = 0.002
sigma_most = 80.0
sigma_power = 7.0
float_type = jnp.float32
low_type = jnp.bfloat16
contract_cols = (((1,), (1,)), ((), ()))


def peers():
    i = lax.axis_index("img")
    r = lax.axis_index("row")
    c = lax.rem(r, 2)
    near = r + 1 - 2 * c
    return (i, r, c, {1: (i, near), 2: (i, lax.rem(r + 2, 4)), 3: (i, 3 - r)})


def half_silu(v):
    h = 0.5 * v
    return h * jnp.tanh(h) + h


def fill_row(buf, start, act, channels, width):
    col = lax.broadcasted_iota(jnp.int32, (width, channels), 0)
    left = jnp.where(col == 0, 0.0, pltpu.roll(act, 1, 0))
    right = jnp.where(col == width - 1, 0.0, pltpu.roll(act, width - 1, 0))
    rows = pl.ds(start, width)
    buf[rows, 0:channels] = left.astype(low_type)
    buf[rows, channels : 2 * channels] = act.astype(low_type)
    buf[rows, 2 * channels : 3 * channels] = right.astype(low_type)


def pack_stats(first, second):
    channels = first.shape[1]
    row = lax.broadcasted_iota(jnp.int32, (8, channels), 0)

    def terms(v):
        a = v.astype(low_type).astype(float_type)
        b = (v - a).astype(low_type).astype(float_type)
        c = v - a - b
        return jnp.where(row == 0, a, jnp.where(row == 1, b, jnp.where(row == 2, c, 0.0)))

    return jnp.concatenate([terms(first), terms(second)], axis=0).astype(low_type)


def block_ones(channels, per):
    a = lax.broadcasted_iota(jnp.int32, (channels, channels), 0)
    b = lax.broadcasted_iota(jnp.int32, (channels, channels), 1)
    a = lax.shift_right_logical(a * 43691, 19)
    b = lax.shift_right_logical(b * 43691, 19)
    return jnp.where(a == b, 1.0, 0.0).astype(low_type)


def combine_stats(parts, ones, entries):
    total = jnp.dot(jnp.concatenate(parts, axis=0), ones, preferred_element_type=float_type)
    first = total[0:8] + total[16:24] + total[32:40] + total[48:56]
    second = total[8:16] + total[24:32] + total[40:48] + total[56:64]
    first = jnp.sum(first, axis=0, keepdims=True) * (1.0 / entries)
    second = jnp.sum(second, axis=0, keepdims=True) * (1.0 / entries)
    return first, second


def chip_peers(i, r):
    size = lax.axis_size("img")
    z = lax.rem(lax.div(i, 2), 4)
    e = lax.div(i, 8)
    y = lax.rem(i, 2)
    others = (z + 1 - 2 * lax.rem(z, 2), lax.rem(z + 2, 4), 3 - z)
    more = size // 8
    near = [(i + 2 * (n - z), r) for n in others]
    over = [(i + 1 - 2 * y + 2 * (n - z), r) for n in others]
    aside = [(i + 1 - 2 * y, r)]
    return {
        "y": aside,
        "z": near,
        "all": near + aside + over,
        "e": [(i + 8 * (lax.rem(e + k, more) - e), r) for k in range(1, more)],
        "at": (y, z),
        "pieces": others,
        "places": [(y, n) for n in others] + [(1 - y, z)] + [(1 - y, n) for n in others],
    }


class Reduction:
    def __init__(self, out, start, size, mode, q, refs, who, place, cs, cr, es, er):
        def cut(ref, part):
            lead = (slice(None),) * (len(ref.shape) - 2)
            return ref.at[lead + (pl.ds(start // part, size // part),)]

        grad, core, got_x, own, got_y, got_z, got_e, two, every = refs
        self.grad, self.got_core, self.got_x = cut(grad, 1), cut(core, 1), cut(got_x, 1)
        self.own, self.got_y = cut(own, 2), cut(got_y, 2)
        self.got_z, self.got_e = cut(got_z, 8), cut(got_e, 8)
        self.got_two, self.got_all = two, every
        self.out = out.at[pl.ds(start, size)]
        self.mode, self.q, self.who, self.size = mode, q, who, size
        self.c, self.x, self.chips = place
        self.y, self.z = self.chips["at"]
        self.sems = (cs, cr, es, er)
        self.near, self.far = 2 * self.x + self.c, 2 * (1 - self.x) + self.c
        self.low, self.high = lax.rem(self.z, 2), lax.div(self.z, 2)
        self.slot = 2 * self.low + self.high if mode == "h" else self.z

    def copy(self, src, dst, n, at, extra=False):
        send, recv = self.sems[2:] if extra else self.sems[:2]
        return pltpu.make_async_remote_copy(
            src, dst, send.at[self.q, n], recv.at[self.q, n], device_id=at, device_id_type=MESH
        )

    def half(self, y):
        size = self.size // 2
        return pl.ds(pl.multiple_of(y * size, size), size)

    def piece(self, z, y=0):
        size = self.size // 8
        return pl.ds(pl.multiple_of(y * (self.size // 2) + z * size, size), size)

    def core_copies(self):
        return [
            self.copy(self.grad.at[2 * n + 1 - self.c], self.got_core.at[n], n, self.who[1])
            for n in range(2)
        ]

    def x_copies(self):
        if self.mode == "y":
            rows = self.half(self.y)
            return [self.copy(self.grad.at[self.far, rows], self.got_x.at[rows], 2, self.who[2])]
        return [self.copy(self.grad.at[self.far], self.got_x, 2, self.who[2])]

    def y_copies(self):
        rows, at = self.half(1 - self.y), self.chips["y"][0]
        if self.mode == "y":
            return [
                self.copy(self.grad.at[2 * n + self.c, rows], self.got_two.at[n], 3 + n, at)
                for n in range(2)
            ]
        return [self.copy(self.got_x.at[rows], self.got_y, 3, at)]

    def first_z_copies(self):
        return [
            self.copy(
                self.got_x.at[self.piece(2 * (1 - self.low) + n, self.y)], self.got_z.at[n], 5 + n,
                self.chips["z"][0],
            )
            for n in range(2)
        ]

    def second_z_copies(self):
        part = self.got_x.at[self.piece(2 * self.low + 1 - self.high, self.y)]
        return [self.copy(part, self.got_z.at[2], 7, self.chips["z"][1])]

    def back_second_copies(self):
        part = self.out.at[self.piece(self.slot, self.y)]
        return [self.copy(part, part, 8, self.chips["z"][1])]

    def back_first_copies(self):
        part = self.out.at[self.quarter()]
        return [self.copy(part, part, 9, self.chips["z"][0])]

    def quarter(self, y=None):
        size = self.size // 4
        y = self.y if y is None else y
        return pl.ds(pl.multiple_of(y * (self.size // 2) + self.low * size, size), size)

    def z_copies(self):
        return [
            self.copy(self.got_x.at[self.piece(p, self.y)], self.got_z.at[n], 5 + n, at)
            for n, (p, at) in enumerate(zip(self.chips["pieces"], self.chips["z"]))
        ]

    def spread_copies(self):
        return [
            self.copy(self.got_x.at[self.piece(z, y)], self.got_all.at[n], 12 + n, at)
            for n, ((y, z), at) in enumerate(zip(self.chips["places"], self.chips["all"]))
        ]

    def extra_copies(self):
        src = self.got_x.at[self.piece(self.slot, self.y)]
        return [
            self.copy(src, self.got_e.at[n], n, at, True) for n, at in enumerate(self.chips["e"])
        ]

    def back_z_copies(self):
        part = self.out.at[self.piece(self.z, self.y)]
        return [self.copy(part, part, 8 + n, at) for n, at in enumerate(self.chips["z"])]

    def back_y_copies(self):
        part = self.out.at[self.half(self.y)]
        return [self.copy(part, part, 11, self.chips["y"][0])]

    def back_copies(self):
        part = self.out.at[self.piece(self.z, self.y)]
        return [self.copy(part, part, 19 + n, at) for n, at in enumerate(self.chips["all"])]

    @staticmethod
    def start(copies):
        for cp in copies:
            cp.start()

    @staticmethod
    def arrived(copies):
        for cp in copies:
            cp.wait_recv()

    def core(self):
        self.start(self.core_copies())

    def pair_sum(self, n, *rows):
        return self.grad[(2 * n + self.c, *rows)].astype(float_type) + self.got_core[
            (n, *rows)
        ].astype(float_type)

    def chip_sum(self, rows):
        return self.pair_sum(self.x, rows) + self.got_x[rows].astype(float_type)

    def across_x(self):
        if self.mode == "y":
            self.arrived(self.y_copies())
            rows = self.half(self.y)
            for n, far in ((1 - self.x, True), (self.x, False)):
                v = self.pair_sum(n, rows) + self.got_two[n].astype(float_type)
                if far:
                    self.grad[self.far, rows] = v.astype(low_type)
                    self.start(self.x_copies())
                else:
                    self.own[...] = v
            return
        self.arrived(self.core_copies())
        self.grad[self.far] = self.pair_sum(1 - self.x).astype(low_type)
        self.start(self.x_copies())

    def across_y(self):
        rows = self.half(1 - self.y)
        if self.mode == "y":
            self.arrived(self.core_copies())
            for n in range(2):
                self.grad[2 * n + self.c, rows] = self.pair_sum(n, rows).astype(low_type)
            self.start(self.y_copies())
            return
        self.arrived(self.x_copies())
        self.got_x[rows] = self.chip_sum(rows).astype(low_type)
        self.start(self.y_copies())
        self.own[...] = self.chip_sum(self.half(self.y))

    def across_z(self):
        rows = self.half(self.y)
        if self.mode == "y":
            self.arrived(self.x_copies())
            v = self.own[...] + self.got_x[rows].astype(float_type)
        else:
            self.arrived(self.y_copies())
            v = self.own[...] + self.got_y[...].astype(float_type)
        self.own[...] = v
        self.got_x[rows] = v.astype(low_type)
        self.start(self.first_z_copies() if self.mode == "h" else self.z_copies())

    def second_z(self):
        self.arrived(self.first_z_copies())
        for n in range(2):
            rows = self.piece(2 * self.low + n)
            v = self.own[rows] + self.got_z[n].astype(float_type)
            self.own[rows] = v
            self.got_x[self.piece(2 * self.low + n, self.y)] = v.astype(low_type)
        self.start(self.second_z_copies())

    def second_back(self):
        self.arrived(self.back_second_copies())
        self.start(self.back_first_copies())

    def finish(self, v):
        if self.chips["e"]:
            self.got_x[self.piece(self.slot, self.y)] = v.astype(low_type)
            self.start(self.extra_copies())
            for n, cp in enumerate(self.extra_copies()):
                cp.wait_recv()
                v = v + self.got_e[n].astype(float_type)
        self.out[self.piece(self.slot, self.y)] = v.astype(low_type)

    def back_z(self):
        if self.mode == "h":
            self.arrived(self.second_z_copies())
            self.finish(self.own[self.piece(self.slot)] + self.got_z[2].astype(float_type))
            self.start(self.back_second_copies())
            return
        self.arrived(self.z_copies())
        v = self.own[self.piece(self.z)]
        for n in range(3):
            v = v + self.got_z[n].astype(float_type)
        self.finish(v)
        self.start(self.back_z_copies())

    def spread(self):
        self.arrived(self.x_copies())
        size = self.size // 8
        self.own[0:size] = self.chip_sum(self.piece(self.z, self.y))
        for y in range(2):
            rows = self.half(y)
            self.got_x[rows] = self.chip_sum(rows).astype(low_type)
        self.start(self.spread_copies())

    def back(self):
        self.arrived(self.spread_copies())
        v = self.own[0 : self.size // 8]
        for n in range(7):
            v = v + self.got_all[n].astype(float_type)
        self.finish(v)
        self.start(self.back_copies())

    def back_y(self):
        self.arrived(self.back_first_copies() if self.mode == "h" else self.back_z_copies())
        self.start(self.back_y_copies())

    def end(self):
        self.arrived(self.back_copies() if self.mode == "all" else self.back_y_copies())

    def drain(self):
        sent = self.core_copies() + self.x_copies() + self.extra_copies()
        if self.mode == "all":
            sent += self.spread_copies() + self.back_copies()
        elif self.mode == "h":
            sent += self.y_copies() + self.first_z_copies() + self.second_z_copies()
            sent += self.back_second_copies() + self.back_first_copies() + self.back_y_copies()
        else:
            sent += (
                self.y_copies() + self.z_copies() + self.back_z_copies() + self.back_y_copies()
            )
        for cp in sent:
            cp.wait_send()


CHUNKS2 = ((384, "x"), (256, "x"), (256, "x"))
CHUNKS1 = ((384, "x"), (256, "x"), (256, "x"))


def out_rows(pixels, channels, classes):
    def laid(sizes):
        found, at = {}, 0
        for name, size in sizes:
            found[name] = (at, size)
            at += size
        return found

    padded = -(-9 * channels // 4 // 128) * 128
    rows = -(-classes // 4 // 16) * 16
    low_at = laid((("result", pixels), ("w1", padded), ("w2", padded), ("jo", channels)))
    wide_at = laid((
        ("images", pixels), ("lines", 32), ("embed", channels), ("classes", 2 * rows),
        ("offset", 16),
    ))
    return low_at, wide_at


def block_kernel(
    *rest,
):
    small_any, rest = rest[:16], rest[16:]
    (w1_any, w2_any, jw_any, ow_any, ew_any, ct_any,
    low_any, wide_any,
    w1, w2, jw, ow, ew, ct, ones, hid, mid, mod, emb, act1_t, act2_t, st, m1, m3, got,
    att, att_t, kv, kv_t, q8, d_out_t, qm, dom, s_ref, eb, dsb, mix_t, dq_t, dq, dkv,
    got_core, to_x, got_x, ag, q_sum, kv_sum, o_sum, gjo,
    grad, slope_grad, gs, mg,
    gw, w_core, w_got_x, w_own, w_got_y, w_got_z, w_got_e, got_two, got_all,
    o_core, o_got_x, o_own, o_got_y, o_got_z, o_got_e,
    v_own, v_row, v_one, v_y, v_two, v_z, v_three, v_e, g_row, gat, left, hot,
    vec_ref, prep_ref, wsem, ssem, rsem, gsend, grecv, asem, bsem, cs, cr, es, er, vs, vr, gsem,
    hsem, low_out, wide_out, osem, isem, x_ref, cot_ref, *held) = rest
    lines, (count_ref, index_ref, label_ref) = held[:11], held[11:]
    enter = [
        pltpu.make_async_copy(src, dst, isem.at[n])
        for n, (src, dst) in enumerate(zip(small_any, (x_ref, cot_ref, *held)))
    ]
    images, pixels, channels = x_ref.shape
    width = 32
    edge = pixels - width
    rows_in = pixels // width
    whole = 4 * pixels
    entries = float(whole * (channels // GROUPS))
    half = math.sqrt(0.5)
    quarter = 9 * channels // 4
    padded = gw.shape[2]
    chunk = 128
    pair_lanes = 2 * HEAD
    pairs = channels // pair_lanes
    i, r, c, who = peers()
    chips = chip_peers(i, r)
    place = (c, lax.div(r, 2), chips)
    inner = pl.multiple_of(edge * (1 - c), width)
    outer = pl.multiple_of(edge * c, width)
    inner_halo = pl.multiple_of((pixels + width) * (1 - c), width)
    outer_halo = pl.multiple_of((pixels + width) * c, width)
    outer_live = jnp.logical_and(r > 0, r < 3)
    barrier = pltpu.get_barrier_semaphore()
    greeted = list(who.values()) + chips["all"] + chips["e"]
    for at in greeted:
        pl.semaphore_signal(barrier, inc=1, device_id=at, device_id_type=MESH)
    loads = {
        name: pltpu.make_async_copy(src, dst, wsem.at[n])
        for n, (name, src, dst) in enumerate((
            ("ct", ct_any, ct), ("ew", ew_any, ew), ("w1", w1_any, w1), ("w2", w2_any, w2),
            ("jw", jw_any, jw), ("ow", ow_any, ow),
        ))
    }
    for cp in enter + list(loads.values()):
        cp.start()

    abuf = grad.at[0]
    low_at, wide_at = out_rows(images * pixels, channels, ct.shape[0])
    gw1_ref, gw2_ref, go_ref = (low_out.at[pl.ds(*low_at[n])] for n in ("w1", "w2", "jo"))
    gv_ref, ge_ref, gc_ref, geo_ref = (
        wide_out.at[pl.ds(*wide_at[n])] for n in ("lines", "embed", "classes", "offset")
    )

    def dot(a, b):
        return jnp.dot(a, b, preferred_element_type=float_type)

    def dot_nt(a, b):
        return lax.dot_general(a, b, contract_cols, preferred_element_type=float_type)

    def vec(n):
        return vec_ref[n : n + 1, :]

    def col_sum(v):
        return jnp.sum(v, axis=0, keepdims=True)

    def slope_of(pre):
        s = 0.5 * jnp.tanh(0.5 * pre) + 0.5
        return s * (1.0 + pre * (1.0 - s))

    def remote(src, dst, send, recv, at):
        return pltpu.make_async_remote_copy(
            src, dst, send, recv, device_id=at, device_id_type=MESH
        )

    def start(copies):
        for cp in copies:
            cp.start()

    def arrived(copies):
        for cp in copies:
            cp.wait_recv()

    def some_images(step, first, last):
        def run(b, _):
            step(b)
            return 0

        lax.fori_loop(first, last, run, 0)

    def each_image(step):
        some_images(step, 0, images)

    message_rows = (48, 48, 48, 16, 48, 16, 48)

    def copies(p, b):
        full, stat = pl.ds(0, message_rows[p]), pl.ds(0, 16)
        return [
            remote(
                src.at[p, b, rows], got.at[p, b, k - 1, rows], ssem.at[p, b, k - 1],
                rsem.at[p, b, k - 1], who[k],
            )
            for k, src, rs in ((1, m1, full), (2, m1, stat), (3, m3, full))
            for rows in (rs,)
        ]

    def fill_message(p, b, first, second, edges=None):
        packed = pack_stats(first, second)
        m1[p, b, 0:16] = packed
        m3[p, b, 0:16] = packed
        if edges is not None:
            m1[p, b, 16:48] = edges(inner).astype(low_type)
            m3[p, b, 16:48] = edges(outer).astype(low_type)

    def send(p, b, first, second, edges=None):
        fill_message(p, b, first, second, edges)
        start(copies(p, b))

    def receive(p, b):
        arrived(copies(p, b))
        parts = [m1[p, b, 0:16]] + [got[p, b, k, 0:16] for k in range(3)]
        return combine_stats(parts, ones[...], entries)

    def receive_scale(p, b):
        first, second = receive(p, b)
        scaled = lax.rsqrt(second - first * first + norm_eps)
        st[b, 2 * p : 2 * p + 1] = first
        st[b, 2 * p + 1 : 2 * p + 2] = scaled
        return first, scaled

    def far_rows(p, b, k):
        return got[p, b, k, 16:48].astype(float_type)

    def fill_halo(buf, value):
        fill_row(buf, inner_halo, value(0), channels, width)
        fill_row(buf, outer_halo, jnp.where(outer_live, value(2), 0.0), channels, width)

    def convolve(w):
        depth = 3 * channels
        return sum(
            dot(abuf[width * dy : width * dy + pixels, :], w[depth * dy : depth * (dy + 1), :])
            for dy in range(3)
        )

    def data_grad(buf, b, w):
        total = None
        for dy in range(3):
            for dx in range(3):
                tap = 3 * dy + dx
                more = dot_nt(
                    buf[b, (2 - dy) * width : (2 - dy) * width + pixels,
                        (2 - dx) * channels : (3 - dx) * channels],
                    w[tap * channels : (tap + 1) * channels, :],
                )
                total = more if total is None else total + more
        return total

    def kernel_grad(act_t, buf, base, first, last):
        for dy in range(3):
            for dx in range(3):
                tap = 3 * dy + dx
                at = (2 - dx) * channels
                g = None
                for b in range(first, last):
                    more = dot(
                        act_t[:, b * pixels : (b + 1) * pixels],
                        buf[b, (2 - dy) * width : (2 - dy) * width + pixels, at : at + channels],
                    )
                    g = more if g is None else g + more
                for m in range(4):
                    lo = max(tap * channels, m * quarter)
                    hi = min((tap + 1) * channels, (m + 1) * quarter)
                    if lo < hi:
                        v = g[lo - tap * channels : hi - tap * channels]
                        rows = slice(lo - m * quarter, hi - m * quarter)
                        if first > 0:
                            v = v + gw[base, m, rows].astype(float_type)
                        gw[base, m, rows] = v.astype(low_type)

    def reduction(out, start, size, mode, q, refs):
        return Reduction(out, start, size, mode, q, refs, who, place, cs, cr, es, er)

    def reductions(n, out, first, sizes):
        refs = tuple(ref.at[n] for ref in (gw, w_core, w_got_x, w_own, w_got_y, w_got_z, w_got_e))
        found, at = [], 0
        for q, (size, mode) in enumerate(sizes):
            found.append(reduction(out, at, size, mode, first + q, refs + (got_two, got_all)))
            at += size
        return found

    red2 = reductions(1, gw2_ref, 0, CHUNKS2)
    red1 = reductions(0, gw1_ref, 4, CHUNKS1)
    refs = (gjo, o_core, o_got_x, o_own, o_got_y, o_got_z, o_got_e, got_two, got_all)
    red0 = reduction(go_ref, 0, channels, "x", 8, refs)
    zs, extras = chips["z"], chips["e"]

    def small_row_copies(s):
        return [
            remote(v_own.at[s], v_row.at[s, k - 1], vs.at[s, k - 1], vr.at[s, k - 1], who[k])
            for k in (1, 2)
        ]

    def small_y_copies(s):
        return [remote(v_one.at[s], v_y.at[s], vs.at[s, 3], vr.at[s, 3], chips["y"][0])]

    def small_z_copies(s):
        return [
            remote(v_two.at[s], v_z.at[s, n], vs.at[s, 4 + n], vr.at[s, 4 + n], at)
            for n, at in enumerate(zs)
        ]

    def small_e_copies(s):
        return [
            remote(v_three.at[s], v_e.at[s, n], vs.at[s, 7 + n], vr.at[s, 7 + n], at)
            for n, at in enumerate(extras)
        ]

    def small_row(s):
        v_own[s] = gs[...]
        start(small_row_copies(s)[:1])

    def small_x(s):
        small_row_copies(s)[0].wait_send()
        small_row_copies(s)[0].wait_recv()
        v_own[s] = v_own[s] + v_row[s, 0]
        start(small_row_copies(s)[1:])

    def small_y(s):
        arrived(small_row_copies(s)[1:])
        v = v_own[s] + v_row[s, 1]
        quarter_of = channels // 4
        v = pltpu.roll(v, lax.rem(channels - r * quarter_of, channels), 1)
        v_one[s] = v[:, 0:128]
        if s == 0:
            double = lax.rem(r, 2) * 2 * quarter_of
            pair = v_own[0, 8:10] + v_row[0, 1, 8:10]
            pair = jnp.where(r < 2, pair[0:1], pair[1:2])
            pair = pltpu.roll(pair, lax.rem(channels - double, channels), 1)
            v_one[0, 8:9] = pair[:, 0:128]
            v_one[0, 9:10] = pltpu.roll(pair, channels - 128, 1)[:, 0:128]
        start(small_y_copies(s))

    def small_z(s):
        arrived(small_y_copies(s))
        v_two[s] = v_one[s] + v_y[s]
        start(small_z_copies(s))

    def small_end(s):
        arrived(small_z_copies(s))
        v_three[s] = v_two[s] + v_z[s, 0] + v_z[s, 1] + v_z[s, 2]
        total = v_three[s]
        if extras:
            start(small_e_copies(s))
            arrived(small_e_copies(s))
            for n in range(len(extras)):
                total = total + v_e[s, n]
        gv_ref[pl.ds(16 * s, 16), 0:128] = total

    def gather_row_copies():
        return [
            remote(mg, g_row.at[k - 1], gsem.at[k - 1], hsem.at[k - 1], who[k])
            for k in (1, 2)
        ]

    def gather_copies():
        blocks = [pl.ds(i, 1), pl.ds(pl.multiple_of(i - lax.rem(i, 2), 2), 2)]
        blocks.append(pl.ds(pl.multiple_of(i - lax.rem(i, 8), 8), 8))
        found = []
        for rows, places in zip(blocks, (chips["y"], zs, extras)):
            for at in places:
                n = 3 + len(found)
                part_of = gat.at[c, rows]
                found.append(remote(part_of, part_of, gsem.at[n], hsem.at[n], at))
        return found

    def gather_core_copies():
        n = 7 + len(extras)
        return [remote(gat.at[c], gat.at[c], gsem.at[n], hsem.at[n], who[1])]

    def gather_row():
        start(gather_row_copies()[:1])

    def gather_x():
        gather_row_copies()[0].wait_send()
        gather_row_copies()[0].wait_recv()
        mg[...] = mg[...] + g_row[0]
        start(gather_row_copies()[1:])

    def gather_y():
        arrived(gather_row_copies()[1:])
        v = emb[...] + mg[...] + g_row[1]
        gat[c, i] = jnp.where(c == 0, v[:, :channels], v[:, channels:])
        start(gather_copies()[:1])

    def gather_z():
        arrived(gather_copies()[:1])
        start(gather_copies()[1:4])

    def gather_end():
        arrived(gather_copies()[1:4])
        start(gather_copies()[4:])
        arrived(gather_copies()[4:])
        start(gather_core_copies())

    def gather_core():
        other = gat.at[1 - c]
        n = 7 + len(extras)
        remote(other, other, gsem.at[n], hsem.at[n], who[1]).wait_recv()

    def three_terms(v):
        a = v.astype(low_type)
        b = (v - a.astype(float_type)).astype(low_type)
        d = (v - a.astype(float_type) - b.astype(float_type)).astype(low_type)
        return jnp.concatenate([a, b, d], axis=0)

    def embedding():
        for ref in (ge_ref, gc_ref, geo_ref):
            ref[...] = jnp.zeros(ref.shape, float_type)
        lax.fori_loop(0, gat.shape[1] // 8, embedding_part, 0)

    def embedding_part(part_of, _):
        every = 64
        groups = pl.ds(pl.multiple_of(part_of * 8, 8), 8)
        full = jnp.concatenate(
            [gat[n, groups].reshape(every, channels) for n in range(2)], axis=1
        )
        place_of = lax.rem(lax.broadcasted_iota(jnp.int32, (every, 2 * channels), 0), 8)
        live = place_of < images
        grad = jnp.where(live, full, 0.0)
        held = jnp.where(live, pltpu.roll(full, every - images, 0), 0.0)
        act = jnp.where(live, half_silu(held), 0.0).astype(low_type)
        left[...] = jnp.concatenate([act, act, act], axis=0).T
        terms = three_terms(grad)
        size = 2 * channels // 4
        own = pl.ds(pl.multiple_of(r * size, size), size)
        v = jnp.dot(left[own, :], terms, preferred_element_type=float_type)
        ge_ref[0:size] += v[:, :channels]
        ge_ref[size : 2 * size] += v[:, channels:]
        v = jnp.sum(grad, axis=0, keepdims=True)
        geo_ref[0:1] += v[:, :channels]
        geo_ref[8:9] += v[:, channels:]
        active = lax.dot_general(terms, ew[...], contract_cols, preferred_element_type=float_type)
        active = active[0:every] + active[every : 2 * every] + active[2 * every :]
        back = jnp.where(live, active * slope_of(held), 0.0)
        classes = ct.shape[0] // 4
        row_of = lax.rem(lax.broadcasted_iota(jnp.int32, (every, 128), 0), 8)
        label = jnp.full((every, 128), -1.0, float_type)
        for b in range(images):
            rolled = pltpu.roll(full[:, 256 * b : 256 * b + 128], every - 2 * images + b, 0)
            label = jnp.where(row_of == b, rolled, label)
        for n in range(hot.shape[0] // 128):
            kind = lax.broadcasted_iota(jnp.int32, (every, 128), 1) + 128 * n + r * classes
            hit = jnp.where(label == kind.astype(float_type), 1.0, 0.0).astype(low_type)
            hot[128 * n : 128 * (n + 1), :] = jnp.concatenate([hit, hit, hit], axis=0).T
        found = jnp.dot(hot[...], three_terms(back), preferred_element_type=float_type)
        height = gc_ref.shape[0] // 2
        gc_ref[0:height] += found[0:height, :channels]
        gc_ref[height:] += found[0:height, channels:]
        return 0

    def embed_forward():
        row = lax.broadcasted_iota(jnp.int32, (8, 2 * channels), 0)
        lane_of = lax.broadcasted_iota(jnp.int32, (8, channels), 1).astype(float_type)

        def spread(ref, other):
            v = jnp.full((8, channels), other, float_type)
            for b in range(images):
                v = jnp.where(row[:, :channels] == b, ref[b].astype(float_type), v)
            return v

        position = (spread(index_ref, 0.0) + 1.0) / (spread(count_ref, 2.0) - 1.0)
        low_root = sigma_least ** (1.0 / sigma_power)
        high_root = sigma_most ** (1.0 / sigma_power)
        root = low_root + position * (high_root - low_root)
        square = root * root
        noise_time = 250.0 * jnp.log(square * square * square * root)
        angles = noise_time * jnp.exp(lane_of * (-math.log(10000.0) / channels))
        features = jnp.concatenate([jnp.cos(angles), jnp.sin(angles)], axis=1)
        count = ct.shape[0]
        label = spread(label_ref, -1.0)[:, 0:1]
        kinds = lax.broadcasted_iota(jnp.int32, (8, count), 1).astype(float_type)
        one_hot = jnp.where(label == kinds, 1.0, 0.0).astype(low_type)
        loads["ct"].wait()
        embedded = features + dot(one_hot, ct[...])
        live = row < images
        embed_act = half_silu(embedded).astype(low_type)
        loads["ew"].wait()
        offset = jnp.concatenate([vec(11), vec(12)], axis=1)
        mod[...] = dot(embed_act, ew[...]) + offset
        rows = pltpu.roll(jnp.where(live, embedded, 0.0), images, 0)
        part_of = lax.broadcasted_iota(jnp.int32, (8, 2 * channels), 1)
        marks = jnp.zeros((8, 2 * channels), float_type)
        for b in range(images):
            here = jnp.logical_and(row == 2 * images, part_of >= 256 * b)
            marks = jnp.where(here, label_ref[b].astype(float_type), marks)
        emb[...] = rows + marks

    leaving = []

    def leave(src, dst, first, size):
        rows = pl.ds(first, size)
        cp = pltpu.make_async_copy(src.at[rows], dst.at[rows], osem.at[len(leaving)])
        cp.start()
        leaving.append(cp)

    def leave_low(name, first=0, size=None):
        at, rows = low_at[name]
        leave(low_out, low_any, at + first, size or rows)

    def leave_wide(name, last=None):
        at, rows = wide_at[name]
        leave(wide_out, wide_any, at, sum(wide_at[last or name]) - at)

    for cp in enter:
        cp.wait()
    at = 0
    for line in lines:
        v = line[...].astype(float_type).reshape(1, line.shape[0])
        for n in range(line.shape[0] // channels):
            vec_ref[at : at + 1] = v[:, n * channels : (n + 1) * channels]
            at += 1
    ones[...] = block_ones(channels, channels // GROUPS)
    gs[...] = jnp.zeros(gs.shape, float_type)
    mg[...] = jnp.zeros(mg.shape, float_type)

    for n in range(2):
        for m in range(4):
            gw[n, m, quarter:padded] = jnp.zeros((padded - quarter, channels), low_type)

    @each_image
    def _(b):
        v = x_ref[b].astype(float_type)
        fill_message(0, b, col_sum(v), col_sum(v * v), lambda at: x_ref[b, pl.ds(at, width)])
        none = jnp.zeros((1, channels), float_type)
        fill_message(6, b, none, none, lambda at: cot_ref[b, pl.ds(at, width)])

    embed_forward()
    pl.semaphore_wait(barrier, len(greeted))

    @each_image
    def _(b):
        start(copies(0, b))

    @each_image
    def _(b):
        start(copies(6, b))

    loads["ow"].wait()

    @each_image
    def _(b):
        d_out_t[b] = dot_nt(cot_ref[b], ow[...]).T.astype(low_type)

    def first_convolution(b):
        centre, scaled = receive_scale(0, b)
        slope = scaled * vec(0)
        shift = vec(1)

        def activate(v):
            return half_silu((v - centre) * slope + shift)

        for row in range(rows_in):
            v = activate(x_ref[b, row * width : (row + 1) * width].astype(float_type))
            fill_row(abuf, (row + 1) * width, v, channels, width)
        fill_halo(abuf, lambda k: activate(far_rows(0, b, k)))
        hidden = convolve(w1) + vec(2)
        hid[b] = hidden
        send(
            1, b, col_sum(hidden), col_sum(hidden * hidden),
            lambda at: hid[b, pl.ds(at, width)],
        )
        own = pl.ds(pl.multiple_of(b * pixels, pixels), pixels)
        act1_t[:, own] = abuf[width : width + pixels, channels : 2 * channels].T

    def block(n):
        return pl.ds(pl.multiple_of(width + n * pixels, width), pixels)

    def wide_block(n):
        return pl.ds(pl.multiple_of(n * pixels, width), pixels + 2 * width)

    def span_of(n):
        return pl.ds(pl.multiple_of(n * pixels, pixels), pixels)

    mate = r + 1 - 2 * c
    across = lax.rem(r + 2, 4)

    def gather(b, n, rows):
        return remote(
            att.at[b, rows], att.at[b, rows], gsend.at[b, n], grecv.at[b, n], who[(1, 2, 1)[n]]
        )

    def shares(b):
        return [gather(b, n, block(rows)) for n, rows in enumerate((r, r, across))]

    def arrivals(b):
        rows = (mate, across, lax.rem(mate + 2, 4))
        return [gather(b, n, block(w)) for n, w in enumerate(rows)]

    def share(b):
        centre, scaled = receive_scale(2, b)
        slope = scaled * vec(6)
        att[b, block(r)] = ((mid[b] - centre) * slope + vec(7)).astype(low_type)
        start(shares(b)[:2])

    def second_convolution(b):
        centre, scaled = receive_scale(1, b)
        grow = 1.0 + mod[pl.ds(b, 1), 0:channels]
        slope = scaled * vec(3) * grow
        shift = vec(4) * grow + mod[pl.ds(b, 1), channels:]

        def activate(v):
            return half_silu((v - centre) * slope + shift)

        for row in range(rows_in):
            v = activate(hid[b, row * width : (row + 1) * width])
            fill_row(abuf, (row + 1) * width, v, channels, width)
        fill_halo(abuf, lambda k: activate(far_rows(1, b, k)))
        middle = (convolve(w2) + vec(5) + x_ref[b].astype(float_type)) * half
        mid[b] = middle
        send(
            2, b, col_sum(middle), col_sum(middle * middle),
            lambda at: mid[b, pl.ds(at, width)],
        )
        own = pl.ds(pl.multiple_of(b * pixels, pixels), pixels)
        act2_t[:, own] = abuf[width : width + pixels, channels : 2 * channels].T

    loads["w1"].wait()
    loads["w2"].wait()
    loads["jw"].wait()
    some_images(first_convolution, 0, 2)
    some_images(second_convolution, 0, 1)
    some_images(first_convolution, 2, images)
    share(0)
    some_images(second_convolution, 1, images)

    part = att

    def forward(b):
        arrivals(b)[1].wait_recv()
        shares(b)[2].start()

    def sums_core(b):
        return [
            remote(
                part.at[b, wide_block(2 * n + 1 - c)], got_core.at[b, n], asem.at[b, n],
                bsem.at[b, n], who[1],
            )
            for n in range(2)
        ]

    def sum_x(b):
        return remote(to_x, got_x.at[b], asem.at[b, 2], bsem.at[b, 2], who[2])

    def pass_on(b):
        x = lax.div(r, 2)
        arrived(sums_core(b))

        @pl.when(b > 0)
        def _():
            sum_x(b - 1).wait_send()

        far = 1 - x
        to_x[...] = (
            part[b, wide_block(2 * far + c)].astype(float_type)
            + got_core[b, far].astype(float_type)
        ).astype(low_type)
        sum_x(b).start()
        ag[b] = part[b, wide_block(r)].astype(float_type) + got_core[b, x].astype(float_type)

    def queries(b):
        q = (dot(att[b, block(r)], jw[:, :channels]) + vec(8)).astype(low_type)
        q8[...] = (q.astype(float_type) * HEAD ** (-0.5)).astype(low_type)

    lane = lax.broadcasted_iota(jnp.int32, (pixels, pair_lanes), 1)

    def masked(v):
        return jnp.concatenate(
            [jnp.where(lane < HEAD, v, 0.0), jnp.where(lane >= HEAD, v, 0.0)], axis=0
        ).astype(low_type)

    q_sum[...] = jnp.zeros(q_sum.shape, float_type)
    kv_sum[...] = jnp.zeros(kv_sum.shape, float_type)
    o_sum[...] = jnp.zeros(o_sum.shape, float_type)
    att_t[channels:] = jnp.ones((16, whole), low_type)
    none = jnp.zeros((width, channels), low_type)
    for b in range(images):
        att[b, 0:width] = none
        att[b, width + whole :] = none

    @each_image
    def _(b):
        a = arrivals(b)
        bias = jnp.concatenate([jnp.zeros((1, channels), float_type), vec(9)], axis=1)

        def project(x):
            rows = pl.ds(pl.multiple_of(width + 2 * x * pixels, width), 2 * pixels)
            to = pl.ds(pl.multiple_of(2 * x * pixels, 2 * pixels), 2 * pixels)
            kv[to] = (dot(att[b, rows], jw[:, channels:]) + bias).astype(low_type)

        queries(b)
        a[0].wait_recv()
        project(lax.div(r, 2))

        @pl.when(b == 0)
        def _():
            forward(0)

        a[2].wait_recv()
        project(1 - lax.div(r, 2))

        @pl.when(b == 0)
        def _():
            some_images(share, 1, images)

        for n in range(2 * channels // 128):
            cols = pl.ds(n * 128, 128)
            kv_t[cols, :] = kv[:, cols].T

        @pl.when(b > 0)
        def _():
            pass_on(b - 1)

        def one_pair(t, _):
            lanes = pl.ds(pl.multiple_of(t * pair_lanes, pair_lanes), pair_lanes)
            v_lanes = pl.ds(pl.multiple_of(channels + t * pair_lanes, pair_lanes), pair_lanes)
            qm[...] = masked(q8[:, lanes].astype(float_type))
            rows_of = [pl.ds(n * chunk, chunk) for n in range(whole // chunk)]
            cols_of = [slice(j * pixels, (j + 1) * pixels) for j in range(2)]
            head_of = [
                pl.ds(pl.multiple_of(t * pair_lanes + j * HEAD, HEAD), HEAD) for j in range(2)
            ]
            value_of = [
                pl.ds(pl.multiple_of(channels + t * pair_lanes + j * HEAD, HEAD), HEAD)
                for j in range(2)
            ]

            def score(j, rows, peak):
                s = dot_nt(kv[rows, lanes], qm[cols_of[j], :])
                s_ref[rows, cols_of[j]] = s
                top = jnp.max(s.reshape(chunk // 8, 8, pixels), axis=0)
                return top if peak is None else jnp.maximum(peak, top)

            def raise_to(j, rows, peak, total):
                e = jnp.exp(s_ref[rows, cols_of[j]] - peak)
                eb[rows, cols_of[j]] = e.astype(low_type)
                more = jnp.sum(e.reshape(chunk // 8, 8, pixels), axis=0)
                return more if total is None else total + more

            def mix(j, total):
                over = 1.0 / col_sum(total)
                mt = dot(kv_t[value_of[j], :], eb[:, cols_of[j]]) * over
                mix_t[head_of[j]] = mt.astype(low_type)
                g = (d_out_t[b, head_of[j]].astype(float_type) * over).astype(low_type)
                g = g.astype(float_type)
                none = jnp.zeros_like(g)
                both = jnp.concatenate([g, none] if j == 0 else [none, g], axis=0)
                dom[cols_of[j], :] = both.T.astype(low_type)
                return col_sum(g * mt)

            def score_back(j, rows, inner_of):
                dp = dot_nt(kv[rows, v_lanes], dom[cols_of[j], :])
                e = eb[rows, cols_of[j]].astype(float_type)
                dsb[rows, cols_of[j]] = (e * (dp - inner_of)).astype(low_type)

            def query_back(j):
                dq_t[head_of[j]] = dot(kv_t[head_of[j], :], dsb[:, cols_of[j]]) * HEAD ** (-0.5)

            peak0 = peak1 = total0 = total1 = None
            for rows in rows_of:
                peak0 = score(0, rows, peak0)
            peak0 = jnp.max(peak0, axis=0, keepdims=True)
            for rows in rows_of:
                peak1 = score(1, rows, peak1)
                total0 = raise_to(0, rows, peak0, total0)
            peak1 = jnp.max(peak1, axis=0, keepdims=True)
            inner0 = mix(0, total0)
            for rows in rows_of:
                score_back(0, rows, inner0)
                total1 = raise_to(1, rows, peak1, total1)
            inner1 = mix(1, total1)
            query_back(0)
            for rows in rows_of:
                score_back(1, rows, inner1)
            dkv[:, v_lanes] = dot(eb[...], dom[...]).astype(low_type)
            query_back(1)
            dkv[:, lanes] = dot(dsb[...], qm[...]).astype(low_type)
            return 0

        lax.fori_loop(0, pairs, one_pair, 0)

        @pl.when(b + 1 < images)
        def _():
            forward(b + 1)

        dq[...] = dq_t[...].T.astype(low_type)
        att_t[0:channels] = att[b, width : width + whole].T
        for cp in shares(b):
            cp.wait_send()
        own = dot_nt(dq[...], jw[:, :channels])
        first = col_sum(own)
        second = col_sum(own * att[b, block(r)].astype(float_type))
        for n in range(4):
            rows = pl.ds(width + n * pixels, pixels)
            v = dot_nt(dkv[n * pixels : (n + 1) * pixels], jw[:, channels:])
            first += col_sum(v)
            second += col_sum(v * att[b, rows].astype(float_type))
            part[b, rows] = v.astype(low_type)
        part[b, block(r)] = (part[b, block(r)].astype(float_type) + own).astype(low_type)
        start(sums_core(b))
        second = (second - vec(7) * first) / vec(6)
        gs[6:7] += second
        gs[7:8] += first
        send(3, b, first * vec(6), second * vec(6))
        q_sum[...] += dot(att_t[:, span_of(r)], dq[...])
        kv_sum[...] += dot(att_t[...], dkv[...])

        o_sum[...] += dot(mix_t[...], cot_ref[b])
        low_out[span_of(b)] = mix_t[...].T

        @pl.when(b == images - 1)
        def _():
            pass_on(b)

    def pack_weights():
        part_rows = channels // 4
        every = (q_sum[0:channels], kv_sum[0:channels, :channels], kv_sum[0:channels, channels:], o_sum[...])
        for n, v in enumerate(every):
            for m in range(4):
                gjo[m, n * part_rows : (n + 1) * part_rows] = v[
                    m * part_rows : (m + 1) * part_rows
                ].astype(low_type)
        gs[8:9] = q_sum[channels : channels + 1]
        gs[9:10] = kv_sum[channels : channels + 1, channels:]
        gs[10:11] = col_sum(jnp.sum(cot_ref[...].astype(float_type), axis=0))

    def result(b):
        v = mid[b] + dot(low_out[span_of(b)], ow[...]) + vec(10)
        low_out[span_of(b)] = v.astype(low_type)

    def branch_grad(b):
        first, second = receive(3, b)
        arrived(copies(6, b))
        sum_x(b).wait_recv()
        centre, scaled = st[b, 4:5], st[b, 5:6]

        def grad_of(cot, rows, v):
            u = ag[b, rows] + got_x[b, rows].astype(float_type)
            return (cot + scaled * (u * vec(6) - first - (v - centre) * scaled * second)) * half

        total = jnp.zeros((1, channels), float_type)
        for row in range(rows_in):
            rows = pl.ds(row * width, width)
            inside = pl.ds((row + 1) * width, width)
            v = grad_of(cot_ref[b, rows].astype(float_type), inside, mid[b, rows])
            ag[b, inside] = v
            v = v.astype(low_type).astype(float_type)
            fill_row(grad.at[b], (row + 1) * width, v, channels, width)
            total += col_sum(v)
        gs[5:6] += total
        places = {0: pl.ds(inner_halo, width), 2: pl.ds(outer_halo, width)}
        fill_halo(grad.at[b], lambda k: grad_of(far_rows(6, b, k), places[k], far_rows(2, b, k)))

    def branch_back(b):
        upstream = data_grad(grad, b, w2)
        grow = 1.0 + mod[pl.ds(b, 1), 0:channels]
        normed = (hid[b] - st[b, 2:3]) * st[b, 3:4]
        pre = (normed * vec(3) + vec(4)) * grow + mod[pl.ds(b, 1), channels:]
        v = upstream * slope_of(pre)
        slope_grad[b] = v
        first, second = col_sum(v), col_sum(v * normed)
        mg[pl.ds(b, 1), 0:channels] = vec(3) * second + vec(4) * first
        mg[pl.ds(b, 1), channels:] = first
        first, second = grow * first, grow * second
        gs[3:4] += second
        gs[4:5] += first
        send(
            4, b, first * vec(3), second * vec(3),
            lambda at: slope_grad[b, pl.ds(at, width)],
        )

    def hidden_grad(b):
        first, second = receive(4, b)
        centre, scaled = st[b, 2:3], st[b, 3:4]
        gain = (1.0 + mod[pl.ds(b, 1), 0:channels]) * vec(3)

        def grad_of(u, v):
            return scaled * (u * gain - first - (v - centre) * scaled * second)

        total = jnp.zeros((1, channels), float_type)
        for row in range(rows_in):
            rows = pl.ds(row * width, width)
            v = grad_of(slope_grad[b, rows], hid[b, rows]).astype(low_type).astype(float_type)
            fill_row(grad.at[b], (row + 1) * width, v, channels, width)
            total += col_sum(v)
        gs[2:3] += total
        fill_halo(grad.at[b], lambda k: grad_of(far_rows(4, b, k), far_rows(1, b, k)))

    def hidden_back(b):
        upstream = data_grad(grad, b, w1)
        normed = (x_ref[b].astype(float_type) - st[b, 0:1]) * st[b, 1:2]
        v = upstream * slope_of(normed * vec(0) + vec(1))
        slope_grad[b] = v
        first, second = col_sum(v), col_sum(v * normed)
        gs[0:1] += second
        gs[1:2] += first
        send(5, b, first * vec(0), second * vec(0))

    def images_grad(b):
        first, second = receive(5, b)
        scaled = st[b, 1:2]
        normed = (x_ref[b].astype(float_type) - st[b, 0:1]) * scaled
        v = scaled * (slope_grad[b] * vec(0) - first - normed * second)
        wide_out[span_of(b)] = ag[b, width : width + pixels] + v

    some_images(branch_grad, 0, images - 1)
    pack_weights()
    red0.core()
    kernel_grad(act2_t, grad, 1, 0, images - 1)
    red0.across_x()
    some_images(branch_back, 0, images - 1)
    some_images(branch_grad, images - 1, images)
    kernel_grad(act2_t, grad, 1, images - 1, images)
    red2[2].core()
    some_images(branch_back, images - 1, images)
    red2[1].core()
    red2[2].across_x()
    red2[0].core()
    each_image(result)
    leave_low("result")
    small_row(0)
    gather_row()
    red0.across_y()
    some_images(hidden_grad, 0, images - 1)
    some_images(hidden_grad, images - 1, images)
    red2[0].across_x()
    kernel_grad(act1_t, grad, 0, 0, images)
    red2[1].across_x()
    red0.across_z()
    red1[0].core()
    red1[2].core()
    red1[2].across_x()
    red2[2].across_y()
    red1[0].across_x()
    red2[0].across_y()
    red0.back_z()
    red2[2].across_z()
    red1[1].core()
    red2[1].across_y()
    red2[0].across_z()
    red1[1].across_x()
    red0.back_y()
    some_images(hidden_back, images - 1, images)
    red1[2].across_y()
    red2[1].across_z()
    red2[2].back_z()
    small_x(0)
    gather_x()
    some_images(hidden_back, 0, images - 1)
    small_row(1)
    red2[0].back_z()
    red1[2].across_z()
    red2[1].back_z()
    red1[0].across_y()
    red1[0].across_z()
    small_x(1)
    red1[1].across_y()
    red2[2].back_y()
    small_y(0)
    gather_y()
    red1[2].back_z()
    red1[1].across_z()
    red2[0].back_y()
    red1[0].back_z()
    red0.end()
    leave_low("jo")
    small_y(1)
    red1[2].back_y()
    red2[1].back_y()
    red1[1].back_z()
    red2[0].end()
    leave_low("w2", 0, red2[0].size)
    small_z(0)
    gather_z()
    red1[0].back_y()
    small_z(1)
    red2[2].end()
    leave_low("w2", 640, red2[2].size)
    each_image(images_grad)
    leave_wide("images")
    red1[1].back_y()
    small_end(0)
    gather_end()
    gather_core()
    embedding()
    leave_wide("embed", "offset")
    red1[2].end()
    leave_low("w1", 640, red1[2].size)
    red1[0].end()
    leave_low("w1", 0, red1[0].size)
    small_end(1)
    leave_wide("lines")
    red2[1].end()
    leave_low("w2", 384, red2[1].size)
    red1[1].end()
    leave_low("w1", 384, red1[1].size)

    for cp in leaving:
        cp.wait()
    @each_image
    def _(b):
        sent = sums_core(b)
        for p in range(7):
            sent += copies(p, b)
        for cp in sent:
            cp.wait_send()

    sum_x(images - 1).wait_send()

    for red in [red0] + red1 + red2:
        red.drain()
    for s in range(2):
        for cp in small_row_copies(s)[1:] + small_y_copies(s) + small_z_copies(s) + small_e_copies(s):
            cp.wait_send()
    for cp in gather_row_copies()[1:] + gather_copies() + gather_core_copies():
        cp.wait_send()


def block_call(x, cot, lines, scalars, w1, w2, jw, ow, ew, ct):
    images, pixels, channels = x.shape
    span = pixels + 64
    whole = 4 * pixels
    padded = -(-9 * channels // 4 // 128) * 128
    every = lax.axis_size("img")
    more = every // 8
    some = max(more - 1, 1)
    low_at, wide_at = out_rows(images * pixels, channels, ct.shape[0])
    hbm = pl.BlockSpec(memory_space=pl.ANY)

    def low(*shape):
        return pltpu.VMEM(shape, low_type)

    def wide(*shape):
        return pltpu.VMEM(shape, float_type)

    def dma(*shape):
        return pltpu.SemaphoreType.DMA(shape)

    def out(*shape, kind=float_type):
        return jax.ShapeDtypeStruct(shape, kind)

    return pl.pallas_call(
        block_kernel,
        out_shape=(
            out(sum(low_at["jo"]), channels, kind=low_type), out(sum(wide_at["offset"]), channels),
        ),
        in_specs=[hbm] * (2 + len(lines) + 3 + 6),
        out_specs=(hbm,) * 2,
        scratch_shapes=[
            low(*w1.shape), low(*w2.shape), low(*jw.shape), low(*ow.shape), low(*ew.shape),
            low(*ct.shape), low(channels, channels), wide(*x.shape), wide(*x.shape),
            wide(8, 2 * channels), wide(8, 2 * channels),
            low(channels, images * pixels), low(channels, images * pixels),
            wide(images, 8, channels), low(7, images, 48, channels), low(7, images, 48, channels),
            low(7, images, 3, 48, channels),
            low(images, whole + 64, channels), low(channels + 16, whole), low(whole, 2 * channels),
            low(2 * channels, whole), low(pixels, channels), low(images, channels, pixels),
            low(2 * pixels, 2 * HEAD), low(2 * pixels, 2 * HEAD), wide(whole, 2 * pixels),
            low(whole, 2 * pixels), low(whole, 2 * pixels), low(channels, pixels),
            wide(channels, pixels), low(pixels, channels), low(whole, 2 * channels),
            low(images, 2, span, channels), low(span, channels), low(images, span, channels),
            wide(images, span, channels),
            wide(channels + 16, channels),
            wide(channels + 16, 2 * channels), wide(channels, channels), low(4, channels, channels),
            low(images, span, 3 * channels), wide(*x.shape), wide(16, channels), wide(8, 2 * channels),
            low(2, 4, padded, channels), low(2, 2, padded, channels), low(2, padded, channels),
            wide(2, padded // 2, channels), low(2, padded // 2, channels),
            low(2, 3, padded // 8, channels), low(2, some, padded // 8, channels),
            low(2, 128, channels), low(7, 16, channels),
            low(2, channels, channels), low(channels, channels), wide(channels // 2, channels),
            low(channels // 2, channels), low(3, channels // 8, channels),
            low(some, channels // 8, channels),
            wide(2, 16, channels), wide(2, 2, 16, channels), wide(2, 16, 128),
            wide(2, 16, 128), wide(2, 16, 128), wide(2, 3, 16, 128), wide(2, 16, 128),
            wide(2, some, 16, 128), wide(2, 8, 2 * channels), wide(2, every, 8, channels),
            low(2 * channels, 192), low(256, 192), wide(16, channels), wide(8, 2 * channels),
            dma(6), dma(7, images, 3), dma(7, images, 3), dma(images, 3), dma(images, 3),
            dma(images, 3), dma(images, 3), dma(9, 26), dma(9, 26), dma(9, some), dma(9, some),
            dma(2, 6 + more), dma(2, 6 + more), dma(7 + more), dma(7 + more),
            low(sum(low_at["jo"]), channels), wide(sum(wide_at["offset"]), channels), dma(16),
            dma(16), low(*x.shape), low(*cot.shape),
        ]
        + [low(*v.shape) for v in lines]
        + [pltpu.SMEM(v.shape, jnp.int32) for v in scalars],
        compiler_params=pltpu.CompilerParams(
            collective_id=0, has_side_effects=True, vmem_limit_bytes=62 << 20
        ),
        name="block",
    )(x, cot, *lines, *scalars, w1, w2, jw, ow, ew, ct)


def finish_kernel(
    low_any, wide_any,
    result, images, first_gain, first_shift, first_any, first_offset, embed_any, embed_offset,
    classes_any, second_gain, second_shift, second_any, second_offset, third_gain, third_shift,
    joint_any, joint_offset, output_any, output_offset,
    low_in, wide_in, first_kernel, second_kernel, joint_weight, output_weight, embed_weight,
    class_table, sems,
):
    r = lax.axis_index("row")
    rows, channels = output_weight.shape
    pixels = result.shape[0]
    low_at, wide_at = out_rows(pixels, channels, 4 * class_table.shape[0])
    used = []

    def move(src, dst):
        cp = pltpu.make_async_copy(src, dst, sems.at[len(used)])
        cp.start()
        used.append(cp)
        return cp

    head = pl.ds(0, pixels)
    low_tail = pl.ds(pixels, low_in.shape[0] - pixels)
    wide_tail = pl.ds(pixels, wide_in.shape[0] - pixels)
    reads = [
        move(src.at[part], dst.at[part])
        for src, dst, part in (
            (low_any, low_in, low_tail), (wide_any, wide_in, wide_tail),
            (low_any, low_in, head), (wide_any, wide_in, head),
        )
    ]

    def low_rows(name, start, size):
        at = low_at[name][0] + start
        return low_in[at : at + size].astype(float_type)

    def wide_rows(name, start, size):
        at = wide_at[name][0] + start
        return wide_in[at : at + size]

    reads[0].wait()
    first_kernel[...] = low_rows("w1", 0, 9 * rows)
    move(first_kernel, first_any)
    second_kernel[...] = low_rows("w2", 0, 9 * rows)
    move(second_kernel, second_any)
    for n in range(3):
        joint_weight[:, n * channels : (n + 1) * channels] = low_rows("jo", n * rows, rows)
    output_weight[...] = low_rows("jo", 3 * rows, rows)
    move(joint_weight, joint_any)
    move(output_weight, output_any)
    reads[2].wait()
    move(low_in.at[head], result)
    reads[3].wait()
    move(wide_in.at[head], images)
    reads[1].wait()
    size = 2 * rows
    classes = class_table.shape[0]
    reach = wide_at["classes"][1] // 2
    for n in range(2):
        cols = slice(n * channels, (n + 1) * channels)
        embed_weight[:, cols] = wide_rows("embed", n * size, size)
        class_table[:, cols] = wide_rows("classes", n * reach, reach)[0:classes]
    move(embed_weight, embed_any)
    move(class_table, classes_any)
    lines = wide_rows("lines", 0, 32)
    for n, ref in (
        (16, first_gain), (17, first_shift), (18, first_offset), (3, second_gain),
        (4, second_shift), (5, second_offset), (6, third_gain), (7, third_shift),
        (10, output_offset),
    ):
        ref[...] = lines[n, 0:rows]
    joint_offset[...] = jnp.concatenate([lines[8:9, 0:128], lines[9:10, 0:128]], axis=1)[
        0, 0 : 2 * rows
    ]
    whole = jnp.concatenate([wide_rows("offset", 0, 8), wide_rows("offset", 8, 8)], axis=1)
    turn = lax.rem(2 * channels - r * size, 2 * channels)
    embed_offset[...] = pltpu.roll(whole, turn, 1)[0, 0:size]
    for cp in used[4:]:
        cp.wait()


def finish_call(low, wide, pixels, classes):
    channels = low.shape[1]
    rows = channels // 4
    vm = pl.BlockSpec(memory_space=pltpu.VMEM)
    hbm = pl.BlockSpec(memory_space=pl.ANY)

    def out(*shape, kind=float_type):
        return jax.ShapeDtypeStruct(shape, kind)

    kernel = out(9 * rows, channels)
    line = out(rows)
    return pl.pallas_call(
        finish_kernel,
        out_shape=(
            out(pixels, channels, kind=low_type), out(pixels, channels), line, line, kernel, line,
            out(2 * rows, 2 * channels), out(2 * rows), out(classes // 4, 2 * channels), line, line,
            kernel, line, line, line, out(rows, 3 * channels), out(2 * rows), out(rows, channels),
            line,
        ),
        in_specs=[hbm] * 2,
        out_specs=(hbm, hbm, vm, vm, hbm, vm, hbm, vm, hbm, vm, vm, hbm, vm, vm, vm, hbm, vm, hbm, vm),
        scratch_shapes=[
            pltpu.VMEM(low.shape, low_type),
            pltpu.VMEM(wide.shape, float_type),
            pltpu.VMEM((9 * rows, channels), float_type),
            pltpu.VMEM((9 * rows, channels), float_type),
            pltpu.VMEM((rows, 3 * channels), float_type), pltpu.VMEM((rows, channels), float_type),
            pltpu.VMEM((2 * rows, 2 * channels), float_type),
            pltpu.VMEM((classes // 4, 2 * channels), float_type),
            pltpu.SemaphoreType.DMA((12,)),
        ],
        compiler_params=pltpu.CompilerParams(vmem_limit_bytes=60 << 20),
        name="finish",
    )(low, wide)


def shards(
    images,
    level_count,
    level_index,
    labels,
    first_gain,
    first_shift,
    first_kernel,
    first_offset,
    embed_weight,
    embed_offset,
    class_table,
    second_gain,
    second_shift,
    second_kernel,
    second_offset,
    third_gain,
    third_shift,
    joint_weight,
    joint_offset,
    output_weight,
    output_offset,
    cotangent,
):
    image_count, stripe_rows, image_width, channels = images.shape
    pixels = stripe_rows * image_width
    x = images.reshape(image_count, pixels, channels)
    cot = cotangent.reshape(image_count, pixels, channels)
    lines = (
        first_gain, first_shift, first_offset, second_gain, second_shift, second_offset,
        third_gain, third_shift, joint_offset, output_offset, embed_offset,
    )
    found = block_call(
        x, cot, lines, (level_count, level_index, labels), first_kernel, second_kernel,
        joint_weight, output_weight, embed_weight, class_table,
    )
    outs = finish_call(*found, image_count * pixels, class_table.shape[0])
    return (outs[0].reshape(images.shape), outs[1].reshape(images.shape)) + tuple(outs[2:])


def solution(mesh):
    in_specs = (
        (P("img", "row", None, None),) + (P("img"),) * 3 + (P(),) * 17
        + (P("img", "row", None, None),)
    )
    row, rows = P("row"), P("row", None)
    out_specs = (
        P("img", "row", None, None), P("img", "row", None, None), row, row, rows, row, rows, row,
        rows, row, row, rows, row, row, row, rows, row, rows, row,
    )
    return jax.shard_map(shards, mesh=mesh, in_specs=in_specs, out_specs=out_specs, check_vma=False)
```
